512 devices in a mesh: seq: 128 (over y_hi, z, x), head: 4 (over y_lo, core).
Axes of the slice: x: 4, y: 8 (y_hi: 4, y_lo: 2; y = y_hi * 2 + y_lo), z: 8, core: 2. Of those that a mesh axis runs over, the one named last changes fastest.
Arguments:
- inputs: bfloat16 [65536, 1024], P('seq', 'head'), may hold values from -6 to 6
- row_gain: float32 [1024], replicated, may hold values from 0.1 to 1.9
- row_qkv: bfloat16 [1024, 3, 1024], P(None, None, 'head'), may hold values from -4 to 4, as said below
- row_out: bfloat16 [1024, 1024], P('head'), may hold values from -0.75 to 0.75
- col_gain: float32 [1024], replicated, may hold values from 0.1 to 1.9
- col_qkv: bfloat16 [1024, 3, 1024], P(None, None, 'head'), may hold values from -4 to 4, as said below
- col_out: bfloat16 [1024, 1024], P('head'), may hold values from -0.75 to 0.75
Outputs:
- mixed: bfloat16 [65536, 1024], P('seq', 'head')
The draws below stay inside these ranges and needn't reach their ends.
Inputs may be any that keep to these rules, and one draw needn't show every extreme that they name: `row_qkv`: Query, key and value projections of each head, stacked along the middle dimension; columns are grouped by head. `col_qkv`: laid out as row_qkv.
All inputs are finite; a program needn't handle non-finite values.
Results may differ from the reference program's by a relative error of at most 0.034.
Values may be sent and summed in bfloat16 or wider, within the bound.
No kernel may reach another device: no remote copies, remote signals or barrier semaphores. Data moves between devices by JAX's collectives and lax.ppermute only.
A program may use at most 64 MiB of HBM per device.

```python
import math
import jax
import jax.numpy as jnp
from jax import lax

D = 1024
HEADS = 16
COLS = 512
HEAD_DIM = 64
ROWS = 128
TOKENS = 65536
N_HEAD = 4


def projection_draw(key):
    key_q, key_k, key_v = jax.random.split(key, 3)
    base = D ** (-0.5)
    q_part = jnp.clip(jax.random.normal(key_q, (D, D), jnp.float32), -4.0, 4.0) * base
    noise = jnp.clip(jax.random.normal(key_k, (D, D), jnp.float32), -4.0, 4.0) * base
    v_part = jnp.clip(jax.random.normal(key_v, (D, D), jnp.float32), -4.0, 4.0) * (2.0 * base)
    k_part = noise
    stacked = jnp.stack([q_part, k_part, v_part], axis=1)
    return jnp.clip(stacked, -4.0, 4.0).astype(jnp.bfloat16)


def draw_row_qkv(key, part):
    key = jax.random.fold_in(key, 1)
    return projection_draw(key)


def draw_col_qkv(key, part):
    key = jax.random.fold_in(key, 2)
    return projection_draw(key)


def block_levels(stream_key, extent, cuts, smallest, top_value):
    factor_of, own = 1.0, jax.random.fold_in(stream_key, 6)
    for dim, parts in cuts:
        draws = jnp.exp(jax.random.uniform(jax.random.fold_in(own, dim), (parts,), jnp.float32, smallest / len(cuts), top_value / len(cuts)))
        factor_of = factor_of * jnp.repeat(draws, extent[dim] // parts).reshape([-1 if axis == dim else 1 for axis in range(len(extent))])
    return factor_of


def centred(key, dims, scale, most, pieces=(), kind=jnp.bfloat16):
    loudness = block_levels(key, dims, pieces, -0.22, 0.18) if pieces else 1.0
    result = jax.random.normal(key, dims, jnp.float32) * scale * loudness
    return jnp.minimum(jnp.maximum(result, -most), most).astype(kind)


def setup_inputs(seed: int = 0) -> dict:
    arg_keys = jax.random.split(jax.random.key(seed), 8)
    inputs = centred(arg_keys[0], (TOKENS, D), 1.0, 6.0, ((0, 128), (1, 4)))
    row_gain = jnp.clip(1.0 + 0.18 * jax.random.normal(arg_keys[1], (D,), jnp.float32), 0.1, 1.9)
    row_qkv = draw_row_qkv(jax.random.fold_in(arg_keys[7], 71), 0)
    row_out = centred(arg_keys[3], (D, D), (D // 16) ** -0.5, 0.75, ((0, 4),))
    col_gain = jnp.clip(1.0 + 0.18 * jax.random.normal(arg_keys[4], (D,), jnp.float32), 0.1, 1.9)
    col_qkv = draw_col_qkv(jax.random.fold_in(arg_keys[7], 71), 0)
    col_out = centred(arg_keys[6], (D, D), (D // 16) ** -0.5, 0.75, ((0, 4),))
    return {"inputs": inputs, "row_gain": row_gain, "row_qkv": row_qkv, "row_out": row_out, "col_gain": col_gain, "col_qkv": col_qkv, "col_out": col_out}


def norm_rows(values, gain):
    flat = values.astype(jnp.float32)
    mean = lax.optimization_barrier(jnp.mean(flat, axis=-1, keepdims=True))
    centered = flat - mean
    var = lax.optimization_barrier(jnp.mean(centered * centered, axis=-1, keepdims=True))
    return (centered * lax.rsqrt(var + 1e-05) * gain).astype(jnp.bfloat16)

def project(normed, weight):
    width = weight.shape[2]
    combined = jnp.dot(normed, weight.reshape(weight.shape[0], 3 * width), preferred_element_type=jnp.float32).astype(jnp.bfloat16)
    return (combined[:, :width], combined[:, width:2 * width], combined[:, 2 * width:])

def attend(query, keys, values, allowed):
    scores = jnp.einsum('...qhe,...khe->...hqk', query.astype(jnp.float32), keys.astype(jnp.float32)) * HEAD_DIM ** (-0.5)
    scores = jnp.where(allowed, scores, -1e+30)
    peak = lax.optimization_barrier(jnp.max(scores, axis=-1, keepdims=True))
    expo = jnp.exp(scores - peak)
    weights = (expo / lax.optimization_barrier(jnp.sum(expo, axis=-1, keepdims=True))).astype(jnp.bfloat16)
    return jnp.einsum('...hqk,...khe->...qhe', weights.astype(jnp.float32), values.astype(jnp.float32)).astype(jnp.bfloat16)

def heads_out(att, weight, resid):
    group = D // N_HEAD
    total = jnp.zeros((att.shape[0], D), jnp.float32)
    for index in range(N_HEAD):
        term = jnp.dot(att[:, index * group:(index + 1) * group], weight[index * group:(index + 1) * group], preferred_element_type=jnp.float32)
        term = lax.optimization_barrier(term.astype(jnp.bfloat16))
        total = total + term.astype(jnp.float32)
    return (resid.astype(jnp.float32) + total).astype(jnp.bfloat16)

def row_layer(source, gain, weight, out_weight):
    query, keys, values = project(norm_rows(source, gain), weight)
    key_pad = jnp.concatenate([jnp.zeros((COLS, D), jnp.bfloat16), keys], axis=0)
    val_pad = jnp.concatenate([jnp.zeros((COLS, D), jnp.bfloat16), values], axis=0)
    column = jnp.arange(COLS, dtype=jnp.int32)[:, None]
    slot = jnp.arange(2 * COLS, dtype=jnp.int32)[None, :]

    def one_row(row):
        start = (row * COLS).astype(jnp.int32)
        keys_row = lax.dynamic_slice_in_dim(key_pad, start, 2 * COLS, 0).reshape(2 * COLS, HEADS, HEAD_DIM)
        vals_row = lax.dynamic_slice_in_dim(val_pad, start, 2 * COLS, 0).reshape(2 * COLS, HEADS, HEAD_DIM)
        query_row = lax.dynamic_slice_in_dim(query, start, COLS, 0).reshape(COLS, HEADS, HEAD_DIM)
        allowed = (slot >= column + 1) & (slot <= column + COLS) & ((row > 0) | (slot >= COLS))
        return attend(query_row, keys_row, vals_row, allowed).reshape(COLS, D)
    att = lax.map(one_row, jnp.arange(ROWS, dtype=jnp.int32)).reshape(TOKENS, D)
    return heads_out(att, out_weight, source)

def col_layer(hidden, gain, weight, out_weight):
    query, keys, values = project(norm_rows(hidden, gain), weight)
    block = math.gcd(COLS, 32)

    def by_column(values_in):
        moved = values_in.reshape(ROWS, COLS, D).transpose(1, 0, 2)
        return moved.reshape(COLS // block, block, ROWS, HEADS, HEAD_DIM)
    allowed = jnp.arange(ROWS, dtype=jnp.int32)[:, None] >= jnp.arange(ROWS, dtype=jnp.int32)[None, :]

    def one_block(items):
        return attend(items[0], items[1], items[2], allowed)
    att = lax.map(one_block, (by_column(query), by_column(keys), by_column(values)))
    att = att.reshape(COLS, ROWS, D).transpose(1, 0, 2).reshape(TOKENS, D)
    return heads_out(att, out_weight, hidden)

def reference(inputs, row_gain, row_qkv, row_out, col_gain, col_qkv, col_out):
    hidden = row_layer(inputs, row_gain, row_qkv, row_out)
    return col_layer(hidden, col_gain, col_qkv, col_out)
```

```python
import functools

import jax
import jax.numpy as jnp
from jax import lax
from jax.experimental import pallas as pl
from jax.experimental.pallas import tpu as pltpu
from jax.sharding import Mesh, PartitionSpec as P

COLS = 512
HEAD_DIM = 64
SEQ = ("yh", "z", "x")
HEAD = ("yl", "c")
GROUP = 256
PARTS = 4
HEADS_HERE = GROUP // HEAD_DIM
MIB = 1 << 20
VMEM = pl.BlockSpec(memory_space=pltpu.VMEM)
SMEM = pl.BlockSpec(memory_space=pltpu.SMEM)


def dot(a, b):
    return jnp.dot(a, b, preferred_element_type=jnp.float32)


def dot_t(a, b):
    return lax.dot_general(a, b, (((1,), (1,)), ((), ())), preferred_element_type=jnp.float32)


def normed_pieces(pieces, gains):
    flat = [p.astype(jnp.float32) for p in pieces]
    width = sum(p.shape[1] for p in pieces)
    mean = sum(jnp.sum(p, axis=-1, keepdims=True) for p in flat) / width
    flat = [p - mean for p in flat]
    var = sum(jnp.sum(p * p, axis=-1, keepdims=True) for p in flat) / width
    scale = lax.rsqrt(var + 1e-05)
    return [(p * scale * g).astype(jnp.bfloat16) for p, g in zip(flat, gains)]


def row_project_kernel(place, near, far, gain, weight, query, kv):
    first = [place[0], place[1]]
    block = 256

    def step(i):
        rows = pl.ds(pl.multiple_of(i * block, block), block)
        order = [first[0], first[0] + 1, first[1], first[1] + 1]
        pieces = [near[0, rows, :], near[1, rows, :], far[0, rows, :], far[1, rows, :]]
        normed = normed_pieces(pieces, [gain[n] for n in order])
        total = sum(dot(p, weight[n]) for p, n in zip(normed, order)).astype(jnp.bfloat16)
        query[rows, :] = total[:, :GROUP]
        kv[0, rows, :] = total[:, GROUP : 2 * GROUP]
        kv[1, rows, :] = total[:, 2 * GROUP :]

    pl.loop(0, COLS // block)(step)


def row_project(place, near, far, gain, weight):
    return pl.pallas_call(
        row_project_kernel,
        out_shape=(
            jax.ShapeDtypeStruct((COLS, GROUP), jnp.bfloat16),
            jax.ShapeDtypeStruct((2, COLS, GROUP), jnp.bfloat16),
        ),
        in_specs=[SMEM, VMEM, VMEM, VMEM, VMEM],
        out_specs=(VMEM, VMEM),
        compiler_params=pltpu.CompilerParams(vmem_limit_bytes=24 * MIB),
        cost_estimate=pl.CostEstimate(
            flops=2 * COLS * 1024 * 768, bytes_accessed=4 * MIB, transcendentals=COLS
        ),
        name="row_project",
    )(place, near, far, gain, weight)


def head_mask(rows, head):
    lane = lax.broadcasted_iota(jnp.int32, (rows, GROUP), 1)
    return (lane >= head * HEAD_DIM) & (lane < (head + 1) * HEAD_DIM)


def row_attend_kernel(place, query, kv, before, out):
    block = 256
    blocked = jnp.where(place[2] > 0, 0.0, -1e30).astype(jnp.float32)
    row = lax.broadcasted_iota(jnp.int32, (block, block), 0)
    col = lax.broadcasted_iota(jnp.int32, (block, block), 1)
    late, early = col > row, col <= row
    scale = HEAD_DIM ** (-0.5)
    for half in range(2):
        rows = slice(half * block, (half + 1) * block)
        if half == 0:
            keys = [before[0, :block], before[0, block:], kv[0, :block]]
            vals = [before[1, :block], before[1, block:], kv[1, :block]]
        else:
            keys = [before[0, block:], kv[0, :block], kv[0, block:]]
            vals = [before[1, block:], kv[1, :block], kv[1, block:]]
        q = query[rows, :]
        total = jnp.zeros((block, GROUP), jnp.float32)
        for head in range(HEADS_HERE):
            mask = head_mask(block, head)
            qh = jnp.where(mask, q * jnp.bfloat16(scale), jnp.bfloat16(0))
            s0, s1, s2 = [dot_t(qh, k) for k in keys]
            s0 = jnp.where(late, s0, -1e30) + blocked
            if half == 0:
                s1 = s1 + blocked
            s2 = jnp.where(early, s2, -1e30)
            peak = jnp.max(jnp.maximum(jnp.maximum(s0, s1), s2), axis=-1, keepdims=True)
            p = [jnp.exp(s - peak) for s in (s0, s1, s2)]
            norm = jnp.sum(p[0] + p[1] + p[2], axis=-1, keepdims=True)
            acc = sum(dot(w.astype(jnp.bfloat16), v) for w, v in zip(p, vals))
            total = jnp.where(mask, acc / norm, total)
        out[rows, :] = total.astype(jnp.bfloat16)


def row_attend(place, query, kv, before):
    return pl.pallas_call(
        row_attend_kernel,
        out_shape=jax.ShapeDtypeStruct((COLS, GROUP), jnp.bfloat16),
        in_specs=[SMEM, VMEM, VMEM, VMEM],
        out_specs=VMEM,
        compiler_params=pltpu.CompilerParams(vmem_limit_bytes=24 * MIB),
        cost_estimate=pl.CostEstimate(
            flops=4 * COLS * 768 * 1024, bytes_accessed=2 * MIB, transcendentals=4 * COLS * 768
        ),
        name="row_attend",
    )(place, query, kv, before)


ROW_OUT, COL_QKV, COL_OUT, WEIGHT_ROWS = 0, 1024, 4096, 5120


def pack_weights(row_out, col_qkv, col_out):
    def blocks(w):
        return w.reshape(GROUP, PARTS, GROUP).transpose(1, 0, 2).reshape(PARTS * GROUP, GROUP)

    return jnp.concatenate(
        [blocks(row_out), col_qkv.transpose(1, 0, 2).reshape(3 * 1024, GROUP), blocks(col_out)], axis=0
    )


def row_out_kernel(place, att, near, far, w0, w1, w2, w3, out):
    rows = pl.ds(pl.multiple_of(place[3] * 128, 128), 128)
    groups = [place[0] + place[4], place[0] + 1 - place[4], place[1] + place[4], place[1] + 1 - place[4]]
    parts = [att[g] for g in groups]

    def resid(n):
        use_near = (n // 2) * 2 == place[0]
        return jnp.where(use_near, near[n % 2, rows, :], far[n % 2, rows, :])

    for n in range(PARTS):
        total = sum(
            dot(p, w[ROW_OUT + n * GROUP : ROW_OUT + (n + 1) * GROUP, :])
            for p, w in zip(parts, (w0, w1, w2, w3))
        )
        out[:, n * GROUP : (n + 1) * GROUP] = (resid(n).astype(jnp.float32) + total).astype(jnp.bfloat16)


def row_output(place, att, near, far, weights):
    weights = [w[ROW_OUT : ROW_OUT + 1024] for w in weights]
    return pl.pallas_call(
        row_out_kernel,
        out_shape=jax.ShapeDtypeStruct((128, 1024), jnp.bfloat16),
        in_specs=[SMEM] + [VMEM] * 7,
        out_specs=VMEM,
        compiler_params=pltpu.CompilerParams(vmem_limit_bytes=24 * MIB),
        cost_estimate=pl.CostEstimate(
            flops=2 * 128 * 1024 * 1024, bytes_accessed=4 * MIB, transcendentals=0
        ),
        name="row_output",
    )(place, att, near, far, *weights)


def col_layer_kernel(hidden, gain, w0, w1, w2, w3, out):
    h = hidden[...]
    pieces = [h[:, n * GROUP : (n + 1) * GROUP] for n in range(PARTS)]
    normed = normed_pieces(pieces, [gain[n] for n in range(PARTS)])
    normed = jnp.concatenate(normed, axis=1)
    rows = h.shape[0]
    allowed = lax.broadcasted_iota(jnp.int32, (rows, rows), 0) >= lax.broadcasted_iota(
        jnp.int32, (rows, rows), 1
    )
    scale = HEAD_DIM ** (-0.5)
    atts = []
    for w in (w0, w1, w2, w3):
        q, k, v = [
            dot(normed, w[COL_QKV + i * 1024 : COL_QKV + (i + 1) * 1024, :]).astype(jnp.bfloat16)
            for i in range(3)
        ]
        total = jnp.zeros((rows, GROUP), jnp.float32)
        for head in range(HEADS_HERE):
            mask = head_mask(rows, head)
            qh = jnp.where(mask, q * jnp.bfloat16(scale), jnp.bfloat16(0))
            s = jnp.where(allowed, dot_t(qh, k), -1e30)
            p = jnp.exp(s - jnp.max(s, axis=-1, keepdims=True))
            norm = jnp.sum(p, axis=-1, keepdims=True)
            total = jnp.where(mask, dot(p.astype(jnp.bfloat16), v) / norm, total)
        atts.append(total.astype(jnp.bfloat16))
    for n in range(PARTS):
        total = sum(
            dot(a, w[COL_OUT + n * GROUP : COL_OUT + (n + 1) * GROUP, :])
            for a, w in zip(atts, (w0, w1, w2, w3))
        )
        out[n] = (pieces[n].astype(jnp.float32) + total).astype(jnp.bfloat16)


def col_layer(hidden, gain, weights):
    return pl.pallas_call(
        col_layer_kernel,
        out_shape=jax.ShapeDtypeStruct((PARTS, 128, GROUP), jnp.bfloat16),
        in_specs=[VMEM] * 6,
        out_specs=VMEM,
        compiler_params=pltpu.CompilerParams(vmem_limit_bytes=40 * MIB),
        cost_estimate=pl.CostEstimate(
            flops=2 * 128 * 1024 * 4096, bytes_accessed=10 * MIB, transcendentals=16 * 128 * 128
        ),
        name="col_layer",
    )(hidden, gain, *weights)


def on_device(inputs, row_gain, row_qkv, row_out, col_gain, col_qkv, col_out):
    yl, core = lax.axis_index("yl"), lax.axis_index("c")
    place = jnp.stack(
        [yl * 2, (1 - yl) * 2, lax.axis_index(SEQ), yl * 2 + core, core, core]
    ).astype(jnp.int32)

    with jax.named_scope("gather_inputs"):
        other = lax.ppermute(inputs, "yl", [(0, 1), (1, 0)])
        near = lax.all_gather(inputs, "c", axis=0)
        far = lax.all_gather(other, "c", axis=0)

    with jax.named_scope("gather_weights"):
        mine = pack_weights(row_out, col_qkv, col_out)
        route = []
        for yh in range(4):
            a, b = yh * 4, yh * 4 + 2
            route += [(a, b), (b, a)]
            a, b = yh * 4 + 3, ((yh + 1) % 4) * 4 + 1
            route += [(a, b), (b, a)]
        mine, far = lax.optimization_barrier((mine, far))
        theirs = lax.ppermute(mine, ("yh", "yl", "c"), route)
        mine_swapped = lax.ppermute(mine, "c", [(0, 1), (1, 0)])
        theirs_swapped = lax.ppermute(theirs, "c", [(0, 1), (1, 0)])
        weights = [mine, mine_swapped, theirs, theirs_swapped]

    query, kv = row_project(
        place, near, far, row_gain.reshape(PARTS, 1, GROUP), row_qkv.reshape(PARTS, GROUP, 3 * GROUP)
    )
    before = lax.ppermute(kv, SEQ, [(i, i + 1) for i in range(127)])
    att = row_attend(place, query, kv, before)
    att = lax.all_to_all(att.reshape(PARTS, 128, GROUP), HEAD, 0, 0, tiled=True)
    hidden = row_output(place, att, near, far, weights)
    hidden = lax.all_to_all(hidden.reshape(128, 8, 128), SEQ, 0, 0, tiled=True)
    mixed = col_layer(hidden.reshape(128, 1024), col_gain.reshape(PARTS, 1, GROUP), weights)
    mixed = lax.all_to_all(mixed.reshape(512, 2, 128), HEAD + SEQ, 0, 0, tiled=True)
    return mixed.reshape(512, GROUP)


def solution(mesh):
    fine = Mesh(mesh.devices.reshape(4, 8, 4, 2, 2), SEQ + HEAD)
    return jax.shard_map(
        on_device,
        mesh=fine,
        in_specs=(
            P(SEQ, HEAD),
            P(),
            P(None, None, HEAD),
            P(HEAD, None),
            P(),
            P(None, None, HEAD),
            P(HEAD, None),
        ),
        out_specs=P(SEQ, HEAD),
        check_vma=False,
    )
```

```python
import functools

import jax
import jax.numpy as jnp
from jax import lax
from jax.experimental import pallas as pl
from jax.experimental.pallas import tpu as pltpu
from jax.sharding import Mesh, PartitionSpec as P

COLS = 512
HEAD_DIM = 64
SEQ = ("yh", "z", "x")
HEAD = ("yl", "c")
GROUP = 256
PARTS = 4
HEADS_HERE = GROUP // HEAD_DIM
MIB = 1 << 20
VMEM = pl.BlockSpec(memory_space=pltpu.VMEM)
SMEM = pl.BlockSpec(memory_space=pltpu.SMEM)


def dot(a, b):
    return jnp.dot(a, b, preferred_element_type=jnp.float32)


def dot_t(a, b):
    return lax.dot_general(a, b, (((1,), (1,)), ((), ())), preferred_element_type=jnp.float32)


def normed_pieces(pieces, gains):
    flat = [p.astype(jnp.float32) for p in pieces]
    width = sum(p.shape[1] for p in pieces)
    mean = sum(jnp.sum(p, axis=-1, keepdims=True) for p in flat) / width
    flat = [p - mean for p in flat]
    var = sum(jnp.sum(p * p, axis=-1, keepdims=True) for p in flat) / width
    scale = lax.rsqrt(var + 1e-05)
    return [(p * scale * g).astype(jnp.bfloat16) for p, g in zip(flat, gains)]


def project(normed, order, weight, which):
    return sum(dot(p, weight[which, n]) for p, n in zip(normed, order)).astype(jnp.bfloat16)


def head_mask(rows, head):
    lane = lax.broadcasted_iota(jnp.int32, (rows, GROUP), 1)
    return (lane >= head * HEAD_DIM) & (lane < (head + 1) * HEAD_DIM)


def one_head(query, head):
    return jnp.where(head_mask(query.shape[0], head), query, jnp.bfloat16(0))


def triangle(block):
    row = lax.broadcasted_iota(jnp.int32, (block, block), 0)
    col = lax.broadcasted_iota(jnp.int32, (block, block), 1)
    return row, col


def attend_blocks(query, keys, vals, adjust):
    rows = query.shape[0]
    peak_all = norm_all = acc_all = jnp.zeros((rows, GROUP), jnp.float32)
    for head in range(HEADS_HERE):
        mask = head_mask(rows, head)
        qh = one_head(query, head)
        scores = [f(dot_t(qh, k)) for k, f in zip(keys, adjust)]
        peak = functools.reduce(jnp.maximum, scores)
        peak = jnp.max(peak, axis=-1, keepdims=True)
        expo = [jnp.exp(s - peak) for s in scores]
        norm = jnp.sum(sum(expo[1:], expo[0]), axis=-1, keepdims=True)
        acc = sum(dot(w.astype(jnp.bfloat16), v) for w, v in zip(expo, vals))
        peak_all = jnp.where(mask, peak, peak_all)
        norm_all = jnp.where(mask, norm, norm_all)
        acc_all = jnp.where(mask, acc, acc_all)
    return peak_all, norm_all, acc_all


BLOCK = 256
SCALE = HEAD_DIM ** (-0.5)


def row_own_kernel(place, near, far, gain, weight, query, peak, norm, acc, resid, kv):
    order = [place[0], place[0] + 1, place[1], place[1] + 1]
    mine = pl.ds(pl.multiple_of(place[3] * 128, 128), 128)
    for n, piece in zip(order, (near[0, mine], near[1, mine], far[0, mine], far[1, mine])):
        resid[n] = piece
    row, col = triangle(BLOCK)
    for i in range(COLS // BLOCK):
        rows = slice(i * BLOCK, (i + 1) * BLOCK)
        pieces = [near[0, rows], near[1, rows], far[0, rows], far[1, rows]]
        normed = normed_pieces(pieces, [gain[n] for n in order])
        query[rows] = project(normed, order, weight, 0) * jnp.bfloat16(SCALE)
        kv[0, rows] = project(normed, order, weight, 1)
        kv[1, rows] = project(normed, order, weight, 2)
    for i in range(COLS // BLOCK):
        rows = slice(i * BLOCK, (i + 1) * BLOCK)
        parts = [slice(j * BLOCK, (j + 1) * BLOCK) for j in range(i + 1)]
        adjust = [lambda s: s] * i + [lambda s: jnp.where(col <= row, s, -1e30)]
        peak[rows], norm[rows], acc[rows] = attend_blocks(
            query[rows], [kv[0, p] for p in parts], [kv[1, p] for p in parts], adjust
        )


def row_own(place, near, far, gain, weight):
    return pl.pallas_call(
        row_own_kernel,
        out_shape=(
            jax.ShapeDtypeStruct((COLS, GROUP), jnp.bfloat16),
            *[jax.ShapeDtypeStruct((COLS, GROUP), jnp.float32)] * 3,
            jax.ShapeDtypeStruct((PARTS, 128, GROUP), jnp.bfloat16),
        ),
        in_specs=[SMEM, VMEM, VMEM, VMEM, VMEM],
        out_specs=(VMEM,) * 5,
        scratch_shapes=[pltpu.VMEM((2, COLS, GROUP), jnp.bfloat16)],
        compiler_params=pltpu.CompilerParams(vmem_limit_bytes=16 * MIB),
        cost_estimate=pl.CostEstimate(
            flops=2 * COLS * 1024 * 768 + 4 * COLS * 384 * 1024,
            bytes_accessed=5 * MIB,
            transcendentals=4 * COLS * 384,
        ),
        name="row_own",
    )(place, near, far, gain, weight)


def row_halo_kernel(place, near, far, gain, weight, query, peak, norm, acc, out, kv):
    order = [place[0], place[0] + 1, place[1], place[1] + 1]
    row, col = triangle(BLOCK)
    blocked = jnp.where(place[2] > 0, 0.0, -1e30).astype(jnp.float32)
    blocks = COLS // BLOCK
    for i in range(blocks):
        rows = slice(i * BLOCK, (i + 1) * BLOCK)
        pieces = [near[0, rows], near[1, rows], far[0, rows], far[1, rows]]
        normed = normed_pieces(pieces, [gain[n] for n in order])
        kv[0, rows] = project(normed, order, weight, 1)
        kv[1, rows] = project(normed, order, weight, 2)
    for i in range(blocks):
        rows = slice(i * BLOCK, (i + 1) * BLOCK)
        parts = [slice(j * BLOCK, (j + 1) * BLOCK) for j in range(i, blocks)]
        adjust = [lambda s: jnp.where(col > row, s, -1e30) + blocked] + [lambda s: s + blocked] * (blocks - 1 - i)
        peak2, norm2, acc2 = attend_blocks(
            query[rows], [kv[0, p] for p in parts], [kv[1, p] for p in parts], adjust
        )
        top = jnp.maximum(peak[rows], peak2)
        one, two = jnp.exp(peak[rows] - top), jnp.exp(peak2 - top)
        att = (acc[rows] * one + acc2 * two) / (norm[rows] * one + norm2 * two)
        att = att.astype(jnp.bfloat16)
        for j in range(BLOCK // 128):
            out[i * BLOCK // 128 + j] = att[j * 128 : (j + 1) * 128]


def row_halo(place, near, far, gain, weight, state):
    return pl.pallas_call(
        row_halo_kernel,
        out_shape=jax.ShapeDtypeStruct((PARTS, 128, GROUP), jnp.bfloat16),
        in_specs=[SMEM] + [VMEM] * 8,
        out_specs=VMEM,
        scratch_shapes=[pltpu.VMEM((2, COLS, GROUP), jnp.bfloat16)],
        compiler_params=pltpu.CompilerParams(vmem_limit_bytes=16 * MIB),
        cost_estimate=pl.CostEstimate(
            flops=2 * COLS * 1024 * 512 + 4 * COLS * 384 * 1024,
            bytes_accessed=5 * MIB,
            transcendentals=4 * COLS * 384,
        ),
        name="row_halo",
    )(place, near, far, gain, weight, *state)


OUT_ROWS, COL_ROWS = 1024, 4096


def column_blocks(w):
    return w.reshape(GROUP, PARTS, GROUP).transpose(1, 0, 2).reshape(PARTS * GROUP, GROUP)


ANY = pl.BlockSpec(memory_space=pl.ANY)


def row_out_kernel(place, att, resid, weights, swapped, out, held, sem):
    copies = [pltpu.make_async_copy(w, held.at[i], sem.at[i]) for i, w in enumerate((weights, swapped))]
    for copy in copies:
        copy.start()
    groups = [place[0] + place[4], place[1] + place[4], place[0] + 1 - place[4], place[1] + 1 - place[4]]
    parts = [att[g] for g in groups]
    for copy in copies:
        copy.wait()
    for n in range(PARTS):
        cols = slice(n * GROUP, (n + 1) * GROUP)
        total = 0
        for i, p in enumerate(parts):
            first = (i % 2) * OUT_ROWS + n * GROUP
            total = total + dot(p, held[i // 2, first : first + GROUP, :])
        out[:, cols] = (resid[n].astype(jnp.float32) + total).astype(jnp.bfloat16)


def row_output(place, att, resid, weights, swapped):
    return pl.pallas_call(
        row_out_kernel,
        out_shape=jax.ShapeDtypeStruct((128, 1024), jnp.bfloat16),
        in_specs=[SMEM, VMEM, VMEM, ANY, ANY],
        out_specs=VMEM,
        scratch_shapes=[pltpu.VMEM((2, 2 * OUT_ROWS, GROUP), jnp.bfloat16), pltpu.SemaphoreType.DMA((2,))],
        compiler_params=pltpu.CompilerParams(vmem_limit_bytes=10 * MIB),
        cost_estimate=pl.CostEstimate(
            flops=2 * 128 * 1024 * 1024, bytes_accessed=4 * MIB, transcendentals=0
        ),
        name="row_output",
    )(place, att, resid, weights, swapped)


def col_layer_kernel(hidden, gain, w0, w1, w2, w3, out, held, sem):
    copies = [
        pltpu.make_async_copy(w, held.at[i], sem.at[i]) for i, w in enumerate((w0, w1, w2, w3))
    ]
    for copy in copies:
        copy.start()
    h = hidden[...]
    pieces = [h[:, n * GROUP : (n + 1) * GROUP] for n in range(PARTS)]
    normed = normed_pieces(pieces, [gain[n] for n in range(PARTS)])
    normed = jnp.concatenate(normed, axis=1)
    row, col = triangle(h.shape[0])
    atts = []
    for i, copy in enumerate(copies):
        copy.wait()
        q, k, v = [
            dot(normed, held[i, j * 1024 : (j + 1) * 1024, :]).astype(jnp.bfloat16) for j in range(3)
        ]
        _, norm, acc = attend_blocks(
            q * jnp.bfloat16(SCALE), [k], [v], [lambda s: jnp.where(col <= row, s, -1e30)]
        )
        atts.append((acc / norm).astype(jnp.bfloat16))
    for n in range(PARTS):
        rows = slice(3 * 1024 + n * GROUP, 3 * 1024 + (n + 1) * GROUP)
        total = sum(dot(a, held[i, rows, :]) for i, a in enumerate(atts))
        out[n] = (pieces[n].astype(jnp.float32) + total).astype(jnp.bfloat16)


def col_layer(hidden, gain, weights):
    return pl.pallas_call(
        col_layer_kernel,
        out_shape=jax.ShapeDtypeStruct((PARTS, 128, GROUP), jnp.bfloat16),
        in_specs=[VMEM] * 2 + [ANY] * 4,
        out_specs=VMEM,
        scratch_shapes=[pltpu.VMEM((PARTS, COL_ROWS, GROUP), jnp.bfloat16), pltpu.SemaphoreType.DMA((PARTS,))],
        compiler_params=pltpu.CompilerParams(vmem_limit_bytes=20 * MIB),
        cost_estimate=pl.CostEstimate(
            flops=2 * 128 * 1024 * 4096, bytes_accessed=10 * MIB, transcendentals=16 * 128 * 128
        ),
        name="col_layer",
    )(hidden, gain, *weights)


SWAP = [(0, 1), (1, 0)]


def after(value, *others):
    return lax.optimization_barrier((value, *others))[0]


def cross_route():
    route = []
    for yh in range(4):
        a, b = yh * 4, yh * 4 + 2
        route += [(a, b), (b, a)]
        a, b = yh * 4 + 3, ((yh + 1) % 4) * 4 + 1
        route += [(a, b), (b, a)]
    return route


def on_device(inputs, row_gain, row_qkv, row_out, col_gain, col_qkv, col_out):
    yl, core = lax.axis_index("yl"), lax.axis_index("c")
    place = jnp.stack([yl * 2, (1 - yl) * 2, lax.axis_index(SEQ), yl * 2 + core, core]).astype(jnp.int32)
    row_gain = row_gain.reshape(PARTS, 1, GROUP)
    row_qkv = row_qkv.transpose(1, 0, 2).reshape(3, PARTS, GROUP, GROUP)
    everywhere = ("yh", "yl", "c")

    other = lax.ppermute(inputs, "yl", SWAP)
    before = lax.ppermute(inputs, SEQ, [(i, i + 1) for i in range(127)])
    near = lax.all_gather(inputs, "c", axis=0)
    far = lax.all_gather(after(other, near), "c", axis=0)
    before_other = lax.ppermute(after(before, far), "yl", SWAP)

    out_mine = column_blocks(row_out)
    col_mine = jnp.concatenate([col_qkv.transpose(1, 0, 2).reshape(3 * 1024, GROUP), column_blocks(col_out)])
    out_mine = after(out_mine, far)
    out_theirs = lax.ppermute(out_mine, everywhere, cross_route())
    col_mine = after(col_mine, before, far)
    col_theirs = lax.ppermute(col_mine, everywhere, cross_route())
    col_swapped = lax.ppermute(col_mine, "c", SWAP)

    *state, resid = row_own(place, near, far, row_gain, row_qkv)
    before_near = lax.all_gather(after(before, resid), "c", axis=0)
    before_far = lax.all_gather(after(before_other, before_near), "c", axis=0)
    out_both = jnp.concatenate([out_mine, after(out_theirs, before_far)])
    out_swapped = lax.ppermute(out_both, "c", SWAP)
    att = row_halo(place, before_near, before_far, row_gain, row_qkv, state)
    att = lax.all_to_all(att, HEAD, 0, 0, tiled=True)
    hidden = row_output(place, att, resid, out_both, out_swapped)
    col_theirs = after(col_theirs, hidden)
    col_theirs_swapped = lax.ppermute(col_theirs, "c", SWAP)
    hidden = lax.all_to_all(hidden.reshape(128, 8, 128), SEQ, 0, 0, tiled=True)
    mixed = col_layer(
        hidden.reshape(128, 1024),
        col_gain.reshape(PARTS, 1, GROUP),
        [col_mine, col_swapped, col_theirs, col_theirs_swapped],
    )
    mixed = lax.all_to_all(mixed.reshape(512, 2, 128), HEAD + SEQ, 0, 0, tiled=True)
    return mixed.reshape(512, GROUP)


def solution(mesh):
    fine = Mesh(mesh.devices.reshape(4, 8, 4, 2, 2), SEQ + HEAD)
    return jax.shard_map(
        on_device,
        mesh=fine,
        in_specs=(
            P(SEQ, HEAD),
            P(),
            P(None, None, HEAD),
            P(HEAD, None),
            P(),
            P(None, None, HEAD),
            P(HEAD, None),
        ),
        out_specs=P(SEQ, HEAD),
        check_vma=False,
    )
```

```python
import functools

import jax
import jax.numpy as jnp
from jax import lax
from jax.experimental import pallas as pl
from jax.experimental.pallas import tpu as pltpu
from jax.sharding import Mesh, PartitionSpec as P

COLS = 512
HEAD_DIM = 64
SEQ = ("yh", "z", "x")
HEAD = ("yl", "c")
GROUP = 256
PARTS = 4
HEADS_HERE = GROUP // HEAD_DIM
MIB = 1 << 20
VMEM = pl.BlockSpec(memory_space=pltpu.VMEM)
SMEM = pl.BlockSpec(memory_space=pltpu.SMEM)
ANY = pl.BlockSpec(memory_space=pl.ANY)


def dot(a, b):
    return jnp.dot(a, b, preferred_element_type=jnp.float32)


def dot_t(a, b):
    return lax.dot_general(a, b, (((1,), (1,)), ((), ())), preferred_element_type=jnp.float32)


def normed_pieces(pieces, gains):
    flat = [p.astype(jnp.float32) for p in pieces]
    width = sum(p.shape[1] for p in pieces)
    mean = sum(jnp.sum(p, axis=-1, keepdims=True) for p in flat) / width
    flat = [p - mean for p in flat]
    var = sum(jnp.sum(p * p, axis=-1, keepdims=True) for p in flat) / width
    scale = lax.rsqrt(var + 1e-05)
    return [(p * scale * g).astype(jnp.bfloat16) for p, g in zip(flat, gains)]


def project(normed, order, weight, which):
    return sum(dot(p, weight[which, n]) for p, n in zip(normed, order)).astype(jnp.bfloat16)


def head_mask(rows, head):
    lane = lax.broadcasted_iota(jnp.int32, (rows, GROUP), 1)
    return (lane >= head * HEAD_DIM) & (lane < (head + 1) * HEAD_DIM)


def one_head(query, head):
    return jnp.where(head_mask(query.shape[0], head), query, jnp.bfloat16(0))


def triangle(block):
    row = lax.broadcasted_iota(jnp.int32, (block, block), 0)
    col = lax.broadcasted_iota(jnp.int32, (block, block), 1)
    return row, col


def attend_blocks(query, keys, vals, adjust):
    rows = query.shape[0]
    peak_all = norm_all = acc_all = jnp.zeros((rows, GROUP), jnp.float32)
    for head in range(HEADS_HERE):
        mask = head_mask(rows, head)
        qh = one_head(query, head)
        scores = [f(dot_t(qh, k)) for k, f in zip(keys, adjust)]
        peak = functools.reduce(jnp.maximum, scores)
        peak = jnp.max(peak, axis=-1, keepdims=True)
        expo = [jnp.exp(s - peak) for s in scores]
        norm = jnp.sum(sum(expo[1:], expo[0]), axis=-1, keepdims=True)
        acc = sum(dot(w.astype(jnp.bfloat16), v) for w, v in zip(expo, vals))
        peak_all = jnp.where(mask, peak, peak_all)
        norm_all = jnp.where(mask, norm, norm_all)
        acc_all = jnp.where(mask, acc, acc_all)
    return peak_all, norm_all, acc_all


BLOCK = 256
SCALE = HEAD_DIM ** (-0.5)


def row_own_kernel(place, near, far, gain, weight, query, peak, norm, acc, kv):
    order = [place[0], place[0] + 1, place[1], place[1] + 1]
    row, col = triangle(BLOCK)
    for i in range(COLS // BLOCK):
        rows = slice(i * BLOCK, (i + 1) * BLOCK)
        pieces = [near[0, rows], near[1, rows], far[0, rows], far[1, rows]]
        normed = normed_pieces(pieces, [gain[n] for n in order])
        query[rows] = project(normed, order, weight, 0)
        kv[0, rows] = project(normed, order, weight, 1)
        kv[1, rows] = project(normed, order, weight, 2)
    for i in range(COLS // BLOCK):
        rows = slice(i * BLOCK, (i + 1) * BLOCK)
        parts = [slice(j * BLOCK, (j + 1) * BLOCK) for j in range(i + 1)]
        adjust = [lambda s: s] * i + [lambda s: jnp.where(col <= row, s, -1e30)]
        peak[rows], norm[rows], acc[rows] = attend_blocks(
            query[rows], [kv[0, p] for p in parts], [kv[1, p] for p in parts], adjust
        )


def row_own(place, near, far, gain, weight):
    return pl.pallas_call(
        row_own_kernel,
        out_shape=(
            jax.ShapeDtypeStruct((COLS, GROUP), jnp.bfloat16),
            *[jax.ShapeDtypeStruct((COLS, GROUP), jnp.float32)] * 3,
        ),
        in_specs=[SMEM, VMEM, VMEM, VMEM, VMEM],
        out_specs=(VMEM,) * 4,
        scratch_shapes=[
            pltpu.VMEM((2, COLS, GROUP), jnp.bfloat16),
        ],
        compiler_params=pltpu.CompilerParams(vmem_limit_bytes=16 * MIB),
        cost_estimate=pl.CostEstimate(flops=1, bytes_accessed=1, transcendentals=0),
        name="row_own",
    )(place, near, far, gain, weight)


def row_halo_kernel(place, near, far, gain, weight, query, peak, norm, acc, source, out, kv):
    order = [place[0], place[0] + 1, place[1], place[1] + 1]
    row, col = triangle(BLOCK)
    blocked = jnp.where(place[2] > 0, 0.0, -1e30).astype(jnp.float32)
    blocks = COLS // BLOCK
    for i in range(blocks):
        rows = slice(i * BLOCK, (i + 1) * BLOCK)
        pieces = [near[0, rows], near[1, rows], far[0, rows], far[1, rows]]
        normed = normed_pieces(pieces, [gain[n] for n in order])
        kv[0, rows] = project(normed, order, weight, 1)
        kv[1, rows] = project(normed, order, weight, 2)
    for i in range(blocks):
        rows = slice(i * BLOCK, (i + 1) * BLOCK)
        parts = [slice(j * BLOCK, (j + 1) * BLOCK) for j in range(i, blocks)]
        adjust = [lambda s: jnp.where(col > row, s, -1e30) + blocked] + [lambda s: s + blocked] * (blocks - 1 - i)
        peak2, norm2, acc2 = attend_blocks(
            query[rows], [kv[0, p] for p in parts], [kv[1, p] for p in parts], adjust
        )
        top = jnp.maximum(peak[rows], peak2)
        one, two = jnp.exp(peak[rows] - top), jnp.exp(peak2 - top)
        att = (acc[rows] * one + acc2 * two) / (norm[rows] * one + norm2 * two)
        out[rows, :GROUP] = att.astype(jnp.bfloat16)
        out[rows, GROUP:] = source[rows]


def row_halo(place, near, far, gain, weight, state, source):
    return pl.pallas_call(
        row_halo_kernel,
        out_shape=jax.ShapeDtypeStruct((COLS, 2 * GROUP), jnp.bfloat16),
        in_specs=[SMEM] + [VMEM] * 9,
        out_specs=VMEM,
        scratch_shapes=[
            pltpu.VMEM((2, COLS, GROUP), jnp.bfloat16),
        ],
        compiler_params=pltpu.CompilerParams(vmem_limit_bytes=16 * MIB),
        cost_estimate=pl.CostEstimate(flops=1, bytes_accessed=1, transcendentals=0),
        name="row_halo",
    )(place, near, far, gain, weight, *state, source)


QKV_AT, OUT_AT, WEIGHT_ROWS = 1024, 4096, 5120


def column_blocks(w):
    return w.reshape(GROUP, PARTS, GROUP).transpose(1, 0, 2).reshape(PARTS * GROUP, GROUP)


def col_layer_kernel(place, moved, gain, w0, w1, w2, w3, out, held, sem):
    arrays = (w0, w1, w2, w3)
    groups = [place[0] + place[3], place[0] + 1 - place[3], place[1] + place[3], place[1] + 1 - place[3]]
    first = [pltpu.make_async_copy(w.at[:QKV_AT], held.at[i, :QKV_AT], sem.at[0, i]) for i, w in enumerate(arrays)]
    rest = [pltpu.make_async_copy(w.at[QKV_AT:], held.at[i, QKV_AT:], sem.at[1, i]) for i, w in enumerate(arrays)]
    for copy in first + rest:
        copy.start()

    def add_projected(pieces, atts, at):
        result = []
        for n in range(PARTS):
            rows = slice(at + n * GROUP, at + (n + 1) * GROUP)
            total = sum(dot(a, held[i, rows, :]) for i, a in enumerate(atts))
            result.append((pieces[n].astype(jnp.float32) + total).astype(jnp.bfloat16))
        return result

    atts = [moved[g, :, :GROUP] for g in groups]
    for copy in first:
        copy.wait()
    pieces = add_projected([moved[n, :, GROUP:] for n in range(PARTS)], atts, 0)
    normed = normed_pieces(pieces, [gain[n] for n in range(PARTS)])
    normed = jnp.concatenate(normed, axis=1)
    row, col = triangle(normed.shape[0])
    atts = []
    for i, copy in enumerate(rest):
        copy.wait()
        q, k, v = [
            dot(normed, held[i, QKV_AT + j * 1024 : QKV_AT + (j + 1) * 1024, :]).astype(jnp.bfloat16)
            for j in range(3)
        ]
        _, norm, acc = attend_blocks(
            q * jnp.bfloat16(SCALE), [k], [v], [lambda s: jnp.where(col <= row, s, -1e30)]
        )
        atts.append((acc / norm).astype(jnp.bfloat16))
    for n, piece in enumerate(add_projected(pieces, atts, OUT_AT)):
        out[n] = piece


def col_layer(place, moved, gain, weights):
    return pl.pallas_call(
        col_layer_kernel,
        out_shape=jax.ShapeDtypeStruct((PARTS, 128, GROUP), jnp.bfloat16),
        in_specs=[SMEM, VMEM, VMEM] + [ANY] * 4,
        out_specs=VMEM,
        scratch_shapes=[pltpu.VMEM((PARTS, WEIGHT_ROWS, GROUP), jnp.bfloat16), pltpu.SemaphoreType.DMA((2, PARTS))],
        compiler_params=pltpu.CompilerParams(vmem_limit_bytes=20 * MIB),
        cost_estimate=pl.CostEstimate(flops=1, bytes_accessed=1, transcendentals=0),
        name="col_layer",
    )(place, moved, gain, *weights)


SWAP = [(0, 1), (1, 0)]


def after(value, *others):
    return lax.optimization_barrier((value, *others))[0]


def cross_route(outer):
    route = []
    for yh in range(4):
        for core in range(2):
            a = yh * 4 + 2 + core
            b = ((yh + 1) % 4 if core in outer else yh) * 4 + core
            route += [(a, b), (b, a)]
    return route


def on_device(inputs, row_gain, row_qkv, row_out, col_gain, col_qkv, col_out):
    yl, core = lax.axis_index("yl"), lax.axis_index("c")
    place = jnp.stack([yl * 2, (1 - yl) * 2, lax.axis_index(SEQ), core]).astype(jnp.int32)
    row_gain = row_gain.reshape(PARTS, 1, GROUP)
    row_qkv = row_qkv.transpose(1, 0, 2).reshape(3, PARTS, GROUP, GROUP)
    row_qkv = row_qkv * jnp.array([SCALE, 1, 1], jnp.bfloat16)[:, None, None, None]

    other = lax.ppermute(inputs, "yl", SWAP)
    before = lax.ppermute(inputs, SEQ, [(i, i + 1) for i in range(127)])
    near = lax.all_gather(inputs, "c", axis=0)
    far = lax.all_gather(after(other, near), "c", axis=0)
    before_other = lax.ppermute(after(before, far), "yl", SWAP)

    mine = jnp.concatenate(
        [column_blocks(row_out), col_qkv.transpose(1, 0, 2).reshape(3 * 1024, GROUP), column_blocks(col_out)]
    )
    mine, row_qkv = lax.optimization_barrier((mine, row_qkv, before, other, near))[:2]
    theirs = lax.ppermute(mine, ("yh", "yl", "c"), cross_route((1,)))

    state = row_own(place, near, far, row_gain, row_qkv)
    mine_swapped = lax.ppermute(after(mine, state[0]), "c", SWAP)
    before_near = lax.all_gather(after(before, state[0]), "c", axis=0)
    before_far = lax.all_gather(after(before_other, before_near), "c", axis=0)
    sent = row_halo(place, before_near, before_far, row_gain, row_qkv, state, inputs)
    theirs_swapped = lax.ppermute(after(theirs, sent), "c", SWAP)

    moved = lax.all_to_all(sent.reshape(COLS, 4, 128), HEAD + SEQ, 0, 0, tiled=True)
    mixed = col_layer(
        place,
        moved.reshape(PARTS, 128, 2 * GROUP),
        col_gain.reshape(PARTS, 1, GROUP),
        [mine, mine_swapped, theirs, theirs_swapped],
    )
    mixed = lax.all_to_all(mixed.reshape(COLS, 2, 128), HEAD + SEQ, 0, 0, tiled=True)
    return mixed.reshape(COLS, GROUP)


def solution(mesh):
    fine = Mesh(mesh.devices.reshape(4, 8, 4, 2, 2), SEQ + HEAD)
    return jax.shard_map(
        on_device,
        mesh=fine,
        in_specs=(
            P(SEQ, HEAD),
            P(),
            P(None, None, HEAD),
            P(HEAD, None),
            P(),
            P(None, None, HEAD),
            P(HEAD, None),
        ),
        out_specs=P(SEQ, HEAD),
        check_vma=False,
    )
```

```python
import functools

import jax
import jax.numpy as jnp
from jax import lax
from jax.experimental import pallas as pl
from jax.experimental.pallas import tpu as pltpu
from jax.sharding import Mesh, PartitionSpec as P

COLS = 512
HEAD_DIM = 64
SEQ = ("yh", "z", "x")
HEAD = ("yl", "c")
GROUP = 256
PARTS = 4
HEADS_HERE = GROUP // HEAD_DIM
MIB = 1 << 20
VMEM = pl.BlockSpec(memory_space=pltpu.VMEM)
SMEM = pl.BlockSpec(memory_space=pltpu.SMEM)
ANY = pl.BlockSpec(memory_space=pl.ANY)


def dot(a, b):
    return jnp.dot(a, b, preferred_element_type=jnp.float32)


def dot_t(a, b):
    return lax.dot_general(a, b, (((1,), (1,)), ((), ())), preferred_element_type=jnp.float32)


def normed_pieces(pieces, gains):
    flat = [p.astype(jnp.float32) for p in pieces]
    width = sum(p.shape[1] for p in pieces)
    mean = sum(jnp.sum(p, axis=-1, keepdims=True) for p in flat) / width
    flat = [p - mean for p in flat]
    var = sum(jnp.sum(p * p, axis=-1, keepdims=True) for p in flat) / width
    scale = lax.rsqrt(var + 1e-05)
    return [(p * scale * g).astype(jnp.bfloat16) for p, g in zip(flat, gains)]


def project(normed, order, weight, which):
    return sum(dot(p, weight[which, n]) for p, n in zip(normed, order)).astype(jnp.bfloat16)


def head_mask(rows, head):
    lane = lax.broadcasted_iota(jnp.int32, (rows, GROUP), 1)
    return (lane >= head * HEAD_DIM) & (lane < (head + 1) * HEAD_DIM)


def one_head(query, head):
    return jnp.where(head_mask(query.shape[0], head), query, jnp.bfloat16(0))


def triangle(block):
    row = lax.broadcasted_iota(jnp.int32, (block, block), 0)
    col = lax.broadcasted_iota(jnp.int32, (block, block), 1)
    return row, col


def attend_blocks(query, keys, vals, adjust):
    rows = query.shape[0]
    peak_all = norm_all = acc_all = jnp.zeros((rows, GROUP), jnp.float32)
    for head in range(HEADS_HERE):
        mask = head_mask(rows, head)
        qh = one_head(query, head)
        scores = [f(dot_t(qh, k)) for k, f in zip(keys, adjust)]
        peak = functools.reduce(jnp.maximum, scores)
        peak = jnp.max(peak, axis=-1, keepdims=True)
        expo = [jnp.exp(s - peak) for s in scores]
        norm = jnp.sum(sum(expo[1:], expo[0]), axis=-1, keepdims=True)
        acc = sum(dot(w.astype(jnp.bfloat16), v) for w, v in zip(expo, vals))
        peak_all = jnp.where(mask, peak, peak_all)
        norm_all = jnp.where(mask, norm, norm_all)
        acc_all = jnp.where(mask, acc, acc_all)
    return peak_all, norm_all, acc_all


BLOCK = 256
SCALE = HEAD_DIM ** (-0.5)


def row_own_kernel(place, near, far, gain, weight, query, peak, norm, acc, kv):
    order = [place[0], place[0] + 1, place[1], place[1] + 1]
    row, col = triangle(BLOCK)
    for i in range(COLS // BLOCK):
        rows = slice(i * BLOCK, (i + 1) * BLOCK)
        pieces = [near[0, rows], near[1, rows], far[0, rows], far[1, rows]]
        normed = normed_pieces(pieces, [gain[n] for n in order])
        query[rows] = project(normed, order, weight, 0)
        kv[0, rows] = project(normed, order, weight, 1)
        kv[1, rows] = project(normed, order, weight, 2)
    for i in range(COLS // BLOCK):
        rows = slice(i * BLOCK, (i + 1) * BLOCK)
        parts = [slice(j * BLOCK, (j + 1) * BLOCK) for j in range(i + 1)]
        adjust = [lambda s: s] * i + [lambda s: jnp.where(col <= row, s, -1e30)]
        peak[rows], norm[rows], acc[rows] = attend_blocks(
            query[rows], [kv[0, p] for p in parts], [kv[1, p] for p in parts], adjust
        )


def row_own(place, near, far, gain, weight):
    return pl.pallas_call(
        row_own_kernel,
        out_shape=(
            jax.ShapeDtypeStruct((COLS, GROUP), jnp.bfloat16),
            *[jax.ShapeDtypeStruct((COLS, GROUP), jnp.float32)] * 3,
        ),
        in_specs=[SMEM, VMEM, VMEM, VMEM, VMEM],
        out_specs=(VMEM,) * 4,
        scratch_shapes=[
            pltpu.VMEM((2, COLS, GROUP), jnp.bfloat16),
        ],
        compiler_params=pltpu.CompilerParams(vmem_limit_bytes=16 * MIB),
        cost_estimate=pl.CostEstimate(flops=1, bytes_accessed=1, transcendentals=0),
        name="row_own",
    )(place, near, far, gain, weight)


def row_halo_kernel(place, near, far, gain, weight, query, peak, norm, acc, source, out, kv):
    order = [place[0], place[0] + 1, place[1], place[1] + 1]
    row, col = triangle(BLOCK)
    blocked = jnp.where(place[2] > 0, 0.0, -1e30).astype(jnp.float32)
    blocks = COLS // BLOCK
    for i in range(blocks):
        rows = slice(i * BLOCK, (i + 1) * BLOCK)
        pieces = [near[0, rows], near[1, rows], far[0, rows], far[1, rows]]
        normed = normed_pieces(pieces, [gain[n] for n in order])
        kv[0, rows] = project(normed, order, weight, 1)
        kv[1, rows] = project(normed, order, weight, 2)
    for i in range(blocks):
        rows = slice(i * BLOCK, (i + 1) * BLOCK)
        parts = [slice(j * BLOCK, (j + 1) * BLOCK) for j in range(i, blocks)]
        adjust = [lambda s: jnp.where(col > row, s, -1e30) + blocked] + [lambda s: s + blocked] * (blocks - 1 - i)
        peak2, norm2, acc2 = attend_blocks(
            query[rows], [kv[0, p] for p in parts], [kv[1, p] for p in parts], adjust
        )
        top = jnp.maximum(peak[rows], peak2)
        one, two = jnp.exp(peak[rows] - top), jnp.exp(peak2 - top)
        att = (acc[rows] * one + acc2 * two) / (norm[rows] * one + norm2 * two)
        out[rows, :GROUP] = att.astype(jnp.bfloat16)
        out[rows, GROUP:] = source[rows]


def row_halo(place, near, far, gain, weight, state, source):
    return pl.pallas_call(
        row_halo_kernel,
        out_shape=jax.ShapeDtypeStruct((COLS, 2 * GROUP), jnp.bfloat16),
        in_specs=[SMEM] + [VMEM] * 9,
        out_specs=VMEM,
        scratch_shapes=[
            pltpu.VMEM((2, COLS, GROUP), jnp.bfloat16),
        ],
        compiler_params=pltpu.CompilerParams(vmem_limit_bytes=16 * MIB),
        cost_estimate=pl.CostEstimate(flops=1, bytes_accessed=1, transcendentals=0),
        name="row_halo",
    )(place, near, far, gain, weight, *state, source)


QKV_AT, OUT_AT, WEIGHT_ROWS = 1024, 4096, 5120


def column_blocks(w):
    return w.reshape(GROUP, PARTS, GROUP).transpose(1, 0, 2).reshape(PARTS * GROUP, GROUP)


def col_layer_kernel(place, moved, gain, w0, w1, w2, w3, out, held, sem):
    arrays = (w0, w1, w2, w3)
    groups = [place[0] + place[3], place[0] + 1 - place[3], place[1] + place[3], place[1] + 1 - place[3]]
    first = [pltpu.make_async_copy(w.at[:QKV_AT], held.at[i, :QKV_AT], sem.at[0, i]) for i, w in enumerate(arrays)]
    rest = [pltpu.make_async_copy(w.at[QKV_AT:], held.at[i, QKV_AT:], sem.at[1, i]) for i, w in enumerate(arrays)]
    for copy in first + rest:
        copy.start()

    def add_projected(pieces, atts, at):
        result = []
        for n in range(PARTS):
            rows = slice(at + n * GROUP, at + (n + 1) * GROUP)
            total = sum(dot(a, held[i, rows, :]) for i, a in enumerate(atts))
            result.append((pieces[n].astype(jnp.float32) + total).astype(jnp.bfloat16))
        return result

    atts = [moved[g, :, :GROUP] for g in groups]
    for copy in first:
        copy.wait()
    pieces = add_projected([moved[n, :, GROUP:] for n in range(PARTS)], atts, 0)
    normed = normed_pieces(pieces, [gain[n] for n in range(PARTS)])
    normed = jnp.concatenate(normed, axis=1)
    row, col = triangle(normed.shape[0])
    atts = []
    for i, copy in enumerate(rest):
        copy.wait()
        q, k, v = [
            dot(normed, held[i, QKV_AT + j * 1024 : QKV_AT + (j + 1) * 1024, :]).astype(jnp.bfloat16)
            for j in range(3)
        ]
        _, norm, acc = attend_blocks(
            q * jnp.bfloat16(SCALE), [k], [v], [lambda s: jnp.where(col <= row, s, -1e30)]
        )
        atts.append((acc / norm).astype(jnp.bfloat16))
    for n, piece in enumerate(add_projected(pieces, atts, OUT_AT)):
        out[n] = piece


def col_layer(place, moved, gain, weights):
    return pl.pallas_call(
        col_layer_kernel,
        out_shape=jax.ShapeDtypeStruct((PARTS, 128, GROUP), jnp.bfloat16),
        in_specs=[SMEM, VMEM, VMEM] + [ANY] * 4,
        out_specs=VMEM,
        scratch_shapes=[pltpu.VMEM((PARTS, WEIGHT_ROWS, GROUP), jnp.bfloat16), pltpu.SemaphoreType.DMA((2, PARTS))],
        compiler_params=pltpu.CompilerParams(vmem_limit_bytes=20 * MIB),
        cost_estimate=pl.CostEstimate(flops=1, bytes_accessed=1, transcendentals=0),
        name="col_layer",
    )(place, moved, gain, *weights)


SWAP = [(0, 1), (1, 0)]


def after(value, *others):
    return lax.optimization_barrier((value, *others))[0]


def cross_route(outer):
    route = []
    for yh in range(4):
        for core in range(2):
            a = yh * 4 + 2 + core
            b = ((yh + 1) % 4 if core in outer else yh) * 4 + core
            route += [(a, b), (b, a)]
    return route


def on_device(inputs, row_gain, row_qkv, row_out, col_gain, col_qkv, col_out):
    yl, core = lax.axis_index("yl"), lax.axis_index("c")
    place = jnp.stack([yl * 2, (1 - yl) * 2, lax.axis_index(SEQ), core]).astype(jnp.int32)
    row_gain = row_gain.reshape(PARTS, 1, GROUP)
    row_qkv = row_qkv.transpose(1, 0, 2).reshape(3, PARTS, GROUP, GROUP)
    row_qkv = row_qkv * jnp.array([SCALE, 1, 1], jnp.bfloat16)[:, None, None, None]

    other = lax.ppermute(inputs, "yl", SWAP)
    before = lax.ppermute(inputs, SEQ, [(i, i + 1) for i in range(127)])
    near = lax.all_gather(inputs, "c", axis=0)
    other, before = lax.optimization_barrier((other, before, near))[:2]
    before_other = lax.ppermute(before, "yl", SWAP)
    far = lax.all_gather(other, "c", axis=0)
    before_near = lax.all_gather(after(before, far), "c", axis=0)
    before_far = lax.all_gather(after(before_other, before_near), "c", axis=0)

    mine = jnp.concatenate(
        [column_blocks(row_out), col_qkv.transpose(1, 0, 2).reshape(3 * 1024, GROUP), column_blocks(col_out)]
    )
    mine, row_qkv = lax.optimization_barrier((mine, row_qkv, near))[:2]
    mine = after(mine, before_far)
    theirs = lax.ppermute(mine, ("yh", "yl", "c"), cross_route((1,)))
    mine_swapped = lax.ppermute(mine, "c", SWAP)

    state = row_own(place, near, after(far, before_far), row_gain, row_qkv)
    sent = row_halo(place, before_near, before_far, row_gain, row_qkv, state, inputs)

    moved = lax.all_to_all(sent.reshape(COLS, 4, 128), HEAD + SEQ, 0, 0, tiled=True)
    theirs_swapped = lax.ppermute(after(theirs, moved), "c", SWAP)
    mixed = col_layer(
        place,
        moved.reshape(PARTS, 128, 2 * GROUP),
        col_gain.reshape(PARTS, 1, GROUP),
        [mine, mine_swapped, theirs, theirs_swapped],
    )
    mixed = lax.all_to_all(mixed.reshape(COLS, 2, 128), HEAD + SEQ, 0, 0, tiled=True)
    return mixed.reshape(COLS, GROUP)


def solution(mesh):
    fine = Mesh(mesh.devices.reshape(4, 8, 4, 2, 2), SEQ + HEAD)
    return jax.shard_map(
        on_device,
        mesh=fine,
        in_specs=(
            P(SEQ, HEAD),
            P(),
            P(None, None, HEAD),
            P(HEAD, None),
            P(),
            P(None, None, HEAD),
            P(HEAD, None),
        ),
        out_specs=P(SEQ, HEAD),
        check_vma=False,
    )
```

```python
import functools

import jax
import jax.numpy as jnp
from jax import lax
from jax.experimental import pallas as pl
from jax.experimental.pallas import tpu as pltpu
from jax.sharding import Mesh, PartitionSpec as P

COLS = 512
HEAD_DIM = 64
SEQ = ("yh", "z", "x")
HEAD = ("yl", "c")
GROUP = 256
PARTS = 4
HEADS_HERE = GROUP // HEAD_DIM
MIB = 1 << 20
VMEM = pl.BlockSpec(memory_space=pltpu.VMEM)
SMEM = pl.BlockSpec(memory_space=pltpu.SMEM)
ANY = pl.BlockSpec(memory_space=pl.ANY)


def dot(a, b):
    return jnp.dot(a, b, preferred_element_type=jnp.float32)


def dot_t(a, b):
    return lax.dot_general(a, b, (((1,), (1,)), ((), ())), preferred_element_type=jnp.float32)


def normed_pieces(pieces, gains):
    flat = [p.astype(jnp.float32) for p in pieces]
    width = sum(p.shape[1] for p in pieces)
    mean = sum(jnp.sum(p, axis=-1, keepdims=True) for p in flat) / width
    flat = [p - mean for p in flat]
    var = sum(jnp.sum(p * p, axis=-1, keepdims=True) for p in flat) / width
    scale = lax.rsqrt(var + 1e-05)
    return [(p * scale * g).astype(jnp.bfloat16) for p, g in zip(flat, gains)]


def project(normed, order, weight, which):
    return sum(dot(p, weight[which, n]) for p, n in zip(normed, order)).astype(jnp.bfloat16)


def head_mask(rows, head):
    lane = lax.broadcasted_iota(jnp.int32, (rows, GROUP), 1)
    return (lane >= head * HEAD_DIM) & (lane < (head + 1) * HEAD_DIM)


def one_head(query, head):
    return jnp.where(head_mask(query.shape[0], head), query, jnp.bfloat16(0))


def triangle(block):
    row = lax.broadcasted_iota(jnp.int32, (block, block), 0)
    col = lax.broadcasted_iota(jnp.int32, (block, block), 1)
    return row, col


def attend_blocks(query, keys, vals, adjust):
    rows = query.shape[0]
    peak_all = norm_all = acc_all = jnp.zeros((rows, GROUP), jnp.float32)
    for head in range(HEADS_HERE):
        mask = head_mask(rows, head)
        qh = one_head(query, head)
        scores = [f(dot_t(qh, k)) for k, f in zip(keys, adjust)]
        peak = functools.reduce(jnp.maximum, scores)
        peak = jnp.max(peak, axis=-1, keepdims=True)
        expo = [jnp.exp(s - peak) for s in scores]
        norm = jnp.sum(sum(expo[1:], expo[0]), axis=-1, keepdims=True)
        acc = sum(dot(w.astype(jnp.bfloat16), v) for w, v in zip(expo, vals))
        peak_all = jnp.where(mask, peak, peak_all)
        norm_all = jnp.where(mask, norm, norm_all)
        acc_all = jnp.where(mask, acc, acc_all)
    return peak_all, norm_all, acc_all


BLOCK = 256
SCALE = HEAD_DIM ** (-0.5)


def row_own_kernel(place, near, far, gain, weight, query, peak, norm, acc, kv):
    order = [place[0], place[0] + 1, place[1], place[1] + 1]
    row, col = triangle(BLOCK)
    for i in range(COLS // BLOCK):
        rows = slice(i * BLOCK, (i + 1) * BLOCK)
        pieces = [near[0, rows], near[1, rows], far[0, rows], far[1, rows]]
        normed = normed_pieces(pieces, [gain[n] for n in order])
        query[rows] = project(normed, order, weight, 0)
        kv[0, rows] = project(normed, order, weight, 1)
        kv[1, rows] = project(normed, order, weight, 2)
    for i in range(COLS // BLOCK):
        rows = slice(i * BLOCK, (i + 1) * BLOCK)
        parts = [slice(j * BLOCK, (j + 1) * BLOCK) for j in range(i + 1)]
        adjust = [lambda s: s] * i + [lambda s: jnp.where(col <= row, s, -1e30)]
        peak[rows], norm[rows], acc[rows] = attend_blocks(
            query[rows], [kv[0, p] for p in parts], [kv[1, p] for p in parts], adjust
        )


def row_own(place, near, far, gain, weight):
    return pl.pallas_call(
        row_own_kernel,
        out_shape=(
            jax.ShapeDtypeStruct((COLS, GROUP), jnp.bfloat16),
            *[jax.ShapeDtypeStruct((COLS, GROUP), jnp.float32)] * 3,
        ),
        in_specs=[SMEM, VMEM, VMEM, VMEM, VMEM],
        out_specs=(VMEM,) * 4,
        scratch_shapes=[
            pltpu.VMEM((2, COLS, GROUP), jnp.bfloat16),
        ],
        compiler_params=pltpu.CompilerParams(vmem_limit_bytes=16 * MIB),
        cost_estimate=pl.CostEstimate(flops=1, bytes_accessed=1, transcendentals=0),
        name="row_own",
    )(place, near, far, gain, weight)


def row_halo_kernel(place, near, far, gain, weight, query, peak, norm, acc, source, out, kv):
    order = [place[0], place[0] + 1, place[1], place[1] + 1]
    row, col = triangle(BLOCK)
    blocked = jnp.where(place[2] > 0, 0.0, -1e30).astype(jnp.float32)
    blocks = COLS // BLOCK
    for i in range(blocks):
        rows = slice(i * BLOCK, (i + 1) * BLOCK)
        pieces = [near[0, rows], near[1, rows], far[0, rows], far[1, rows]]
        normed = normed_pieces(pieces, [gain[n] for n in order])
        kv[0, rows] = project(normed, order, weight, 1)
        kv[1, rows] = project(normed, order, weight, 2)
    for i in range(blocks):
        rows = slice(i * BLOCK, (i + 1) * BLOCK)
        parts = [slice(j * BLOCK, (j + 1) * BLOCK) for j in range(i, blocks)]
        adjust = [lambda s: jnp.where(col > row, s, -1e30) + blocked] + [lambda s: s + blocked] * (blocks - 1 - i)
        peak2, norm2, acc2 = attend_blocks(
            query[rows], [kv[0, p] for p in parts], [kv[1, p] for p in parts], adjust
        )
        top = jnp.maximum(peak[rows], peak2)
        one, two = jnp.exp(peak[rows] - top), jnp.exp(peak2 - top)
        att = (acc[rows] * one + acc2 * two) / (norm[rows] * one + norm2 * two)
        out[rows, :GROUP] = att.astype(jnp.bfloat16)
        out[rows, GROUP:] = source[rows]


def row_halo(place, near, far, gain, weight, state, source):
    return pl.pallas_call(
        row_halo_kernel,
        out_shape=jax.ShapeDtypeStruct((COLS, 2 * GROUP), jnp.bfloat16),
        in_specs=[SMEM] + [VMEM] * 9,
        out_specs=VMEM,
        scratch_shapes=[
            pltpu.VMEM((2, COLS, GROUP), jnp.bfloat16),
        ],
        compiler_params=pltpu.CompilerParams(vmem_limit_bytes=16 * MIB),
        cost_estimate=pl.CostEstimate(flops=1, bytes_accessed=1, transcendentals=0),
        name="row_halo",
    )(place, near, far, gain, weight, *state, source)


QKV_AT, OUT_AT, WEIGHT_ROWS = 1024, 4096, 5120


def pack_kernel(row_out, col_qkv, col_out, packed, sem):
    pairs = [(col_qkv, packed.at[QKV_AT:OUT_AT])]
    for source, at in ((row_out, 0), (col_out, OUT_AT)):
        for n in range(PARTS):
            rows = slice(at + n * GROUP, at + (n + 1) * GROUP)
            pairs.append((source.at[:, n * GROUP : (n + 1) * GROUP], packed.at[rows]))
    copies = [pltpu.make_async_copy(a, b, sem.at[i]) for i, (a, b) in enumerate(pairs)]
    for copy in copies:
        copy.start()
    for copy in copies:
        copy.wait()


def pack_weights(row_out, col_qkv, col_out):
    return pl.pallas_call(
        pack_kernel,
        out_shape=jax.ShapeDtypeStruct((WEIGHT_ROWS, GROUP), jnp.bfloat16),
        in_specs=[ANY] * 3,
        out_specs=ANY,
        scratch_shapes=[pltpu.SemaphoreType.DMA((2 * PARTS + 1,))],
        compiler_params=pltpu.CompilerParams(vmem_limit_bytes=MIB),
        cost_estimate=pl.CostEstimate(flops=1, bytes_accessed=1, transcendentals=0),
        name="pack_weights",
    )(row_out, col_qkv, col_out)


def col_layer_kernel(place, moved, gain, w0, w1, w2, w3, out, held, sem):
    arrays = (w0, w1, w2, w3)
    groups = [place[0] + place[3], place[0] + 1 - place[3], place[1] + place[3], place[1] + 1 - place[3]]
    first = [pltpu.make_async_copy(w.at[:QKV_AT], held.at[i, :QKV_AT], sem.at[0, i]) for i, w in enumerate(arrays)]
    rest = [pltpu.make_async_copy(w.at[QKV_AT:], held.at[i, QKV_AT:], sem.at[1, i]) for i, w in enumerate(arrays)]
    for copy in first + rest:
        copy.start()

    def add_projected(pieces, atts, at):
        result = []
        for n in range(PARTS):
            rows = slice(at + n * GROUP, at + (n + 1) * GROUP)
            total = sum(dot(a, held[i, rows, :]) for i, a in enumerate(atts))
            result.append((pieces[n].astype(jnp.float32) + total).astype(jnp.bfloat16))
        return result

    atts = [moved[g, :, :GROUP] for g in groups]
    for copy in first:
        copy.wait()
    pieces = add_projected([moved[n, :, GROUP:] for n in range(PARTS)], atts, 0)
    normed = normed_pieces(pieces, [gain[n] for n in range(PARTS)])
    normed = jnp.concatenate(normed, axis=1)
    row, col = triangle(normed.shape[0])
    atts = []
    for i, copy in enumerate(rest):
        copy.wait()
        q, k, v = [
            dot(normed, held[i, QKV_AT + j * 1024 : QKV_AT + (j + 1) * 1024, :]).astype(jnp.bfloat16)
            for j in range(3)
        ]
        _, norm, acc = attend_blocks(
            q * jnp.bfloat16(SCALE), [k], [v], [lambda s: jnp.where(col <= row, s, -1e30)]
        )
        atts.append((acc / norm).astype(jnp.bfloat16))
    for n, piece in enumerate(add_projected(pieces, atts, OUT_AT)):
        out[n] = piece


def col_layer(place, moved, gain, weights):
    return pl.pallas_call(
        col_layer_kernel,
        out_shape=jax.ShapeDtypeStruct((PARTS, 128, GROUP), jnp.bfloat16),
        in_specs=[SMEM, VMEM, VMEM] + [ANY] * 4,
        out_specs=VMEM,
        scratch_shapes=[pltpu.VMEM((PARTS, WEIGHT_ROWS, GROUP), jnp.bfloat16), pltpu.SemaphoreType.DMA((2, PARTS))],
        compiler_params=pltpu.CompilerParams(vmem_limit_bytes=20 * MIB),
        cost_estimate=pl.CostEstimate(flops=1, bytes_accessed=1, transcendentals=0),
        name="col_layer",
    )(place, moved, gain, *weights)


SWAP = [(0, 1), (1, 0)]


def after(value, *others):
    return lax.optimization_barrier((value, *others))[0]


def cross_route(outer):
    route = []
    for yh in range(4):
        for core in range(2):
            a = yh * 4 + 2 + core
            b = ((yh + 1) % 4 if core in outer else yh) * 4 + core
            route += [(a, b), (b, a)]
    return route


def on_device(inputs, row_gain, row_qkv, row_out, col_gain, col_qkv, col_out):
    yl, core = lax.axis_index("yl"), lax.axis_index("c")
    place = jnp.stack([yl * 2, (1 - yl) * 2, lax.axis_index(SEQ), core]).astype(jnp.int32)
    row_gain = row_gain.reshape(PARTS, 1, GROUP)
    row_qkv = row_qkv.transpose(1, 0, 2).reshape(3, PARTS, GROUP, GROUP)
    row_qkv = row_qkv * jnp.array([SCALE, 1, 1], jnp.bfloat16)[:, None, None, None]

    other = lax.ppermute(inputs, "yl", SWAP)
    before = lax.ppermute(inputs, SEQ, [(i, i + 1) for i in range(127)])
    before_other = lax.ppermute(
        inputs, SEQ + ("yl",), [(2 * i + j, 2 * i + 3 - j) for i in range(127) for j in range(2)]
    )
    near = lax.all_gather(inputs, "c", axis=0)
    mine = pack_weights(row_out, col_qkv.transpose(1, 0, 2).reshape(3 * 1024, GROUP), col_out)
    mine, row_qkv, other = lax.optimization_barrier((mine, row_qkv, other, near))[:3]
    far = lax.all_gather(other, "c", axis=0)
    state = row_own(place, near, far, row_gain, row_qkv)
    mine = after(mine, before, before_other, state[0])
    theirs = lax.ppermute(mine, ("yh", "yl", "c"), cross_route((1,)))
    before_near = lax.all_gather(after(before, state[0]), "c", axis=0)
    before_far = lax.all_gather(after(before_other, before_near), "c", axis=0)
    sent = row_halo(place, before_near, before_far, row_gain, row_qkv, state, inputs)
    mine_swapped = lax.ppermute(after(mine, sent), "c", SWAP)

    moved = lax.all_to_all(sent.reshape(COLS, 4, 128), HEAD + SEQ, 0, 0, tiled=True)
    theirs_swapped = lax.ppermute(after(theirs, moved), "c", SWAP)
    mixed = col_layer(
        place,
        moved.reshape(PARTS, 128, 2 * GROUP),
        col_gain.reshape(PARTS, 1, GROUP),
        [mine, mine_swapped, theirs, theirs_swapped],
    )
    mixed = lax.all_to_all(mixed.reshape(COLS, 2, 128), HEAD + SEQ, 0, 0, tiled=True)
    return mixed.reshape(COLS, GROUP)


def solution(mesh):
    fine = Mesh(mesh.devices.reshape(4, 8, 4, 2, 2), SEQ + HEAD)
    return jax.shard_map(
        on_device,
        mesh=fine,
        in_specs=(
            P(SEQ, HEAD),
            P(),
            P(None, None, HEAD),
            P(HEAD, None),
            P(),
            P(None, None, HEAD),
            P(HEAD, None),
        ),
        out_specs=P(SEQ, HEAD),
        check_vma=False,
    )
```

```python
import functools

import jax
import jax.numpy as jnp
from jax import lax
from jax.experimental import pallas as pl
from jax.experimental.pallas import tpu as pltpu
from jax.sharding import Mesh, PartitionSpec as P

COLS = 512
HEAD_DIM = 64
SEQ = ("yh", "z", "x")
HEAD = ("yl", "c")
GROUP = 256
PARTS = 4
HEADS_HERE = GROUP // HEAD_DIM
MIB = 1 << 20
VMEM = pl.BlockSpec(memory_space=pltpu.VMEM)
SMEM = pl.BlockSpec(memory_space=pltpu.SMEM)
ANY = pl.BlockSpec(memory_space=pl.ANY)


def dot(a, b):
    return jnp.dot(a, b, preferred_element_type=jnp.float32)


def dot_t(a, b):
    return lax.dot_general(a, b, (((1,), (1,)), ((), ())), preferred_element_type=jnp.float32)


def normed_pieces(pieces, gains):
    flat = [p.astype(jnp.float32) for p in pieces]
    width = sum(p.shape[1] for p in pieces)
    mean = sum(jnp.sum(p, axis=-1, keepdims=True) for p in flat) / width
    flat = [p - mean for p in flat]
    var = sum(jnp.sum(p * p, axis=-1, keepdims=True) for p in flat) / width
    scale = lax.rsqrt(var + 1e-05)
    return [(p * scale * g).astype(jnp.bfloat16) for p, g in zip(flat, gains)]


def project(normed, order, weight, which):
    return sum(dot(p, weight[which, n]) for p, n in zip(normed, order)).astype(jnp.bfloat16)


def head_mask(rows, head):
    lane = lax.broadcasted_iota(jnp.int32, (rows, GROUP), 1)
    return (lane >= head * HEAD_DIM) & (lane < (head + 1) * HEAD_DIM)


def one_head(query, head):
    return jnp.where(head_mask(query.shape[0], head), query, jnp.bfloat16(0))


def triangle(block):
    row = lax.broadcasted_iota(jnp.int32, (block, block), 0)
    col = lax.broadcasted_iota(jnp.int32, (block, block), 1)
    return row, col


def attend_blocks(query, keys, vals, adjust):
    rows = query.shape[0]
    peak_all = norm_all = acc_all = jnp.zeros((rows, GROUP), jnp.float32)
    for head in range(HEADS_HERE):
        mask = head_mask(rows, head)
        qh = one_head(query, head)
        scores = [f(dot_t(qh, k)) for k, f in zip(keys, adjust)]
        peak = functools.reduce(jnp.maximum, scores)
        peak = jnp.max(peak, axis=-1, keepdims=True)
        expo = [jnp.exp(s - peak) for s in scores]
        norm = jnp.sum(sum(expo[1:], expo[0]), axis=-1, keepdims=True)
        acc = sum(dot(w.astype(jnp.bfloat16), v) for w, v in zip(expo, vals))
        peak_all = jnp.where(mask, peak, peak_all)
        norm_all = jnp.where(mask, norm, norm_all)
        acc_all = jnp.where(mask, acc, acc_all)
    return peak_all, norm_all, acc_all


BLOCK = 256
SCALE = HEAD_DIM ** (-0.5)


def row_own_kernel(place, near, far, gain, weight, query, peak, norm, acc, kv):
    order = [place[0], place[0] + 1, place[1], place[1] + 1]
    row, col = triangle(BLOCK)
    for i in range(COLS // BLOCK):
        rows = slice(i * BLOCK, (i + 1) * BLOCK)
        pieces = [near[0, rows], near[1, rows], far[0, rows], far[1, rows]]
        normed = normed_pieces(pieces, [gain[n] for n in order])
        query[rows] = project(normed, order, weight, 0)
        kv[0, rows] = project(normed, order, weight, 1)
        kv[1, rows] = project(normed, order, weight, 2)
    for i in range(COLS // BLOCK):
        rows = slice(i * BLOCK, (i + 1) * BLOCK)
        parts = [slice(j * BLOCK, (j + 1) * BLOCK) for j in range(i + 1)]
        adjust = [lambda s: s] * i + [lambda s: jnp.where(col <= row, s, -1e30)]
        peak[rows], norm[rows], acc[rows] = attend_blocks(
            query[rows], [kv[0, p] for p in parts], [kv[1, p] for p in parts], adjust
        )


def row_own(place, near, far, gain, weight):
    return pl.pallas_call(
        row_own_kernel,
        out_shape=(
            jax.ShapeDtypeStruct((COLS, GROUP), jnp.bfloat16),
            *[jax.ShapeDtypeStruct((COLS, GROUP), jnp.float32)] * 3,
        ),
        in_specs=[SMEM, VMEM, VMEM, VMEM, VMEM],
        out_specs=(VMEM,) * 4,
        scratch_shapes=[
            pltpu.VMEM((2, COLS, GROUP), jnp.bfloat16),
        ],
        compiler_params=pltpu.CompilerParams(vmem_limit_bytes=16 * MIB),
        cost_estimate=pl.CostEstimate(flops=1, bytes_accessed=1, transcendentals=0),
        name="row_own",
    )(place, near, far, gain, weight)


def row_halo_kernel(place, near, far, gain, weight, query, peak, norm, acc, source, out, kv):
    order = [place[0], place[0] + 1, place[1], place[1] + 1]
    row, col = triangle(BLOCK)
    blocked = jnp.where(place[2] > 0, 0.0, -1e30).astype(jnp.float32)
    blocks = COLS // BLOCK
    for i in range(blocks):
        rows = slice(i * BLOCK, (i + 1) * BLOCK)
        pieces = [near[0, rows], near[1, rows], far[0, rows], far[1, rows]]
        normed = normed_pieces(pieces, [gain[n] for n in order])
        kv[0, rows] = project(normed, order, weight, 1)
        kv[1, rows] = project(normed, order, weight, 2)
    for i in range(blocks):
        rows = slice(i * BLOCK, (i + 1) * BLOCK)
        parts = [slice(j * BLOCK, (j + 1) * BLOCK) for j in range(i, blocks)]
        adjust = [lambda s: jnp.where(col > row, s, -1e30) + blocked] + [lambda s: s + blocked] * (blocks - 1 - i)
        peak2, norm2, acc2 = attend_blocks(
            query[rows], [kv[0, p] for p in parts], [kv[1, p] for p in parts], adjust
        )
        top = jnp.maximum(peak[rows], peak2)
        one, two = jnp.exp(peak[rows] - top), jnp.exp(peak2 - top)
        att = (acc[rows] * one + acc2 * two) / (norm[rows] * one + norm2 * two)
        out[rows, :GROUP] = att.astype(jnp.bfloat16)
        out[rows, GROUP:] = source[rows]


def row_halo(place, near, far, gain, weight, state, source):
    return pl.pallas_call(
        row_halo_kernel,
        out_shape=jax.ShapeDtypeStruct((COLS, 2 * GROUP), jnp.bfloat16),
        in_specs=[SMEM] + [VMEM] * 9,
        out_specs=VMEM,
        scratch_shapes=[
            pltpu.VMEM((2, COLS, GROUP), jnp.bfloat16),
        ],
        compiler_params=pltpu.CompilerParams(vmem_limit_bytes=16 * MIB),
        cost_estimate=pl.CostEstimate(flops=1, bytes_accessed=1, transcendentals=0),
        name="row_halo",
    )(place, near, far, gain, weight, *state, source)


QKV_AT, OUT_AT, WEIGHT_ROWS = 1024, 4096, 5120


def pack_kernel(row_out, col_qkv, col_out, packed, sem):
    pairs = [(col_qkv, packed.at[QKV_AT:OUT_AT])]
    for source, at in ((row_out, 0), (col_out, OUT_AT)):
        for n in range(PARTS):
            rows = slice(at + n * GROUP, at + (n + 1) * GROUP)
            pairs.append((source.at[:, n * GROUP : (n + 1) * GROUP], packed.at[rows]))
    copies = [pltpu.make_async_copy(a, b, sem.at[i]) for i, (a, b) in enumerate(pairs)]
    for copy in copies:
        copy.start()
    for copy in copies:
        copy.wait()


def pack_weights(row_out, col_qkv, col_out):
    return pl.pallas_call(
        pack_kernel,
        out_shape=jax.ShapeDtypeStruct((WEIGHT_ROWS, GROUP), jnp.bfloat16),
        in_specs=[ANY] * 3,
        out_specs=ANY,
        scratch_shapes=[pltpu.SemaphoreType.DMA((2 * PARTS + 1,))],
        compiler_params=pltpu.CompilerParams(vmem_limit_bytes=MIB),
        cost_estimate=pl.CostEstimate(flops=1, bytes_accessed=1, transcendentals=0),
        name="pack_weights",
    )(row_out, col_qkv, col_out)


def col_layer_kernel(place, moved, gain, w0, w1, w2, w3, out, held, sem):
    arrays = (w0, w1, w2, w3)
    groups = [place[0] + place[3], place[0] + 1 - place[3], place[1] + place[3], place[1] + 1 - place[3]]
    first = [pltpu.make_async_copy(w.at[:QKV_AT], held.at[i, :QKV_AT], sem.at[0, i]) for i, w in enumerate(arrays)]
    rest = [pltpu.make_async_copy(w.at[QKV_AT:], held.at[i, QKV_AT:], sem.at[1, i]) for i, w in enumerate(arrays)]
    for copy in first + rest:
        copy.start()

    def add_projected(pieces, atts, at):
        result = []
        for n in range(PARTS):
            rows = slice(at + n * GROUP, at + (n + 1) * GROUP)
            total = sum(dot(a, held[i, rows, :]) for i, a in enumerate(atts))
            result.append((pieces[n].astype(jnp.float32) + total).astype(jnp.bfloat16))
        return result

    atts = [moved[g, :, :GROUP] for g in groups]
    for copy in first:
        copy.wait()
    pieces = add_projected([moved[n, :, GROUP:] for n in range(PARTS)], atts, 0)
    normed = normed_pieces(pieces, [gain[n] for n in range(PARTS)])
    normed = jnp.concatenate(normed, axis=1)
    row, col = triangle(normed.shape[0])
    atts = []
    for i, copy in enumerate(rest):
        copy.wait()
        q, k, v = [
            dot(normed, held[i, QKV_AT + j * 1024 : QKV_AT + (j + 1) * 1024, :]).astype(jnp.bfloat16)
            for j in range(3)
        ]
        _, norm, acc = attend_blocks(
            q * jnp.bfloat16(SCALE), [k], [v], [lambda s: jnp.where(col <= row, s, -1e30)]
        )
        atts.append((acc / norm).astype(jnp.bfloat16))
    for n, piece in enumerate(add_projected(pieces, atts, OUT_AT)):
        out[n] = piece


def col_layer(place, moved, gain, weights):
    return pl.pallas_call(
        col_layer_kernel,
        out_shape=jax.ShapeDtypeStruct((PARTS, 128, GROUP), jnp.bfloat16),
        in_specs=[SMEM, VMEM, VMEM] + [ANY] * 4,
        out_specs=VMEM,
        scratch_shapes=[pltpu.VMEM((PARTS, WEIGHT_ROWS, GROUP), jnp.bfloat16), pltpu.SemaphoreType.DMA((2, PARTS))],
        compiler_params=pltpu.CompilerParams(vmem_limit_bytes=20 * MIB),
        cost_estimate=pl.CostEstimate(flops=1, bytes_accessed=1, transcendentals=0),
        name="col_layer",
    )(place, moved, gain, *weights)


SWAP = [(0, 1), (1, 0)]


def after(value, *others):
    return lax.optimization_barrier((value, *others))[0]


def cross_route(outer):
    route = []
    for yh in range(4):
        for core in range(2):
            a = yh * 4 + 2 + core
            b = ((yh + 1) % 4 if core in outer else yh) * 4 + core
            route += [(a, b), (b, a)]
    return route


def on_device(inputs, row_gain, row_qkv, row_out, col_gain, col_qkv, col_out):
    yl, core = lax.axis_index("yl"), lax.axis_index("c")
    place = jnp.stack([yl * 2, (1 - yl) * 2, lax.axis_index(SEQ), core]).astype(jnp.int32)
    row_gain = row_gain.reshape(PARTS, 1, GROUP)
    row_qkv = row_qkv.transpose(1, 0, 2).reshape(3, PARTS, GROUP, GROUP)
    row_qkv = row_qkv * jnp.array([SCALE, 1, 1], jnp.bfloat16)[:, None, None, None]

    before = lax.ppermute(inputs, SEQ, [(i, i + 1) for i in range(127)])
    other = lax.ppermute(inputs, "yl", SWAP)
    near = lax.all_gather(inputs, "c", axis=0)
    mine = pack_weights(row_out, col_qkv.transpose(1, 0, 2).reshape(3 * 1024, GROUP), col_out)
    mine, row_qkv, before = lax.optimization_barrier((mine, row_qkv, before, near))[:3]
    before_other = lax.ppermute(before, "yl", SWAP)
    far = lax.all_gather(after(other, before), "c", axis=0)
    before_near = lax.all_gather(after(before, far), "c", axis=0)
    place = after(place, before_near)
    state = row_own(place, near, far, row_gain, row_qkv)
    before_far = lax.all_gather(after(before_other, state[0]), "c", axis=0)

    mine = after(mine, before_far)
    theirs = lax.ppermute(mine, ("yh", "yl", "c"), cross_route((1,)))
    sent = row_halo(place, before_near, before_far, row_gain, row_qkv, state, inputs)
    mine_swapped = lax.ppermute(after(mine, sent), "c", SWAP)

    moved = lax.all_to_all(sent.reshape(COLS, 4, 128), HEAD + SEQ, 0, 0, tiled=True)
    theirs_swapped = lax.ppermute(after(theirs, moved), "c", SWAP)
    mixed = col_layer(
        place,
        moved.reshape(PARTS, 128, 2 * GROUP),
        col_gain.reshape(PARTS, 1, GROUP),
        [mine, mine_swapped, theirs, theirs_swapped],
    )
    mixed = lax.all_to_all(mixed.reshape(COLS, 2, 128), HEAD + SEQ, 0, 0, tiled=True)
    return mixed.reshape(COLS, GROUP)


def solution(mesh):
    fine = Mesh(mesh.devices.reshape(4, 8, 4, 2, 2), SEQ + HEAD)
    return jax.shard_map(
        on_device,
        mesh=fine,
        in_specs=(
            P(SEQ, HEAD),
            P(),
            P(None, None, HEAD),
            P(HEAD, None),
            P(),
            P(None, None, HEAD),
            P(HEAD, None),
        ),
        out_specs=P(SEQ, HEAD),
        check_vma=False,
    )
```

```python
import functools

import jax
import jax.numpy as jnp
from jax import lax
from jax.experimental import pallas as pl
from jax.experimental.pallas import tpu as pltpu
from jax.sharding import Mesh, PartitionSpec as P

COLS = 512
HEAD_DIM = 64
SEQ = ("yh", "z", "x")
HEAD = ("yl", "c")
GROUP = 256
PARTS = 4
HEADS_HERE = GROUP // HEAD_DIM
MIB = 1 << 20
VMEM = pl.BlockSpec(memory_space=pltpu.VMEM)
SMEM = pl.BlockSpec(memory_space=pltpu.SMEM)
ANY = pl.BlockSpec(memory_space=pl.ANY)


def dot(a, b):
    return jnp.dot(a, b, preferred_element_type=jnp.float32)


def dot_t(a, b):
    return lax.dot_general(a, b, (((1,), (1,)), ((), ())), preferred_element_type=jnp.float32)


def normed_pieces(pieces, gains):
    flat = [p.astype(jnp.float32) for p in pieces]
    width = sum(p.shape[1] for p in pieces)
    mean = sum(jnp.sum(p, axis=-1, keepdims=True) for p in flat) / width
    flat = [p - mean for p in flat]
    var = sum(jnp.sum(p * p, axis=-1, keepdims=True) for p in flat) / width
    scale = lax.rsqrt(var + 1e-05)
    return [(p * scale * g).astype(jnp.bfloat16) for p, g in zip(flat, gains)]


def project(normed, order, weight, which):
    return sum(dot(p, weight[which, n]) for p, n in zip(normed, order)).astype(jnp.bfloat16)


def head_mask(rows, head):
    lane = lax.broadcasted_iota(jnp.int32, (rows, GROUP), 1)
    return (lane >= head * HEAD_DIM) & (lane < (head + 1) * HEAD_DIM)


def one_head(query, head):
    return jnp.where(head_mask(query.shape[0], head), query, jnp.bfloat16(0))


def triangle(block):
    row = lax.broadcasted_iota(jnp.int32, (block, block), 0)
    col = lax.broadcasted_iota(jnp.int32, (block, block), 1)
    return row, col


def attend_blocks(query, keys, vals, adjust):
    rows = query.shape[0]
    peak_all = norm_all = acc_all = jnp.zeros((rows, GROUP), jnp.float32)
    for head in range(HEADS_HERE):
        mask = head_mask(rows, head)
        qh = one_head(query, head)
        scores = [f(dot_t(qh, k)) for k, f in zip(keys, adjust)]
        peak = functools.reduce(jnp.maximum, scores)
        peak = jnp.max(peak, axis=-1, keepdims=True)
        expo = [jnp.exp(s - peak) for s in scores]
        norm = jnp.sum(sum(expo[1:], expo[0]), axis=-1, keepdims=True)
        acc = sum(dot(w.astype(jnp.bfloat16), v) for w, v in zip(expo, vals))
        peak_all = jnp.where(mask, peak, peak_all)
        norm_all = jnp.where(mask, norm, norm_all)
        acc_all = jnp.where(mask, acc, acc_all)
    return peak_all, norm_all, acc_all


BLOCK = 256
SCALE = HEAD_DIM ** (-0.5)


def row_own_kernel(place, near, far, gain, weight, query, peak, norm, acc, kv):
    order = [place[0], place[0] + 1, place[1], place[1] + 1]
    row, col = triangle(BLOCK)
    for i in range(COLS // BLOCK):
        rows = slice(i * BLOCK, (i + 1) * BLOCK)
        pieces = [near[0, rows], near[1, rows], far[0, rows], far[1, rows]]
        normed = normed_pieces(pieces, [gain[n] for n in order])
        query[rows] = project(normed, order, weight, 0)
        kv[0, rows] = project(normed, order, weight, 1)
        kv[1, rows] = project(normed, order, weight, 2)
    for i in range(COLS // BLOCK):
        rows = slice(i * BLOCK, (i + 1) * BLOCK)
        parts = [slice(j * BLOCK, (j + 1) * BLOCK) for j in range(i + 1)]
        adjust = [lambda s: s] * i + [lambda s: jnp.where(col <= row, s, -1e30)]
        peak[rows], norm[rows], acc[rows] = attend_blocks(
            query[rows], [kv[0, p] for p in parts], [kv[1, p] for p in parts], adjust
        )


def row_own(place, near, far, gain, weight):
    return pl.pallas_call(
        row_own_kernel,
        out_shape=(
            jax.ShapeDtypeStruct((COLS, GROUP), jnp.bfloat16),
            *[jax.ShapeDtypeStruct((COLS, GROUP), jnp.float32)] * 3,
        ),
        in_specs=[SMEM, VMEM, VMEM, VMEM, VMEM],
        out_specs=(VMEM,) * 4,
        scratch_shapes=[
            pltpu.VMEM((2, COLS, GROUP), jnp.bfloat16),
        ],
        compiler_params=pltpu.CompilerParams(vmem_limit_bytes=16 * MIB),
        cost_estimate=pl.CostEstimate(flops=1, bytes_accessed=1, transcendentals=0),
        name="row_own",
    )(place, near, far, gain, weight)


def row_halo_kernel(place, near, far, gain, weight, query, peak, norm, acc, source, out, kv):
    order = [place[0], place[0] + 1, place[1], place[1] + 1]
    row, col = triangle(BLOCK)
    blocked = jnp.where(place[2] > 0, 0.0, -1e30).astype(jnp.float32)
    blocks = COLS // BLOCK
    for i in range(blocks):
        rows = slice(i * BLOCK, (i + 1) * BLOCK)
        pieces = [near[0, rows], near[1, rows], far[0, rows], far[1, rows]]
        normed = normed_pieces(pieces, [gain[n] for n in order])
        kv[0, rows] = project(normed, order, weight, 1)
        kv[1, rows] = project(normed, order, weight, 2)
    for i in range(blocks):
        rows = slice(i * BLOCK, (i + 1) * BLOCK)
        parts = [slice(j * BLOCK, (j + 1) * BLOCK) for j in range(i, blocks)]
        adjust = [lambda s: jnp.where(col > row, s, -1e30) + blocked] + [lambda s: s + blocked] * (blocks - 1 - i)
        peak2, norm2, acc2 = attend_blocks(
            query[rows], [kv[0, p] for p in parts], [kv[1, p] for p in parts], adjust
        )
        top = jnp.maximum(peak[rows], peak2)
        one, two = jnp.exp(peak[rows] - top), jnp.exp(peak2 - top)
        att = (acc[rows] * one + acc2 * two) / (norm[rows] * one + norm2 * two)
        out[rows, :GROUP] = att.astype(jnp.bfloat16)
        out[rows, GROUP:] = source[rows]


def row_halo(place, near, far, gain, weight, state, source):
    return pl.pallas_call(
        row_halo_kernel,
        out_shape=jax.ShapeDtypeStruct((COLS, 2 * GROUP), jnp.bfloat16),
        in_specs=[SMEM] + [VMEM] * 9,
        out_specs=VMEM,
        scratch_shapes=[
            pltpu.VMEM((2, COLS, GROUP), jnp.bfloat16),
        ],
        compiler_params=pltpu.CompilerParams(vmem_limit_bytes=16 * MIB),
        cost_estimate=pl.CostEstimate(flops=1, bytes_accessed=1, transcendentals=0),
        name="row_halo",
    )(place, near, far, gain, weight, *state, source)


QKV_ROWS, OUT_ROWS = 3072, 1024


def pack_kernel(row_out, col_out, col_qkv, outs, everything, sem):
    copies = [(col_qkv, everything.at[2 * OUT_ROWS :])]
    for i, source in enumerate((row_out, col_out)):
        for n in range(PARTS):
            rows = slice(i * OUT_ROWS + n * GROUP, i * OUT_ROWS + (n + 1) * GROUP)
            part = source.at[:, n * GROUP : (n + 1) * GROUP]
            copies += [(part, outs.at[rows]), (part, everything.at[rows])]
    copies = [pltpu.make_async_copy(a, b, sem.at[i]) for i, (a, b) in enumerate(copies)]
    for copy in copies:
        copy.start()
    for copy in copies:
        copy.wait()


def pack_weights(row_out, col_out, col_qkv):
    return pl.pallas_call(
        pack_kernel,
        out_shape=(
            jax.ShapeDtypeStruct((2 * OUT_ROWS, GROUP), jnp.bfloat16),
            jax.ShapeDtypeStruct((2 * OUT_ROWS + QKV_ROWS, GROUP), jnp.bfloat16),
        ),
        in_specs=[ANY] * 3,
        out_specs=(ANY, ANY),
        scratch_shapes=[pltpu.SemaphoreType.DMA((4 * PARTS + 1,))],
        compiler_params=pltpu.CompilerParams(vmem_limit_bytes=MIB),
        cost_estimate=pl.CostEstimate(flops=1, bytes_accessed=1, transcendentals=0),
        name="pack_weights",
    )(row_out, col_out, col_qkv)


def col_layer_kernel(place, moved, gain, qkv0, out0, both1, qkv2, out2, qkv3, out3, out, qkv, outs, sem):
    pairs = [(a, outs.at[i]) for i, a in enumerate((out0, both1.at[: 2 * OUT_ROWS], out2, out3))]
    pairs += [(a, qkv.at[i]) for i, a in enumerate((qkv0, both1.at[2 * OUT_ROWS :], qkv2, qkv3))]
    copies = [pltpu.make_async_copy(a, b, sem.at[i]) for i, (a, b) in enumerate(pairs)]
    for copy in copies:
        copy.start()
    groups = [place[0] + place[3], place[0] + 1 - place[3], place[1] + place[3], place[1] + 1 - place[3]]

    def add_projected(pieces, atts, at):
        result = []
        for n in range(PARTS):
            rows = slice(at + n * GROUP, at + (n + 1) * GROUP)
            total = sum(dot(a, outs[i, rows, :]) for i, a in enumerate(atts))
            result.append((pieces[n].astype(jnp.float32) + total).astype(jnp.bfloat16))
        return result

    atts = [moved[g, :, :GROUP] for g in groups]
    for copy in copies[:PARTS]:
        copy.wait()
    pieces = add_projected([moved[n, :, GROUP:] for n in range(PARTS)], atts, 0)
    normed = normed_pieces(pieces, [gain[n] for n in range(PARTS)])
    normed = jnp.concatenate(normed, axis=1)
    row, col = triangle(normed.shape[0])
    atts = []
    for i, copy in enumerate(copies[PARTS:]):
        copy.wait()
        q, k, v = [dot(normed, qkv[i, j * 1024 : (j + 1) * 1024, :]).astype(jnp.bfloat16) for j in range(3)]
        _, norm, acc = attend_blocks(
            q * jnp.bfloat16(SCALE), [k], [v], [lambda s: jnp.where(col <= row, s, -1e30)]
        )
        atts.append((acc / norm).astype(jnp.bfloat16))
    for n, piece in enumerate(add_projected(pieces, atts, OUT_ROWS)):
        out[n] = piece


def col_layer(place, moved, gain, weights):
    return pl.pallas_call(
        col_layer_kernel,
        out_shape=jax.ShapeDtypeStruct((PARTS, 128, GROUP), jnp.bfloat16),
        in_specs=[SMEM, VMEM, VMEM] + [ANY] * 7,
        out_specs=VMEM,
        scratch_shapes=[
            pltpu.VMEM((PARTS, QKV_ROWS, GROUP), jnp.bfloat16),
            pltpu.VMEM((PARTS, 2 * OUT_ROWS, GROUP), jnp.bfloat16),
            pltpu.SemaphoreType.DMA((2 * PARTS,)),
        ],
        compiler_params=pltpu.CompilerParams(vmem_limit_bytes=20 * MIB),
        cost_estimate=pl.CostEstimate(flops=1, bytes_accessed=1, transcendentals=0),
        name="col_layer",
    )(place, moved, gain, *weights)


SWAP = [(0, 1), (1, 0)]


def after(value, *others):
    return lax.optimization_barrier((value, *others))[0]


def cross_route():
    route = []
    for yh in range(4):
        for core in range(2):
            a = yh * 4 + 2 + core
            b = ((yh + 1) % 4 if core == 1 else yh) * 4 + core
            route += [(a, b), (b, a)]
    return route


def on_device(inputs, row_gain, row_qkv, row_out, col_gain, col_qkv, col_out):
    yl, core = lax.axis_index("yl"), lax.axis_index("c")
    place = jnp.stack([yl * 2, (1 - yl) * 2, lax.axis_index(SEQ), core]).astype(jnp.int32)
    row_gain = row_gain.reshape(PARTS, 1, GROUP)
    row_qkv = row_qkv.transpose(1, 0, 2).reshape(3, PARTS, GROUP, GROUP)
    row_qkv = row_qkv * jnp.array([SCALE, 1, 1], jnp.bfloat16)[:, None, None, None]

    col_qkv = col_qkv.transpose(1, 0, 2).reshape(QKV_ROWS, GROUP)
    qkv_theirs = lax.ppermute(col_qkv, ("yh", "yl", "c"), cross_route())

    before = lax.ppermute(inputs, SEQ, [(i, i + 1) for i in range(127)])
    other = lax.ppermute(inputs, "yl", SWAP)
    near = lax.all_gather(inputs, "c", axis=0)
    outs, mine = pack_weights(row_out, col_out, col_qkv)
    outs, mine, row_qkv, before = lax.optimization_barrier((outs, mine, row_qkv, before, near))[:4]
    before_other = lax.ppermute(before, "yl", SWAP)
    far = lax.all_gather(after(other, before), "c", axis=0)
    before_near = lax.all_gather(after(before, far), "c", axis=0)
    place = after(place, before_near)
    state = row_own(place, near, far, row_gain, row_qkv)
    before_far = lax.all_gather(after(before_other, state[0]), "c", axis=0)

    outs_theirs = lax.ppermute(after(outs, before_far), ("yh", "yl", "c"), cross_route())
    sent = row_halo(place, before_near, before_far, row_gain, row_qkv, state, inputs)
    mine_swapped = lax.ppermute(after(mine, sent), "c", SWAP)
    qkv_swapped = lax.ppermute(after(qkv_theirs, sent), "c", SWAP)

    moved = lax.all_to_all(sent.reshape(COLS, 4, 128), HEAD + SEQ, 0, 0, tiled=True)
    outs_swapped = lax.ppermute(after(outs_theirs, moved), "c", SWAP)
    mixed = col_layer(
        place,
        moved.reshape(PARTS, 128, 2 * GROUP),
        col_gain.reshape(PARTS, 1, GROUP),
        [col_qkv, outs, mine_swapped, qkv_theirs, outs_theirs, qkv_swapped, outs_swapped],
    )
    mixed = lax.all_to_all(mixed.reshape(COLS, 2, 128), HEAD + SEQ, 0, 0, tiled=True)
    return mixed.reshape(COLS, GROUP)


def solution(mesh):
    fine = Mesh(mesh.devices.reshape(4, 8, 4, 2, 2), SEQ + HEAD)
    return jax.shard_map(
        on_device,
        mesh=fine,
        in_specs=(
            P(SEQ, HEAD),
            P(),
            P(None, None, HEAD),
            P(HEAD, None),
            P(),
            P(None, None, HEAD),
            P(HEAD, None),
        ),
        out_specs=P(SEQ, HEAD),
        check_vma=False,
    )
```

```python
import functools

import jax
import jax.numpy as jnp
from jax import lax
from jax.experimental import pallas as pl
from jax.experimental.pallas import tpu as pltpu
from jax.sharding import Mesh, PartitionSpec as P

COLS = 512
HEAD_DIM = 64
SEQ = ("yh", "z", "x")
HEAD = ("yl", "c")
GROUP = 256
PARTS = 4
HEADS_HERE = GROUP // HEAD_DIM
MIB = 1 << 20
VMEM = pl.BlockSpec(memory_space=pltpu.VMEM)
SMEM = pl.BlockSpec(memory_space=pltpu.SMEM)
ANY = pl.BlockSpec(memory_space=pl.ANY)


def dot(a, b):
    return jnp.dot(a, b, preferred_element_type=jnp.float32)


def dot_t(a, b):
    return lax.dot_general(a, b, (((1,), (1,)), ((), ())), preferred_element_type=jnp.float32)


def normed_pieces(pieces, gains):
    flat = [p.astype(jnp.float32) for p in pieces]
    width = sum(p.shape[1] for p in pieces)
    mean = sum(jnp.sum(p, axis=-1, keepdims=True) for p in flat) / width
    flat = [p - mean for p in flat]
    var = sum(jnp.sum(p * p, axis=-1, keepdims=True) for p in flat) / width
    scale = lax.rsqrt(var + 1e-05)
    return [(p * scale * g).astype(jnp.bfloat16) for p, g in zip(flat, gains)]


def project(normed, order, weight, which):
    return sum(dot(p, weight[which, n]) for p, n in zip(normed, order)).astype(jnp.bfloat16)


def head_mask(rows, head):
    lane = lax.broadcasted_iota(jnp.int32, (rows, GROUP), 1)
    return (lane >= head * HEAD_DIM) & (lane < (head + 1) * HEAD_DIM)


def one_head(query, head):
    return jnp.where(head_mask(query.shape[0], head), query, jnp.bfloat16(0))


def triangle(block):
    row = lax.broadcasted_iota(jnp.int32, (block, block), 0)
    col = lax.broadcasted_iota(jnp.int32, (block, block), 1)
    return row, col


def attend_blocks(query, keys, vals, adjust):
    rows = query.shape[0]
    peak_all = norm_all = acc_all = jnp.zeros((rows, GROUP), jnp.float32)
    for head in range(HEADS_HERE):
        mask = head_mask(rows, head)
        qh = one_head(query, head)
        scores = [f(dot_t(qh, k)) for k, f in zip(keys, adjust)]
        peak = functools.reduce(jnp.maximum, scores)
        peak = jnp.max(peak, axis=-1, keepdims=True)
        expo = [jnp.exp(s - peak) for s in scores]
        norm = jnp.sum(sum(expo[1:], expo[0]), axis=-1, keepdims=True)
        acc = sum(dot(w.astype(jnp.bfloat16), v) for w, v in zip(expo, vals))
        peak_all = jnp.where(mask, peak, peak_all)
        norm_all = jnp.where(mask, norm, norm_all)
        acc_all = jnp.where(mask, acc, acc_all)
    return peak_all, norm_all, acc_all


BLOCK = 256
SCALE = HEAD_DIM ** (-0.5)


def row_own_kernel(place, near, far, gain, weight, query, peak, norm, acc, kv):
    order = [place[0], place[0] + 1, place[1], place[1] + 1]
    row, col = triangle(BLOCK)
    for i in range(COLS // BLOCK):
        rows = slice(i * BLOCK, (i + 1) * BLOCK)
        pieces = [near[0, rows], near[1, rows], far[0, rows], far[1, rows]]
        normed = normed_pieces(pieces, [gain[n] for n in order])
        query[rows] = project(normed, order, weight, 0)
        kv[0, rows] = project(normed, order, weight, 1)
        kv[1, rows] = project(normed, order, weight, 2)
    for i in range(COLS // BLOCK):
        rows = slice(i * BLOCK, (i + 1) * BLOCK)
        parts = [slice(j * BLOCK, (j + 1) * BLOCK) for j in range(i + 1)]
        adjust = [lambda s: s] * i + [lambda s: jnp.where(col <= row, s, -1e30)]
        peak[rows], norm[rows], acc[rows] = attend_blocks(
            query[rows], [kv[0, p] for p in parts], [kv[1, p] for p in parts], adjust
        )


def row_own(place, near, far, gain, weight):
    return pl.pallas_call(
        row_own_kernel,
        out_shape=(
            jax.ShapeDtypeStruct((COLS, GROUP), jnp.bfloat16),
            *[jax.ShapeDtypeStruct((COLS, GROUP), jnp.float32)] * 3,
        ),
        in_specs=[SMEM, VMEM, VMEM, VMEM, VMEM],
        out_specs=(VMEM,) * 4,
        scratch_shapes=[
            pltpu.VMEM((2, COLS, GROUP), jnp.bfloat16),
        ],
        compiler_params=pltpu.CompilerParams(vmem_limit_bytes=16 * MIB),
        cost_estimate=pl.CostEstimate(flops=1, bytes_accessed=1, transcendentals=0),
        name="row_own",
    )(place, near, far, gain, weight)


def row_halo_kernel(place, near, far, gain, weight, query, peak, norm, acc, source, out, kv):
    order = [place[0], place[0] + 1, place[1], place[1] + 1]
    row, col = triangle(BLOCK)
    blocked = jnp.where(place[2] > 0, 0.0, -1e30).astype(jnp.float32)
    blocks = COLS // BLOCK
    for i in range(blocks):
        rows = slice(i * BLOCK, (i + 1) * BLOCK)
        pieces = [near[0, rows], near[1, rows], far[0, rows], far[1, rows]]
        normed = normed_pieces(pieces, [gain[n] for n in order])
        kv[0, rows] = project(normed, order, weight, 1)
        kv[1, rows] = project(normed, order, weight, 2)
    for i in range(blocks):
        rows = slice(i * BLOCK, (i + 1) * BLOCK)
        parts = [slice(j * BLOCK, (j + 1) * BLOCK) for j in range(i, blocks)]
        adjust = [lambda s: jnp.where(col > row, s, -1e30) + blocked] + [lambda s: s + blocked] * (blocks - 1 - i)
        peak2, norm2, acc2 = attend_blocks(
            query[rows], [kv[0, p] for p in parts], [kv[1, p] for p in parts], adjust
        )
        top = jnp.maximum(peak[rows], peak2)
        one, two = jnp.exp(peak[rows] - top), jnp.exp(peak2 - top)
        att = (acc[rows] * one + acc2 * two) / (norm[rows] * one + norm2 * two)
        out[rows, :GROUP] = att.astype(jnp.bfloat16)
        out[rows, GROUP:] = source[rows]


def row_halo(place, near, far, gain, weight, state, source):
    return pl.pallas_call(
        row_halo_kernel,
        out_shape=jax.ShapeDtypeStruct((COLS, 2 * GROUP), jnp.bfloat16),
        in_specs=[SMEM] + [VMEM] * 9,
        out_specs=VMEM,
        scratch_shapes=[
            pltpu.VMEM((2, COLS, GROUP), jnp.bfloat16),
        ],
        compiler_params=pltpu.CompilerParams(vmem_limit_bytes=16 * MIB),
        cost_estimate=pl.CostEstimate(flops=1, bytes_accessed=1, transcendentals=0),
        name="row_halo",
    )(place, near, far, gain, weight, *state, source)


QKV_AT, OUT_AT, WEIGHT_ROWS = 1024, 4096, 5120


def pack_kernel(row_out, col_qkv, col_out, packed, sem):
    pairs = [(col_qkv, packed.at[QKV_AT:OUT_AT])]
    for source, at in ((row_out, 0), (col_out, OUT_AT)):
        for n in range(PARTS):
            rows = slice(at + n * GROUP, at + (n + 1) * GROUP)
            pairs.append((source.at[:, n * GROUP : (n + 1) * GROUP], packed.at[rows]))
    copies = [pltpu.make_async_copy(a, b, sem.at[i]) for i, (a, b) in enumerate(pairs)]
    for copy in copies:
        copy.start()
    for copy in copies:
        copy.wait()


def pack_weights(row_out, col_qkv, col_out):
    return pl.pallas_call(
        pack_kernel,
        out_shape=jax.ShapeDtypeStruct((WEIGHT_ROWS, GROUP), jnp.bfloat16),
        in_specs=[ANY] * 3,
        out_specs=ANY,
        scratch_shapes=[pltpu.SemaphoreType.DMA((2 * PARTS + 1,))],
        compiler_params=pltpu.CompilerParams(vmem_limit_bytes=MIB),
        cost_estimate=pl.CostEstimate(flops=1, bytes_accessed=1, transcendentals=0),
        name="pack_weights",
    )(row_out, col_qkv, col_out)


def col_layer_kernel(place, moved, gain, w0, w1, w2, w3, out, held, sem):
    arrays = (w0, w1, w2, w3)
    groups = [place[0] + place[3], place[0] + 1 - place[3], place[1] + place[3], place[1] + 1 - place[3]]
    first = [pltpu.make_async_copy(w.at[:QKV_AT], held.at[i, :QKV_AT], sem.at[0, i]) for i, w in enumerate(arrays)]
    rest = [pltpu.make_async_copy(w.at[QKV_AT:], held.at[i, QKV_AT:], sem.at[1, i]) for i, w in enumerate(arrays)]
    for copy in first + rest:
        copy.start()

    def add_projected(pieces, atts, at):
        result = []
        for n in range(PARTS):
            rows = slice(at + n * GROUP, at + (n + 1) * GROUP)
            total = sum(dot(a, held[i, rows, :]) for i, a in enumerate(atts))
            result.append((pieces[n].astype(jnp.float32) + total).astype(jnp.bfloat16))
        return result

    atts = [moved[g, :, :GROUP] for g in groups]
    for copy in first:
        copy.wait()
    pieces = add_projected([moved[n, :, GROUP:] for n in range(PARTS)], atts, 0)
    normed = normed_pieces(pieces, [gain[n] for n in range(PARTS)])
    normed = jnp.concatenate(normed, axis=1)
    row, col = triangle(normed.shape[0])
    atts = []
    for i, copy in enumerate(rest):
        copy.wait()
        q, k, v = [
            dot(normed, held[i, QKV_AT + j * 1024 : QKV_AT + (j + 1) * 1024, :]).astype(jnp.bfloat16)
            for j in range(3)
        ]
        _, norm, acc = attend_blocks(
            q * jnp.bfloat16(SCALE), [k], [v], [lambda s: jnp.where(col <= row, s, -1e30)]
        )
        atts.append((acc / norm).astype(jnp.bfloat16))
    for n, piece in enumerate(add_projected(pieces, atts, OUT_AT)):
        out[n] = piece


def col_layer(place, moved, gain, weights):
    return pl.pallas_call(
        col_layer_kernel,
        out_shape=jax.ShapeDtypeStruct((PARTS, 128, GROUP), jnp.bfloat16),
        in_specs=[SMEM, VMEM, VMEM] + [ANY] * 4,
        out_specs=VMEM,
        scratch_shapes=[pltpu.VMEM((PARTS, WEIGHT_ROWS, GROUP), jnp.bfloat16), pltpu.SemaphoreType.DMA((2, PARTS))],
        compiler_params=pltpu.CompilerParams(vmem_limit_bytes=20 * MIB),
        cost_estimate=pl.CostEstimate(flops=1, bytes_accessed=1, transcendentals=0),
        name="col_layer",
    )(place, moved, gain, *weights)


SWAP = [(0, 1), (1, 0)]


def after(value, *others):
    return lax.optimization_barrier((value, *others))[0]


def cross_route(outer):
    route = []
    for yh in range(4):
        for core in range(2):
            a = yh * 4 + 2 + core
            b = ((yh + 1) % 4 if core in outer else yh) * 4 + core
            route += [(a, b), (b, a)]
    return route


def on_device(inputs, row_gain, row_qkv, row_out, col_gain, col_qkv, col_out):
    yl, core = lax.axis_index("yl"), lax.axis_index("c")
    place = jnp.stack([yl * 2, (1 - yl) * 2, lax.axis_index(SEQ), core]).astype(jnp.int32)
    row_gain = row_gain.reshape(PARTS, 1, GROUP)
    row_qkv = row_qkv.transpose(1, 0, 2).reshape(3, PARTS, GROUP, GROUP)
    row_qkv = row_qkv * jnp.array([SCALE, 1, 1], jnp.bfloat16)[:, None, None, None]

    before = lax.ppermute(inputs, SEQ, [(i, i + 1) for i in range(127)])
    other = lax.ppermute(inputs, "yl", SWAP)
    near = lax.all_gather(inputs, "c", axis=0)
    mine = pack_weights(row_out, col_qkv.transpose(1, 0, 2).reshape(3 * 1024, GROUP), col_out)
    mine, row_qkv, other = lax.optimization_barrier((mine, row_qkv, other, near))[:3]
    far = lax.all_gather(other, "c", axis=0)
    state = row_own(place, near, far, row_gain, row_qkv)
    before = after(before, state[0])
    before_other = lax.ppermute(before, "yl", SWAP)
    before_near = lax.all_gather(before, "c", axis=0)
    before_far = lax.all_gather(after(before_other, before_near), "c", axis=0)

    mine = after(mine, before_far)
    theirs = lax.ppermute(mine, ("yh", "yl", "c"), cross_route((1,)))
    sent = row_halo(place, before_near, before_far, row_gain, row_qkv, state, inputs)
    mine_swapped = lax.ppermute(after(mine, sent), "c", SWAP)

    moved = lax.all_to_all(sent.reshape(COLS, 4, 128), HEAD + SEQ, 0, 0, tiled=True)
    theirs_swapped = lax.ppermute(after(theirs, moved), "c", SWAP)
    mixed = col_layer(
        place,
        moved.reshape(PARTS, 128, 2 * GROUP),
        col_gain.reshape(PARTS, 1, GROUP),
        [mine, mine_swapped, theirs, theirs_swapped],
    )
    mixed = lax.all_to_all(mixed.reshape(COLS, 2, 128), HEAD + SEQ, 0, 0, tiled=True)
    return mixed.reshape(COLS, GROUP)


def solution(mesh):
    fine = Mesh(mesh.devices.reshape(4, 8, 4, 2, 2), SEQ + HEAD)
    return jax.shard_map(
        on_device,
        mesh=fine,
        in_specs=(
            P(SEQ, HEAD),
            P(),
            P(None, None, HEAD),
            P(HEAD, None),
            P(),
            P(None, None, HEAD),
            P(HEAD, None),
        ),
        out_specs=P(SEQ, HEAD),
        check_vma=False,
    )
```

```python
import functools

import jax
import jax.numpy as jnp
from jax import lax
from jax.experimental import pallas as pl
from jax.experimental.pallas import tpu as pltpu
from jax.sharding import Mesh, PartitionSpec as P

COLS = 512
HEAD_DIM = 64
SEQ = ("yh", "z", "x")
HEAD = ("yl", "c")
GROUP = 256
PARTS = 4
HEADS_HERE = GROUP // HEAD_DIM
MIB = 1 << 20
VMEM = pl.BlockSpec(memory_space=pltpu.VMEM)
SMEM = pl.BlockSpec(memory_space=pltpu.SMEM)
ANY = pl.BlockSpec(memory_space=pl.ANY)


def dot(a, b):
    return jnp.dot(a, b, preferred_element_type=jnp.float32)


def dot_t(a, b):
    return lax.dot_general(a, b, (((1,), (1,)), ((), ())), preferred_element_type=jnp.float32)


def normed_pieces(pieces, gains):
    flat = [p.astype(jnp.float32) for p in pieces]
    width = sum(p.shape[1] for p in pieces)
    mean = sum(jnp.sum(p, axis=-1, keepdims=True) for p in flat) / width
    flat = [p - mean for p in flat]
    var = sum(jnp.sum(p * p, axis=-1, keepdims=True) for p in flat) / width
    scale = lax.rsqrt(var + 1e-05)
    return [(p * scale * g).astype(jnp.bfloat16) for p, g in zip(flat, gains)]


def project(normed, order, weight, which):
    return sum(dot(p, weight[which, n]) for p, n in zip(normed, order)).astype(jnp.bfloat16)


def head_mask(rows, head):
    lane = lax.broadcasted_iota(jnp.int32, (rows, GROUP), 1)
    return (lane >= head * HEAD_DIM) & (lane < (head + 1) * HEAD_DIM)


def one_head(query, head):
    return jnp.where(head_mask(query.shape[0], head), query, jnp.bfloat16(0))


def triangle(block):
    row = lax.broadcasted_iota(jnp.int32, (block, block), 0)
    col = lax.broadcasted_iota(jnp.int32, (block, block), 1)
    return row, col


def attend_blocks(query, keys, vals, adjust):
    rows = query.shape[0]
    peak_all = norm_all = acc_all = jnp.zeros((rows, GROUP), jnp.float32)
    for head in range(HEADS_HERE):
        mask = head_mask(rows, head)
        qh = one_head(query, head)
        scores = [f(dot_t(qh, k)) for k, f in zip(keys, adjust)]
        peak = functools.reduce(jnp.maximum, scores)
        peak = jnp.max(peak, axis=-1, keepdims=True)
        expo = [jnp.exp(s - peak) for s in scores]
        norm = jnp.sum(sum(expo[1:], expo[0]), axis=-1, keepdims=True)
        acc = sum(dot(w.astype(jnp.bfloat16), v) for w, v in zip(expo, vals))
        peak_all = jnp.where(mask, peak, peak_all)
        norm_all = jnp.where(mask, norm, norm_all)
        acc_all = jnp.where(mask, acc, acc_all)
    return peak_all, norm_all, acc_all


BLOCK = 256
SCALE = HEAD_DIM ** (-0.5)


def row_own_kernel(place, near, far, gain, weight, query, peak, norm, acc, kv):
    order = [place[0], place[0] + 1, place[1], place[1] + 1]
    row, col = triangle(BLOCK)
    for i in range(COLS // BLOCK):
        rows = slice(i * BLOCK, (i + 1) * BLOCK)
        pieces = [near[0, rows], near[1, rows], far[0, rows], far[1, rows]]
        normed = normed_pieces(pieces, [gain[n] for n in order])
        query[rows] = project(normed, order, weight, 0)
        kv[0, rows] = project(normed, order, weight, 1)
        kv[1, rows] = project(normed, order, weight, 2)
    for i in range(COLS // BLOCK):
        rows = slice(i * BLOCK, (i + 1) * BLOCK)
        parts = [slice(j * BLOCK, (j + 1) * BLOCK) for j in range(i + 1)]
        adjust = [lambda s: s] * i + [lambda s: jnp.where(col <= row, s, -1e30)]
        peak[rows], norm[rows], acc[rows] = attend_blocks(
            query[rows], [kv[0, p] for p in parts], [kv[1, p] for p in parts], adjust
        )


def row_own(place, near, far, gain, weight):
    return pl.pallas_call(
        row_own_kernel,
        out_shape=(
            jax.ShapeDtypeStruct((COLS, GROUP), jnp.bfloat16),
            *[jax.ShapeDtypeStruct((COLS, GROUP), jnp.float32)] * 3,
        ),
        in_specs=[SMEM, VMEM, VMEM, VMEM, VMEM],
        out_specs=(VMEM,) * 4,
        scratch_shapes=[
            pltpu.VMEM((2, COLS, GROUP), jnp.bfloat16),
        ],
        compiler_params=pltpu.CompilerParams(vmem_limit_bytes=16 * MIB),
        cost_estimate=pl.CostEstimate(flops=1, bytes_accessed=1, transcendentals=0),
        name="row_own",
    )(place, near, far, gain, weight)


def row_halo_kernel(place, near, far, gain, weight, query, peak, norm, acc, source, out, kv):
    order = [place[0], place[0] + 1, place[1], place[1] + 1]
    row, col = triangle(BLOCK)
    blocked = jnp.where(place[2] > 0, 0.0, -1e30).astype(jnp.float32)
    blocks = COLS // BLOCK
    for i in range(blocks):
        rows = slice(i * BLOCK, (i + 1) * BLOCK)
        pieces = [near[0, rows], near[1, rows], far[0, rows], far[1, rows]]
        normed = normed_pieces(pieces, [gain[n] for n in order])
        kv[0, rows] = project(normed, order, weight, 1)
        kv[1, rows] = project(normed, order, weight, 2)
    for i in range(blocks):
        rows = slice(i * BLOCK, (i + 1) * BLOCK)
        parts = [slice(j * BLOCK, (j + 1) * BLOCK) for j in range(i, blocks)]
        adjust = [lambda s: jnp.where(col > row, s, -1e30) + blocked] + [lambda s: s + blocked] * (blocks - 1 - i)
        peak2, norm2, acc2 = attend_blocks(
            query[rows], [kv[0, p] for p in parts], [kv[1, p] for p in parts], adjust
        )
        top = jnp.maximum(peak[rows], peak2)
        one, two = jnp.exp(peak[rows] - top), jnp.exp(peak2 - top)
        att = (acc[rows] * one + acc2 * two) / (norm[rows] * one + norm2 * two)
        out[rows, :GROUP] = att.astype(jnp.bfloat16)
        out[rows, GROUP:] = source[rows]


def row_halo(place, near, far, gain, weight, state, source):
    return pl.pallas_call(
        row_halo_kernel,
        out_shape=jax.ShapeDtypeStruct((COLS, 2 * GROUP), jnp.bfloat16),
        in_specs=[SMEM] + [VMEM] * 9,
        out_specs=VMEM,
        scratch_shapes=[
            pltpu.VMEM((2, COLS, GROUP), jnp.bfloat16),
        ],
        compiler_params=pltpu.CompilerParams(vmem_limit_bytes=16 * MIB),
        cost_estimate=pl.CostEstimate(flops=1, bytes_accessed=1, transcendentals=0),
        name="row_halo",
    )(place, near, far, gain, weight, *state, source)


QKV_AT, OUT_AT, WEIGHT_ROWS = 1024, 4096, 5120
LONG = 2*10**10


def pack_kernel(row_out, col_qkv, col_out, packed, sem):
    pairs = [(col_qkv, packed.at[QKV_AT:OUT_AT])]
    for source, at in ((row_out, 0), (col_out, OUT_AT)):
        for n in range(PARTS):
            rows = slice(at + n * GROUP, at + (n + 1) * GROUP)
            pairs.append((source.at[:, n * GROUP : (n + 1) * GROUP], packed.at[rows]))
    copies = [pltpu.make_async_copy(a, b, sem.at[i]) for i, (a, b) in enumerate(pairs)]
    for copy in copies:
        copy.start()
    for copy in copies:
        copy.wait()


def pack_weights(row_out, col_qkv, col_out):
    return pl.pallas_call(
        pack_kernel,
        out_shape=jax.ShapeDtypeStruct((WEIGHT_ROWS, GROUP), jnp.bfloat16),
        in_specs=[ANY] * 3,
        out_specs=ANY,
        scratch_shapes=[pltpu.SemaphoreType.DMA((2 * PARTS + 1,))],
        compiler_params=pltpu.CompilerParams(vmem_limit_bytes=MIB),
        cost_estimate=pl.CostEstimate(flops=1, bytes_accessed=1, transcendentals=0),
        name="pack_weights",
    )(row_out, col_qkv, col_out)


def weight_groups(place):
    return [place[0] + place[3], place[0] + 1 - place[3], place[1] + place[3], place[1] + 1 - place[3]]


def row_output_kernel(place, moved, w0, w1, w2, out, held, sem):
    copies = [
        pltpu.make_async_copy(w.at[:QKV_AT], held.at[i], sem.at[i]) for i, w in enumerate((w0, w1, w2))
    ]
    for copy in copies:
        copy.start()
    atts = [moved[g, :, :GROUP] for g in weight_groups(place)[:3]]
    for copy in copies:
        copy.wait()
    for n in range(PARTS):
        total = sum(dot(a, held[i, n * GROUP : (n + 1) * GROUP, :]) for i, a in enumerate(atts))
        out[n] = moved[n, :, GROUP:].astype(jnp.float32) + total


def row_output(place, moved, weights):
    return pl.pallas_call(
        row_output_kernel,
        out_shape=jax.ShapeDtypeStruct((PARTS, 128, GROUP), jnp.float32),
        in_specs=[SMEM, VMEM] + [ANY] * 3,
        out_specs=VMEM,
        scratch_shapes=[pltpu.VMEM((3, QKV_AT, GROUP), jnp.bfloat16), pltpu.SemaphoreType.DMA((3,))],
        compiler_params=pltpu.CompilerParams(vmem_limit_bytes=8 * MIB),
        cost_estimate=pl.CostEstimate(flops=LONG, bytes_accessed=1, transcendentals=0),
        name="row_output",
    )(place, moved, *weights)


def col_layer_kernel(place, moved, partial, gain, w0, w1, w2, w3, out, held, last, sem):
    arrays = (w0, w1, w2, w3)
    first = pltpu.make_async_copy(w3.at[:QKV_AT], last, sem.at[PARTS])
    rest = [pltpu.make_async_copy(w.at[QKV_AT:], held.at[i], sem.at[i]) for i, w in enumerate(arrays)]
    for copy in [first] + rest:
        copy.start()
    att = moved[weight_groups(place)[3], :, :GROUP]
    first.wait()
    pieces = [
        (partial[n] + dot(att, last[n * GROUP : (n + 1) * GROUP, :])).astype(jnp.bfloat16) for n in range(PARTS)
    ]
    normed = normed_pieces(pieces, [gain[n] for n in range(PARTS)])
    normed = jnp.concatenate(normed, axis=1)
    row, col = triangle(normed.shape[0])
    atts = []
    for i, copy in enumerate(rest):
        copy.wait()
        q, k, v = [dot(normed, held[i, j * 1024 : (j + 1) * 1024, :]).astype(jnp.bfloat16) for j in range(3)]
        _, norm, acc = attend_blocks(
            q * jnp.bfloat16(SCALE), [k], [v], [lambda s: jnp.where(col <= row, s, -1e30)]
        )
        atts.append((acc / norm).astype(jnp.bfloat16))
    for n in range(PARTS):
        rows = slice(OUT_AT - QKV_AT + n * GROUP, OUT_AT - QKV_AT + (n + 1) * GROUP)
        total = sum(dot(a, held[i, rows, :]) for i, a in enumerate(atts))
        out[n] = (pieces[n].astype(jnp.float32) + total).astype(jnp.bfloat16)


def col_layer(place, moved, partial, gain, weights):
    return pl.pallas_call(
        col_layer_kernel,
        out_shape=jax.ShapeDtypeStruct((PARTS, 128, GROUP), jnp.bfloat16),
        in_specs=[SMEM, VMEM, VMEM, VMEM] + [ANY] * 4,
        out_specs=VMEM,
        scratch_shapes=[
            pltpu.VMEM((PARTS, WEIGHT_ROWS - QKV_AT, GROUP), jnp.bfloat16),
            pltpu.VMEM((QKV_AT, GROUP), jnp.bfloat16),
            pltpu.SemaphoreType.DMA((PARTS + 1,)),
        ],
        compiler_params=pltpu.CompilerParams(vmem_limit_bytes=20 * MIB),
        cost_estimate=pl.CostEstimate(flops=1, bytes_accessed=1, transcendentals=0),
        name="col_layer",
    )(place, moved, partial, gain, *weights)


SWAP = [(0, 1), (1, 0)]


def after(value, *others):
    return lax.optimization_barrier((value, *others))[0]


def cross_route(outer):
    route = []
    for yh in range(4):
        for core in range(2):
            a = yh * 4 + 2 + core
            b = ((yh + 1) % 4 if core in outer else yh) * 4 + core
            route += [(a, b), (b, a)]
    return route


def on_device(inputs, row_gain, row_qkv, row_out, col_gain, col_qkv, col_out):
    yl, core = lax.axis_index("yl"), lax.axis_index("c")
    place = jnp.stack([yl * 2, (1 - yl) * 2, lax.axis_index(SEQ), core]).astype(jnp.int32)
    row_gain = row_gain.reshape(PARTS, 1, GROUP)
    row_qkv = row_qkv.transpose(1, 0, 2).reshape(3, PARTS, GROUP, GROUP)
    row_qkv = row_qkv * jnp.array([SCALE, 1, 1], jnp.bfloat16)[:, None, None, None]

    before = lax.ppermute(inputs, SEQ, [(i, i + 1) for i in range(127)])
    other = lax.ppermute(inputs, "yl", SWAP)
    near = lax.all_gather(inputs, "c", axis=0)
    mine = pack_weights(row_out, col_qkv.transpose(1, 0, 2).reshape(3 * 1024, GROUP), col_out)
    mine, row_qkv, before = lax.optimization_barrier((mine, row_qkv, before, near))[:3]
    before_other = lax.ppermute(before, "yl", SWAP)
    far = lax.all_gather(after(other, before), "c", axis=0)
    before_near = lax.all_gather(after(before, far), "c", axis=0)
    place = after(place, before_near)
    state = row_own(place, near, far, row_gain, row_qkv)
    before_far = lax.all_gather(after(before_other, state[0]), "c", axis=0)

    mine = after(mine, before_far)
    theirs = lax.ppermute(mine, ("yh", "yl", "c"), cross_route((1,)))
    sent = row_halo(place, before_near, before_far, row_gain, row_qkv, state, inputs)
    mine_swapped = lax.ppermute(after(mine, sent), "c", SWAP)

    moved = lax.all_to_all(sent.reshape(COLS, 4, 128), HEAD + SEQ, 0, 0, tiled=True)
    moved = moved.reshape(PARTS, 128, 2 * GROUP)
    theirs_swapped = lax.ppermute(after(theirs, sent), "c", SWAP)
    partial = row_output(place, moved, [mine, mine_swapped, theirs])
    mixed = col_layer(
        place,
        moved,
        partial,
        col_gain.reshape(PARTS, 1, GROUP),
        [mine, mine_swapped, theirs, theirs_swapped],
    )
    mixed = lax.all_to_all(mixed.reshape(COLS, 2, 128), HEAD + SEQ, 0, 0, tiled=True)
    return mixed.reshape(COLS, GROUP)


def solution(mesh):
    fine = Mesh(mesh.devices.reshape(4, 8, 4, 2, 2), SEQ + HEAD)
    return jax.shard_map(
        on_device,
        mesh=fine,
        in_specs=(
            P(SEQ, HEAD),
            P(),
            P(None, None, HEAD),
            P(HEAD, None),
            P(),
            P(None, None, HEAD),
            P(HEAD, None),
        ),
        out_specs=P(SEQ, HEAD),
        check_vma=False,
    )
```

```python
import functools

import jax
import jax.numpy as jnp
from jax import lax
from jax.experimental import pallas as pl
from jax.experimental.pallas import tpu as pltpu
from jax.sharding import Mesh, PartitionSpec as P

COLS = 512
HEAD_DIM = 64
SEQ = ("yh", "z", "x")
HEAD = ("yl", "c")
GROUP = 256
PARTS = 4
HEADS_HERE = GROUP // HEAD_DIM
MIB = 1 << 20
VMEM = pl.BlockSpec(memory_space=pltpu.VMEM)
SMEM = pl.BlockSpec(memory_space=pltpu.SMEM)
ANY = pl.BlockSpec(memory_space=pl.ANY)


def dot(a, b):
    return jnp.dot(a, b, preferred_element_type=jnp.float32)


def dot_t(a, b):
    return lax.dot_general(a, b, (((1,), (1,)), ((), ())), preferred_element_type=jnp.float32)


def normed_pieces(pieces, gains):
    flat = [p.astype(jnp.float32) for p in pieces]
    width = sum(p.shape[1] for p in pieces)
    mean = sum(jnp.sum(p, axis=-1, keepdims=True) for p in flat) / width
    flat = [p - mean for p in flat]
    var = sum(jnp.sum(p * p, axis=-1, keepdims=True) for p in flat) / width
    scale = lax.rsqrt(var + 1e-05)
    return [(p * scale * g).astype(jnp.bfloat16) for p, g in zip(flat, gains)]


def project(normed, order, weight, which):
    return sum(dot(p, weight[which, n]) for p, n in zip(normed, order)).astype(jnp.bfloat16)


def head_mask(rows, head):
    lane = lax.broadcasted_iota(jnp.int32, (rows, GROUP), 1)
    return (lane >= head * HEAD_DIM) & (lane < (head + 1) * HEAD_DIM)


def one_head(query, head):
    return jnp.where(head_mask(query.shape[0], head), query, jnp.bfloat16(0))


def triangle(block):
    row = lax.broadcasted_iota(jnp.int32, (block, block), 0)
    col = lax.broadcasted_iota(jnp.int32, (block, block), 1)
    return row, col


def attend_blocks(query, keys, vals, adjust):
    rows = query.shape[0]
    peak_all = norm_all = acc_all = jnp.zeros((rows, GROUP), jnp.float32)
    for head in range(HEADS_HERE):
        mask = head_mask(rows, head)
        qh = one_head(query, head)
        scores = [f(dot_t(qh, k)) for k, f in zip(keys, adjust)]
        peak = functools.reduce(jnp.maximum, scores)
        peak = jnp.max(peak, axis=-1, keepdims=True)
        expo = [jnp.exp(s - peak) for s in scores]
        norm = jnp.sum(sum(expo[1:], expo[0]), axis=-1, keepdims=True)
        acc = sum(dot(w.astype(jnp.bfloat16), v) for w, v in zip(expo, vals))
        peak_all = jnp.where(mask, peak, peak_all)
        norm_all = jnp.where(mask, norm, norm_all)
        acc_all = jnp.where(mask, acc, acc_all)
    return peak_all, norm_all, acc_all


BLOCK = 256
SCALE = HEAD_DIM ** (-0.5)


def row_own_kernel(place, near, far, gain, weight, query, peak, norm, acc, kv):
    order = [place[0], place[0] + 1, place[1], place[1] + 1]
    row, col = triangle(BLOCK)
    for i in range(COLS // BLOCK):
        rows = slice(i * BLOCK, (i + 1) * BLOCK)
        pieces = [near[0, rows], near[1, rows], far[0, rows], far[1, rows]]
        normed = normed_pieces(pieces, [gain[n] for n in order])
        query[rows] = project(normed, order, weight, 0)
        kv[0, rows] = project(normed, order, weight, 1)
        kv[1, rows] = project(normed, order, weight, 2)
    for i in range(COLS // BLOCK):
        rows = slice(i * BLOCK, (i + 1) * BLOCK)
        parts = [slice(j * BLOCK, (j + 1) * BLOCK) for j in range(i + 1)]
        adjust = [lambda s: s] * i + [lambda s: jnp.where(col <= row, s, -1e30)]
        peak[rows], norm[rows], acc[rows] = attend_blocks(
            query[rows], [kv[0, p] for p in parts], [kv[1, p] for p in parts], adjust
        )


def row_own(place, near, far, gain, weight):
    return pl.pallas_call(
        row_own_kernel,
        out_shape=(
            jax.ShapeDtypeStruct((COLS, GROUP), jnp.bfloat16),
            *[jax.ShapeDtypeStruct((COLS, GROUP), jnp.float32)] * 3,
        ),
        in_specs=[SMEM, VMEM, VMEM, VMEM, VMEM],
        out_specs=(VMEM,) * 4,
        scratch_shapes=[
            pltpu.VMEM((2, COLS, GROUP), jnp.bfloat16),
        ],
        compiler_params=pltpu.CompilerParams(vmem_limit_bytes=16 * MIB),
        cost_estimate=pl.CostEstimate(flops=1, bytes_accessed=1, transcendentals=0),
        name="row_own",
    )(place, near, far, gain, weight)


def row_halo_kernel(place, near, far, gain, weight, query, peak, norm, acc, source, out, kv):
    order = [place[0], place[0] + 1, place[1], place[1] + 1]
    row, col = triangle(BLOCK)
    blocked = jnp.where(place[2] > 0, 0.0, -1e30).astype(jnp.float32)
    blocks = COLS // BLOCK
    for i in range(blocks):
        rows = slice(i * BLOCK, (i + 1) * BLOCK)
        pieces = [near[0, rows], near[1, rows], far[0, rows], far[1, rows]]
        normed = normed_pieces(pieces, [gain[n] for n in order])
        kv[0, rows] = project(normed, order, weight, 1)
        kv[1, rows] = project(normed, order, weight, 2)
    for i in range(blocks):
        rows = slice(i * BLOCK, (i + 1) * BLOCK)
        parts = [slice(j * BLOCK, (j + 1) * BLOCK) for j in range(i, blocks)]
        adjust = [lambda s: jnp.where(col > row, s, -1e30) + blocked] + [lambda s: s + blocked] * (blocks - 1 - i)
        peak2, norm2, acc2 = attend_blocks(
            query[rows], [kv[0, p] for p in parts], [kv[1, p] for p in parts], adjust
        )
        top = jnp.maximum(peak[rows], peak2)
        one, two = jnp.exp(peak[rows] - top), jnp.exp(peak2 - top)
        att = (acc[rows] * one + acc2 * two) / (norm[rows] * one + norm2 * two)
        out[rows, :GROUP] = att.astype(jnp.bfloat16)
        out[rows, GROUP:] = source[rows]


def row_halo(place, near, far, gain, weight, state, source):
    return pl.pallas_call(
        row_halo_kernel,
        out_shape=jax.ShapeDtypeStruct((COLS, 2 * GROUP), jnp.bfloat16),
        in_specs=[SMEM] + [VMEM] * 9,
        out_specs=VMEM,
        scratch_shapes=[
            pltpu.VMEM((2, COLS, GROUP), jnp.bfloat16),
        ],
        compiler_params=pltpu.CompilerParams(vmem_limit_bytes=16 * MIB),
        cost_estimate=pl.CostEstimate(flops=1, bytes_accessed=1, transcendentals=0),
        name="row_halo",
    )(place, near, far, gain, weight, *state, source)


QKV_AT, OUT_AT, WEIGHT_ROWS = 1024, 4096, 5120
LONG = 2*10**10


def pack_kernel(row_out, col_qkv, col_out, packed, sem):
    pairs = [(col_qkv, packed.at[QKV_AT:OUT_AT])]
    for source, at in ((row_out, 0), (col_out, OUT_AT)):
        for n in range(PARTS):
            rows = slice(at + n * GROUP, at + (n + 1) * GROUP)
            pairs.append((source.at[:, n * GROUP : (n + 1) * GROUP], packed.at[rows]))
    copies = [pltpu.make_async_copy(a, b, sem.at[i]) for i, (a, b) in enumerate(pairs)]
    for copy in copies:
        copy.start()
    for copy in copies:
        copy.wait()


def pack_weights(row_out, col_qkv, col_out):
    return pl.pallas_call(
        pack_kernel,
        out_shape=jax.ShapeDtypeStruct((WEIGHT_ROWS, GROUP), jnp.bfloat16),
        in_specs=[ANY] * 3,
        out_specs=ANY,
        scratch_shapes=[pltpu.SemaphoreType.DMA((2 * PARTS + 1,))],
        compiler_params=pltpu.CompilerParams(vmem_limit_bytes=MIB),
        cost_estimate=pl.CostEstimate(flops=1, bytes_accessed=1, transcendentals=0),
        name="pack_weights",
    )(row_out, col_qkv, col_out)


def weight_groups(place):
    return [place[0] + place[3], place[0] + 1 - place[3], place[1] + place[3], place[1] + 1 - place[3]]


def row_output_kernel(place, moved, weights, out, held, sem):
    copy = pltpu.make_async_copy(weights.at[:QKV_AT], held, sem)
    copy.start()
    att = moved[weight_groups(place)[0], :, :GROUP]
    copy.wait()
    for n in range(PARTS):
        out[n] = moved[n, :, GROUP:].astype(jnp.float32) + dot(att, held[n * GROUP : (n + 1) * GROUP, :])


def row_output(place, moved, weights):
    return pl.pallas_call(
        row_output_kernel,
        out_shape=jax.ShapeDtypeStruct((PARTS, 128, GROUP), jnp.float32),
        in_specs=[SMEM, VMEM, ANY],
        out_specs=VMEM,
        scratch_shapes=[pltpu.VMEM((QKV_AT, GROUP), jnp.bfloat16), pltpu.SemaphoreType.DMA],
        compiler_params=pltpu.CompilerParams(vmem_limit_bytes=8 * MIB),
        cost_estimate=pl.CostEstimate(flops=LONG, bytes_accessed=1, transcendentals=0),
        name="row_output",
    )(place, moved, weights)


def col_layer_kernel(place, moved, partial, gain, w0, w1, w2, w3, out, held, last, sem):
    arrays = (w0, w1, w2, w3)
    first = [pltpu.make_async_copy(w.at[:QKV_AT], last.at[i], sem.at[PARTS + i]) for i, w in enumerate(arrays[1:])]
    rest = [pltpu.make_async_copy(w.at[QKV_AT:], held.at[i], sem.at[i]) for i, w in enumerate(arrays)]
    for copy in first + rest:
        copy.start()
    atts = [moved[g, :, :GROUP] for g in weight_groups(place)[1:]]
    for copy in first:
        copy.wait()
    pieces = []
    for n in range(PARTS):
        total = sum(dot(a, last[i, n * GROUP : (n + 1) * GROUP, :]) for i, a in enumerate(atts))
        pieces.append((partial[n] + total).astype(jnp.bfloat16))
    normed = normed_pieces(pieces, [gain[n] for n in range(PARTS)])
    normed = jnp.concatenate(normed, axis=1)
    rows = normed.shape[0]
    row, col = triangle(rows)
    allowed = jnp.concatenate([col <= row] * HEADS_HERE, axis=0)
    atts = []
    for i, copy in enumerate(rest):
        copy.wait()
        q, k, v = [dot(normed, held[i, j * 1024 : (j + 1) * 1024, :]).astype(jnp.bfloat16) for j in range(3)]
        q = q * jnp.bfloat16(SCALE)
        scores = dot_t(jnp.concatenate([one_head(q, head) for head in range(HEADS_HERE)], axis=0), k)
        scores = jnp.where(allowed, scores, -1e30)
        expo = jnp.exp(scores - jnp.max(scores, axis=-1, keepdims=True))
        norm = jnp.sum(expo, axis=-1, keepdims=True)
        acc = dot(expo.astype(jnp.bfloat16), v) / norm
        att = acc[:rows]
        for head in range(1, HEADS_HERE):
            att = jnp.where(head_mask(rows, head), acc[head * rows : (head + 1) * rows], att)
        atts.append(att.astype(jnp.bfloat16))
    for n in range(PARTS):
        at = OUT_AT - QKV_AT + n * GROUP
        total = sum(dot(a, held[i, at : at + GROUP, :]) for i, a in enumerate(atts))
        out[n] = (pieces[n].astype(jnp.float32) + total).astype(jnp.bfloat16)


def col_layer(place, moved, partial, gain, weights):
    return pl.pallas_call(
        col_layer_kernel,
        out_shape=jax.ShapeDtypeStruct((PARTS, 128, GROUP), jnp.bfloat16),
        in_specs=[SMEM, VMEM, VMEM, VMEM] + [ANY] * 4,
        out_specs=VMEM,
        scratch_shapes=[
            pltpu.VMEM((PARTS, WEIGHT_ROWS - QKV_AT, GROUP), jnp.bfloat16),
            pltpu.VMEM((PARTS - 1, QKV_AT, GROUP), jnp.bfloat16),
            pltpu.SemaphoreType.DMA((2 * PARTS - 1,)),
        ],
        compiler_params=pltpu.CompilerParams(vmem_limit_bytes=20 * MIB),
        cost_estimate=pl.CostEstimate(flops=1, bytes_accessed=1, transcendentals=0),
        name="col_layer",
    )(place, moved, partial, gain, *weights)


SWAP = [(0, 1), (1, 0)]


def after(value, *others):
    return lax.optimization_barrier((value, *others))[0]


def cross_route(outer):
    route = []
    for yh in range(4):
        for core in range(2):
            a = yh * 4 + 2 + core
            b = ((yh + 1) % 4 if core in outer else yh) * 4 + core
            route += [(a, b), (b, a)]
    return route


def on_device(inputs, row_gain, row_qkv, row_out, col_gain, col_qkv, col_out):
    yl, core = lax.axis_index("yl"), lax.axis_index("c")
    place = jnp.stack([yl * 2, (1 - yl) * 2, lax.axis_index(SEQ), core]).astype(jnp.int32)
    row_gain = row_gain.reshape(PARTS, 1, GROUP)
    row_qkv = row_qkv.transpose(1, 0, 2).reshape(3, PARTS, GROUP, GROUP)
    row_qkv = row_qkv * jnp.array([SCALE, 1, 1], jnp.bfloat16)[:, None, None, None]

    before = lax.ppermute(inputs, SEQ, [(i, i + 1) for i in range(127)])
    other = lax.ppermute(inputs, "yl", SWAP)
    near = lax.all_gather(inputs, "c", axis=0)
    mine = pack_weights(row_out, col_qkv.transpose(1, 0, 2).reshape(3 * 1024, GROUP), col_out)
    mine, row_qkv, before = lax.optimization_barrier((mine, row_qkv, before, near))[:3]
    before_other = lax.ppermute(before, "yl", SWAP)
    far = lax.all_gather(after(other, before), "c", axis=0)
    before_near = lax.all_gather(after(before, far), "c", axis=0)
    place = after(place, before_near)
    state = row_own(place, near, far, row_gain, row_qkv)
    before_far = lax.all_gather(after(before_other, state[0]), "c", axis=0)

    mine = after(mine, before_other, state[0])
    theirs = lax.ppermute(mine, ("yh", "yl", "c"), cross_route((1,)))
    sent = row_halo(place, before_near, before_far, row_gain, row_qkv, state, inputs)
    mine_swapped = lax.ppermute(after(mine, sent), "c", SWAP)

    moved = lax.all_to_all(sent.reshape(COLS, 4, 128), HEAD + SEQ, 0, 0, tiled=True)
    moved = moved.reshape(PARTS, 128, 2 * GROUP)
    theirs_swapped = lax.ppermute(after(theirs, sent), "c", SWAP)
    partial = row_output(place, moved, mine)
    mixed = col_layer(
        place,
        moved,
        partial,
        col_gain.reshape(PARTS, 1, GROUP),
        [mine, mine_swapped, theirs, theirs_swapped],
    )
    mixed = lax.all_to_all(mixed.reshape(COLS, 2, 128), HEAD + SEQ, 0, 0, tiled=True)
    return mixed.reshape(COLS, GROUP)


def solution(mesh):
    fine = Mesh(mesh.devices.reshape(4, 8, 4, 2, 2), SEQ + HEAD)
    return jax.shard_map(
        on_device,
        mesh=fine,
        in_specs=(
            P(SEQ, HEAD),
            P(),
            P(None, None, HEAD),
            P(HEAD, None),
            P(),
            P(None, None, HEAD),
            P(HEAD, None),
        ),
        out_specs=P(SEQ, HEAD),
        check_vma=False,
    )
```

```python
import functools

import jax
import jax.numpy as jnp
from jax import lax
from jax.experimental import pallas as pl
from jax.experimental.pallas import tpu as pltpu
from jax.sharding import Mesh, PartitionSpec as P

COLS = 512
HEAD_DIM = 64
SEQ = ("yh", "z", "x")
HEAD = ("yl", "c")
GROUP = 256
PARTS = 4
HEADS_HERE = GROUP // HEAD_DIM
MIB = 1 << 20
VMEM = pl.BlockSpec(memory_space=pltpu.VMEM)
SMEM = pl.BlockSpec(memory_space=pltpu.SMEM)
ANY = pl.BlockSpec(memory_space=pl.ANY)


def dot(a, b):
    return jnp.dot(a, b, preferred_element_type=jnp.float32)


def dot_t(a, b):
    return lax.dot_general(a, b, (((1,), (1,)), ((), ())), preferred_element_type=jnp.float32)


def normed_pieces(pieces, gains):
    flat = [p.astype(jnp.float32) for p in pieces]
    width = sum(p.shape[1] for p in pieces)
    mean = sum(jnp.sum(p, axis=-1, keepdims=True) for p in flat) / width
    flat = [p - mean for p in flat]
    var = sum(jnp.sum(p * p, axis=-1, keepdims=True) for p in flat) / width
    scale = lax.rsqrt(var + 1e-05)
    return [(p * scale * g).astype(jnp.bfloat16) for p, g in zip(flat, gains)]


def project(normed, order, weight, which):
    return sum(dot(p, weight[which, n]) for p, n in zip(normed, order)).astype(jnp.bfloat16)


def head_mask(rows, head):
    lane = lax.broadcasted_iota(jnp.int32, (rows, GROUP), 1)
    return (lane >= head * HEAD_DIM) & (lane < (head + 1) * HEAD_DIM)


def one_head(query, head):
    return jnp.where(head_mask(query.shape[0], head), query, jnp.bfloat16(0))


def triangle(block):
    row = lax.broadcasted_iota(jnp.int32, (block, block), 0)
    col = lax.broadcasted_iota(jnp.int32, (block, block), 1)
    return row, col


def attend_blocks(query, keys, vals, adjust):
    rows = query.shape[0]
    peak_all = norm_all = acc_all = jnp.zeros((rows, GROUP), jnp.float32)
    for head in range(HEADS_HERE):
        mask = head_mask(rows, head)
        qh = one_head(query, head)
        scores = [f(dot_t(qh, k)) for k, f in zip(keys, adjust)]
        peak = functools.reduce(jnp.maximum, scores)
        peak = jnp.max(peak, axis=-1, keepdims=True)
        expo = [jnp.exp(s - peak) for s in scores]
        norm = jnp.sum(sum(expo[1:], expo[0]), axis=-1, keepdims=True)
        acc = sum(dot(w.astype(jnp.bfloat16), v) for w, v in zip(expo, vals))
        peak_all = jnp.where(mask, peak, peak_all)
        norm_all = jnp.where(mask, norm, norm_all)
        acc_all = jnp.where(mask, acc, acc_all)
    return peak_all, norm_all, acc_all


BLOCK = 256
SCALE = HEAD_DIM ** (-0.5)


def row_own_kernel(place, near, far, gain, weight, query, peak, norm, acc, kv):
    order = [place[0], place[0] + 1, place[1], place[1] + 1]
    row, col = triangle(BLOCK)
    for i in range(COLS // BLOCK):
        rows = slice(i * BLOCK, (i + 1) * BLOCK)
        pieces = [near[0, rows], near[1, rows], far[0, rows], far[1, rows]]
        normed = normed_pieces(pieces, [gain[n] for n in order])
        query[rows] = project(normed, order, weight, 0)
        kv[0, rows] = project(normed, order, weight, 1)
        kv[1, rows] = project(normed, order, weight, 2)
    for i in range(COLS // BLOCK):
        rows = slice(i * BLOCK, (i + 1) * BLOCK)
        parts = [slice(j * BLOCK, (j + 1) * BLOCK) for j in range(i + 1)]
        adjust = [lambda s: s] * i + [lambda s: jnp.where(col <= row, s, -1e30)]
        peak[rows], norm[rows], acc[rows] = attend_blocks(
            query[rows], [kv[0, p] for p in parts], [kv[1, p] for p in parts], adjust
        )


def row_own(place, near, far, gain, weight):
    return pl.pallas_call(
        row_own_kernel,
        out_shape=(
            jax.ShapeDtypeStruct((COLS, GROUP), jnp.bfloat16),
            *[jax.ShapeDtypeStruct((COLS, GROUP), jnp.float32)] * 3,
        ),
        in_specs=[SMEM, VMEM, VMEM, VMEM, VMEM],
        out_specs=(VMEM,) * 4,
        scratch_shapes=[
            pltpu.VMEM((2, COLS, GROUP), jnp.bfloat16),
        ],
        compiler_params=pltpu.CompilerParams(vmem_limit_bytes=16 * MIB),
        cost_estimate=pl.CostEstimate(flops=1, bytes_accessed=1, transcendentals=0),
        name="row_own",
    )(place, near, far, gain, weight)


def row_halo_kernel(place, near, far, gain, weight, query, peak, norm, acc, source, out, kv):
    order = [place[0], place[0] + 1, place[1], place[1] + 1]
    row, col = triangle(BLOCK)
    blocked = jnp.where(place[2] > 0, 0.0, -1e30).astype(jnp.float32)
    blocks = COLS // BLOCK
    for i in range(blocks):
        rows = slice(i * BLOCK, (i + 1) * BLOCK)
        pieces = [near[0, rows], near[1, rows], far[0, rows], far[1, rows]]
        normed = normed_pieces(pieces, [gain[n] for n in order])
        kv[0, rows] = project(normed, order, weight, 1)
        kv[1, rows] = project(normed, order, weight, 2)
    for i in range(blocks):
        rows = slice(i * BLOCK, (i + 1) * BLOCK)
        parts = [slice(j * BLOCK, (j + 1) * BLOCK) for j in range(i, blocks)]
        adjust = [lambda s: jnp.where(col > row, s, -1e30) + blocked] + [lambda s: s + blocked] * (blocks - 1 - i)
        peak2, norm2, acc2 = attend_blocks(
            query[rows], [kv[0, p] for p in parts], [kv[1, p] for p in parts], adjust
        )
        top = jnp.maximum(peak[rows], peak2)
        one, two = jnp.exp(peak[rows] - top), jnp.exp(peak2 - top)
        att = (acc[rows] * one + acc2 * two) / (norm[rows] * one + norm2 * two)
        out[rows, :GROUP] = att.astype(jnp.bfloat16)
        out[rows, GROUP:] = source[rows]


def row_halo(place, near, far, gain, weight, state, source):
    return pl.pallas_call(
        row_halo_kernel,
        out_shape=jax.ShapeDtypeStruct((COLS, 2 * GROUP), jnp.bfloat16),
        in_specs=[SMEM] + [VMEM] * 9,
        out_specs=VMEM,
        scratch_shapes=[
            pltpu.VMEM((2, COLS, GROUP), jnp.bfloat16),
        ],
        compiler_params=pltpu.CompilerParams(vmem_limit_bytes=16 * MIB),
        cost_estimate=pl.CostEstimate(flops=1, bytes_accessed=1, transcendentals=0),
        name="row_halo",
    )(place, near, far, gain, weight, *state, source)


QKV_AT, OUT_AT, WEIGHT_ROWS = 1024, 4096, 5120
LONG = 2*10**10


def pack_kernel(row_out, col_qkv, col_out, packed, sem):
    pairs = [(col_qkv, packed.at[QKV_AT:OUT_AT])]
    for source, at in ((row_out, 0), (col_out, OUT_AT)):
        for n in range(PARTS):
            rows = slice(at + n * GROUP, at + (n + 1) * GROUP)
            pairs.append((source.at[:, n * GROUP : (n + 1) * GROUP], packed.at[rows]))
    copies = [pltpu.make_async_copy(a, b, sem.at[i]) for i, (a, b) in enumerate(pairs)]
    for copy in copies:
        copy.start()
    for copy in copies:
        copy.wait()


def pack_weights(row_out, col_qkv, col_out):
    return pl.pallas_call(
        pack_kernel,
        out_shape=jax.ShapeDtypeStruct((WEIGHT_ROWS, GROUP), jnp.bfloat16),
        in_specs=[ANY] * 3,
        out_specs=ANY,
        scratch_shapes=[pltpu.SemaphoreType.DMA((2 * PARTS + 1,))],
        compiler_params=pltpu.CompilerParams(vmem_limit_bytes=MIB),
        cost_estimate=pl.CostEstimate(flops=1, bytes_accessed=1, transcendentals=0),
        name="pack_weights",
    )(row_out, col_qkv, col_out)


def weight_groups(place):
    return [place[0] + place[3], place[0] + 1 - place[3], place[1] + place[3], place[1] + 1 - place[3]]


def row_output_kernel(place, moved, weights, out, held, sem):
    copy = pltpu.make_async_copy(weights.at[:QKV_AT], held, sem)
    copy.start()
    att = moved[weight_groups(place)[0], :, :GROUP]
    copy.wait()
    for n in range(PARTS):
        out[n] = moved[n, :, GROUP:].astype(jnp.float32) + dot(att, held[n * GROUP : (n + 1) * GROUP, :])


def row_output(place, moved, weights):
    return pl.pallas_call(
        row_output_kernel,
        out_shape=jax.ShapeDtypeStruct((PARTS, 128, GROUP), jnp.float32),
        in_specs=[SMEM, VMEM, ANY],
        out_specs=VMEM,
        scratch_shapes=[pltpu.VMEM((QKV_AT, GROUP), jnp.bfloat16), pltpu.SemaphoreType.DMA],
        compiler_params=pltpu.CompilerParams(vmem_limit_bytes=8 * MIB),
        cost_estimate=pl.CostEstimate(flops=LONG, bytes_accessed=1, transcendentals=0),
        name="row_output",
    )(place, moved, weights)


def col_layer_kernel(place, moved, partial, gain, w0, w1, w2, w3, out, held, last, sem):
    arrays = (w0, w1, w2, w3)
    first = [pltpu.make_async_copy(w.at[:QKV_AT], last.at[i], sem.at[PARTS + i]) for i, w in enumerate(arrays[1:])]
    rest = [pltpu.make_async_copy(w.at[QKV_AT:], held.at[i], sem.at[i]) for i, w in enumerate(arrays)]
    for copy in first + rest:
        copy.start()
    atts = [moved[g, :, :GROUP] for g in weight_groups(place)[1:]]
    for copy in first:
        copy.wait()
    pieces = []
    for n in range(PARTS):
        total = sum(dot(a, last[i, n * GROUP : (n + 1) * GROUP, :]) for i, a in enumerate(atts))
        pieces.append((partial[n] + total).astype(jnp.bfloat16))
    normed = normed_pieces(pieces, [gain[n] for n in range(PARTS)])
    normed = jnp.concatenate(normed, axis=1)
    rows = normed.shape[0]
    row, col = triangle(rows)
    allowed = jnp.concatenate([col <= row] * HEADS_HERE, axis=0)
    atts = []
    for i, copy in enumerate(rest):
        copy.wait()
        q, k, v = [dot(normed, held[i, j * 1024 : (j + 1) * 1024, :]).astype(jnp.bfloat16) for j in range(3)]
        q = q * jnp.bfloat16(SCALE)
        scores = dot_t(jnp.concatenate([one_head(q, head) for head in range(HEADS_HERE)], axis=0), k)
        scores = jnp.where(allowed, scores, -1e30)
        expo = jnp.exp(scores - jnp.max(scores, axis=-1, keepdims=True))
        norm = jnp.sum(expo, axis=-1, keepdims=True)
        acc = dot(expo.astype(jnp.bfloat16), v) / norm
        att = acc[:rows]
        for head in range(1, HEADS_HERE):
            att = jnp.where(head_mask(rows, head), acc[head * rows : (head + 1) * rows], att)
        atts.append(att.astype(jnp.bfloat16))
    for n in range(PARTS):
        at = OUT_AT - QKV_AT + n * GROUP
        total = sum(dot(a, held[i, at : at + GROUP, :]) for i, a in enumerate(atts))
        out[n] = (pieces[n].astype(jnp.float32) + total).astype(jnp.bfloat16)


def col_layer(place, moved, partial, gain, weights):
    return pl.pallas_call(
        col_layer_kernel,
        out_shape=jax.ShapeDtypeStruct((PARTS, 128, GROUP), jnp.bfloat16),
        in_specs=[SMEM, VMEM, VMEM, VMEM] + [ANY] * 4,
        out_specs=VMEM,
        scratch_shapes=[
            pltpu.VMEM((PARTS, WEIGHT_ROWS - QKV_AT, GROUP), jnp.bfloat16),
            pltpu.VMEM((PARTS - 1, QKV_AT, GROUP), jnp.bfloat16),
            pltpu.SemaphoreType.DMA((2 * PARTS - 1,)),
        ],
        compiler_params=pltpu.CompilerParams(vmem_limit_bytes=20 * MIB),
        cost_estimate=pl.CostEstimate(flops=1, bytes_accessed=1, transcendentals=0),
        name="col_layer",
    )(place, moved, partial, gain, *weights)


SWAP = [(0, 1), (1, 0)]


def after(value, *others):
    return lax.optimization_barrier((value, *others))[0]


def cross_route(outer):
    route = []
    for yh in range(4):
        for core in range(2):
            a = yh * 4 + 2 + core
            b = ((yh + 1) % 4 if core in outer else yh) * 4 + core
            route += [(a, b), (b, a)]
    return route


def on_device(inputs, row_gain, row_qkv, row_out, col_gain, col_qkv, col_out):
    yl, core = lax.axis_index("yl"), lax.axis_index("c")
    place = jnp.stack([yl * 2, (1 - yl) * 2, lax.axis_index(SEQ), core]).astype(jnp.int32)
    row_gain = row_gain.reshape(PARTS, 1, GROUP)
    row_qkv = row_qkv.transpose(1, 0, 2).reshape(3, PARTS, GROUP, GROUP)
    row_qkv = row_qkv * jnp.array([SCALE, 1, 1], jnp.bfloat16)[:, None, None, None]

    before = lax.ppermute(inputs, SEQ, [(i, i + 1) for i in range(127)])
    near = lax.all_gather(inputs, "c", axis=0)
    mine = pack_weights(row_out, col_qkv.transpose(1, 0, 2).reshape(3 * 1024, GROUP), col_out)
    other = lax.ppermute(after(inputs, near, mine), "yl", SWAP)
    mine, row_qkv, before = lax.optimization_barrier((mine, row_qkv, before, near))[:3]
    before_other = lax.ppermute(before, "yl", SWAP)
    far = lax.all_gather(after(other, before), "c", axis=0)
    before_near = lax.all_gather(after(before, far), "c", axis=0)
    place = after(place, before_near)
    state = row_own(place, near, far, row_gain, row_qkv)
    before_far = lax.all_gather(after(before_other, state[0]), "c", axis=0)

    mine = after(mine, before_other, state[0])
    theirs = lax.ppermute(mine, ("yh", "yl", "c"), cross_route((1,)))
    sent = row_halo(place, before_near, before_far, row_gain, row_qkv, state, inputs)
    mine_swapped = lax.ppermute(after(mine, sent), "c", SWAP)

    moved = lax.all_to_all(sent.reshape(COLS, 4, 128), HEAD + SEQ, 0, 0, tiled=True)
    moved = moved.reshape(PARTS, 128, 2 * GROUP)
    theirs_swapped = lax.ppermute(after(theirs, sent), "c", SWAP)
    partial = row_output(place, moved, mine)
    mixed = col_layer(
        place,
        moved,
        partial,
        col_gain.reshape(PARTS, 1, GROUP),
        [mine, mine_swapped, theirs, theirs_swapped],
    )
    mixed = lax.all_to_all(mixed.reshape(COLS, 2, 128), HEAD + SEQ, 0, 0, tiled=True)
    return mixed.reshape(COLS, GROUP)


def solution(mesh):
    fine = Mesh(mesh.devices.reshape(4, 8, 4, 2, 2), SEQ + HEAD)
    return jax.shard_map(
        on_device,
        mesh=fine,
        in_specs=(
            P(SEQ, HEAD),
            P(),
            P(None, None, HEAD),
            P(HEAD, None),
            P(),
            P(None, None, HEAD),
            P(HEAD, None),
        ),
        out_specs=P(SEQ, HEAD),
        check_vma=False,
    )
```

```python
import functools

import jax
import jax.numpy as jnp
from jax import lax
from jax.experimental import pallas as pl
from jax.experimental.pallas import tpu as pltpu
from jax.sharding import Mesh, PartitionSpec as P

COLS = 512
HEAD_DIM = 64
SEQ = ("yh", "z", "x")
HEAD = ("yl", "c")
GROUP = 256
PARTS = 4
HEADS_HERE = GROUP // HEAD_DIM
MIB = 1 << 20
VMEM = pl.BlockSpec(memory_space=pltpu.VMEM)
SMEM = pl.BlockSpec(memory_space=pltpu.SMEM)
ANY = pl.BlockSpec(memory_space=pl.ANY)


def dot(a, b):
    return jnp.dot(a, b, preferred_element_type=jnp.float32)


def dot_t(a, b):
    return lax.dot_general(a, b, (((1,), (1,)), ((), ())), preferred_element_type=jnp.float32)


def normed_pieces(pieces, gains):
    flat = [p.astype(jnp.float32) for p in pieces]
    width = sum(p.shape[1] for p in pieces)
    mean = sum(jnp.sum(p, axis=-1, keepdims=True) for p in flat) / width
    flat = [p - mean for p in flat]
    var = sum(jnp.sum(p * p, axis=-1, keepdims=True) for p in flat) / width
    scale = lax.rsqrt(var + 1e-05)
    return [(p * scale * g).astype(jnp.bfloat16) for p, g in zip(flat, gains)]


def project(normed, order, weight, which):
    return sum(dot(p, weight[which, n]) for p, n in zip(normed, order)).astype(jnp.bfloat16)


def head_mask(rows, head):
    lane = lax.broadcasted_iota(jnp.int32, (rows, GROUP), 1)
    return (lane >= head * HEAD_DIM) & (lane < (head + 1) * HEAD_DIM)


def one_head(query, head):
    return jnp.where(head_mask(query.shape[0], head), query, jnp.bfloat16(0))


def triangle(block):
    row = lax.broadcasted_iota(jnp.int32, (block, block), 0)
    col = lax.broadcasted_iota(jnp.int32, (block, block), 1)
    return row, col


def attend_blocks(query, keys, vals, adjust):
    rows = query.shape[0]
    peak_all = norm_all = acc_all = jnp.zeros((rows, GROUP), jnp.float32)
    for head in range(HEADS_HERE):
        mask = head_mask(rows, head)
        qh = one_head(query, head)
        scores = [f(dot_t(qh, k)) for k, f in zip(keys, adjust)]
        peak = functools.reduce(jnp.maximum, scores)
        peak = jnp.max(peak, axis=-1, keepdims=True)
        expo = [jnp.exp(s - peak) for s in scores]
        norm = jnp.sum(sum(expo[1:], expo[0]), axis=-1, keepdims=True)
        acc = sum(dot(w.astype(jnp.bfloat16), v) for w, v in zip(expo, vals))
        peak_all = jnp.where(mask, peak, peak_all)
        norm_all = jnp.where(mask, norm, norm_all)
        acc_all = jnp.where(mask, acc, acc_all)
    return peak_all, norm_all, acc_all


BLOCK = 256
SCALE = HEAD_DIM ** (-0.5)


def row_own_kernel(place, near, far, gain, weight, query, peak, norm, acc, kv):
    order = [place[0], place[0] + 1, place[1], place[1] + 1]
    row, col = triangle(BLOCK)
    for i in range(COLS // BLOCK):
        rows = slice(i * BLOCK, (i + 1) * BLOCK)
        pieces = [near[0, rows], near[1, rows], far[0, rows], far[1, rows]]
        normed = normed_pieces(pieces, [gain[n] for n in order])
        query[rows] = project(normed, order, weight, 0)
        kv[0, rows] = project(normed, order, weight, 1)
        kv[1, rows] = project(normed, order, weight, 2)
    for i in range(COLS // BLOCK):
        rows = slice(i * BLOCK, (i + 1) * BLOCK)
        parts = [slice(j * BLOCK, (j + 1) * BLOCK) for j in range(i + 1)]
        adjust = [lambda s: s] * i + [lambda s: jnp.where(col <= row, s, -1e30)]
        peak[rows], norm[rows], acc[rows] = attend_blocks(
            query[rows], [kv[0, p] for p in parts], [kv[1, p] for p in parts], adjust
        )


def row_own(place, near, far, gain, weight):
    return pl.pallas_call(
        row_own_kernel,
        out_shape=(
            jax.ShapeDtypeStruct((COLS, GROUP), jnp.bfloat16),
            *[jax.ShapeDtypeStruct((COLS, GROUP), jnp.float32)] * 3,
        ),
        in_specs=[SMEM, VMEM, VMEM, VMEM, VMEM],
        out_specs=(VMEM,) * 4,
        scratch_shapes=[
            pltpu.VMEM((2, COLS, GROUP), jnp.bfloat16),
        ],
        compiler_params=pltpu.CompilerParams(vmem_limit_bytes=16 * MIB),
        cost_estimate=pl.CostEstimate(flops=1, bytes_accessed=1, transcendentals=0),
        name="row_own",
    )(place, near, far, gain, weight)


def row_halo_kernel(place, near, far, gain, weight, query, peak, norm, acc, source, out, kv):
    order = [place[0], place[0] + 1, place[1], place[1] + 1]
    row, col = triangle(BLOCK)
    blocked = jnp.where(place[2] > 0, 0.0, -1e30).astype(jnp.float32)
    blocks = COLS // BLOCK
    for i in range(blocks):
        rows = slice(i * BLOCK, (i + 1) * BLOCK)
        pieces = [near[0, rows], near[1, rows], far[0, rows], far[1, rows]]
        normed = normed_pieces(pieces, [gain[n] for n in order])
        kv[0, rows] = project(normed, order, weight, 1)
        kv[1, rows] = project(normed, order, weight, 2)
    for i in range(blocks):
        rows = slice(i * BLOCK, (i + 1) * BLOCK)
        parts = [slice(j * BLOCK, (j + 1) * BLOCK) for j in range(i, blocks)]
        adjust = [lambda s: jnp.where(col > row, s, -1e30) + blocked] + [lambda s: s + blocked] * (blocks - 1 - i)
        peak2, norm2, acc2 = attend_blocks(
            query[rows], [kv[0, p] for p in parts], [kv[1, p] for p in parts], adjust
        )
        top = jnp.maximum(peak[rows], peak2)
        one, two = jnp.exp(peak[rows] - top), jnp.exp(peak2 - top)
        att = (acc[rows] * one + acc2 * two) / (norm[rows] * one + norm2 * two)
        out[rows, :GROUP] = att.astype(jnp.bfloat16)
        out[rows, GROUP:] = source[rows]


def row_halo(place, near, far, gain, weight, state, source):
    return pl.pallas_call(
        row_halo_kernel,
        out_shape=jax.ShapeDtypeStruct((COLS, 2 * GROUP), jnp.bfloat16),
        in_specs=[SMEM] + [VMEM] * 9,
        out_specs=VMEM,
        scratch_shapes=[
            pltpu.VMEM((2, COLS, GROUP), jnp.bfloat16),
        ],
        compiler_params=pltpu.CompilerParams(vmem_limit_bytes=16 * MIB),
        cost_estimate=pl.CostEstimate(flops=1, bytes_accessed=1, transcendentals=0),
        name="row_halo",
    )(place, near, far, gain, weight, *state, source)


QKV_AT, OUT_AT, WEIGHT_ROWS = 1024, 4096, 5120
LONG = 2*10**10


def pack_kernel(row_out, col_qkv, col_out, packed, main, last, sem):
    pairs = [(col_qkv, packed.at[QKV_AT:OUT_AT]), (col_qkv, main.at[QKV_AT:OUT_AT])]
    for n in range(PARTS):
        rows = slice(n * GROUP, (n + 1) * GROUP)
        pairs += [(row_out.at[:, rows], to.at[rows]) for to in (packed, main)]
        pairs += [(col_out.at[:, rows], last.at[rows])]
        pairs += [(col_out.at[:, rows], packed.at[OUT_AT + n * GROUP : OUT_AT + (n + 1) * GROUP])]
    copies = [pltpu.make_async_copy(a, b, sem.at[i]) for i, (a, b) in enumerate(pairs)]
    for copy in copies:
        copy.start()
    for copy in copies:
        copy.wait()


def pack_weights(row_out, col_qkv, col_out):
    return pl.pallas_call(
        pack_kernel,
        out_shape=[jax.ShapeDtypeStruct((n, GROUP), jnp.bfloat16) for n in (WEIGHT_ROWS, OUT_AT, WEIGHT_ROWS - OUT_AT)],
        in_specs=[ANY] * 3,
        out_specs=[ANY] * 3,
        scratch_shapes=[pltpu.SemaphoreType.DMA((4 * PARTS + 2,))],
        compiler_params=pltpu.CompilerParams(vmem_limit_bytes=MIB),
        cost_estimate=pl.CostEstimate(flops=1, bytes_accessed=1, transcendentals=0),
        name="pack_weights",
    )(row_out, col_qkv, col_out)


def weight_groups(place):
    return [place[0] + place[3], place[0] + 1 - place[3], place[1] + place[3], place[1] + 1 - place[3]]


def row_output_kernel(place, moved, weights, out, held, sem):
    copy = pltpu.make_async_copy(weights.at[:QKV_AT], held, sem)
    copy.start()
    att = moved[weight_groups(place)[0], :, :GROUP]
    copy.wait()
    for n in range(PARTS):
        out[n] = moved[n, :, GROUP:].astype(jnp.float32) + dot(att, held[n * GROUP : (n + 1) * GROUP, :])


def row_output(place, moved, weights):
    return pl.pallas_call(
        row_output_kernel,
        out_shape=jax.ShapeDtypeStruct((PARTS, 128, GROUP), jnp.float32),
        in_specs=[SMEM, VMEM, ANY],
        out_specs=VMEM,
        scratch_shapes=[pltpu.VMEM((QKV_AT, GROUP), jnp.bfloat16), pltpu.SemaphoreType.DMA],
        compiler_params=pltpu.CompilerParams(vmem_limit_bytes=8 * MIB),
        cost_estimate=pl.CostEstimate(flops=LONG, bytes_accessed=1, transcendentals=0),
        name="row_output",
    )(place, moved, weights)


def col_layer_kernel(place, moved, partial, gain, w0, w1, w2, w3, out2, out3, out, held, last, sem):
    arrays = (w0, w1, w2, w3)
    first = [pltpu.make_async_copy(w.at[:QKV_AT], last.at[i], sem.at[PARTS + i]) for i, w in enumerate(arrays[1:])]
    rest = [
        pltpu.make_async_copy(w.at[QKV_AT:], held.at[i] if i < 2 else held.at[i, : OUT_AT - QKV_AT], sem.at[i])
        for i, w in enumerate(arrays)
    ]
    ends = [
        pltpu.make_async_copy(w, held.at[2 + i, OUT_AT - QKV_AT :], sem.at[2 * PARTS - 1 + i])
        for i, w in enumerate((out2, out3))
    ]
    for copy in first + rest + ends:
        copy.start()
    atts = [moved[g, :, :GROUP] for g in weight_groups(place)[1:]]
    for copy in first:
        copy.wait()
    pieces = []
    for n in range(PARTS):
        total = sum(dot(a, last[i, n * GROUP : (n + 1) * GROUP, :]) for i, a in enumerate(atts))
        pieces.append((partial[n] + total).astype(jnp.bfloat16))
    normed = normed_pieces(pieces, [gain[n] for n in range(PARTS)])
    normed = jnp.concatenate(normed, axis=1)
    rows = normed.shape[0]
    row, col = triangle(rows)
    allowed = jnp.concatenate([col <= row] * HEADS_HERE, axis=0)
    atts = []
    for i, copy in enumerate(rest):
        copy.wait()
        q, k, v = [dot(normed, held[i, j * 1024 : (j + 1) * 1024, :]).astype(jnp.bfloat16) for j in range(3)]
        q = q * jnp.bfloat16(SCALE)
        scores = dot_t(jnp.concatenate([one_head(q, head) for head in range(HEADS_HERE)], axis=0), k)
        scores = jnp.where(allowed, scores, -1e30)
        expo = jnp.exp(scores - jnp.max(scores, axis=-1, keepdims=True))
        norm = jnp.sum(expo, axis=-1, keepdims=True)
        acc = dot(expo.astype(jnp.bfloat16), v) / norm
        att = acc[:rows]
        for head in range(1, HEADS_HERE):
            att = jnp.where(head_mask(rows, head), acc[head * rows : (head + 1) * rows], att)
        atts.append(att.astype(jnp.bfloat16))
    for copy in ends:
        copy.wait()
    for n in range(PARTS):
        at = OUT_AT - QKV_AT + n * GROUP
        total = sum(dot(a, held[i, at : at + GROUP, :]) for i, a in enumerate(atts))
        out[n] = (pieces[n].astype(jnp.float32) + total).astype(jnp.bfloat16)


def col_layer(place, moved, partial, gain, weights):
    return pl.pallas_call(
        col_layer_kernel,
        out_shape=jax.ShapeDtypeStruct((PARTS, 128, GROUP), jnp.bfloat16),
        in_specs=[SMEM, VMEM, VMEM, VMEM] + [ANY] * 6,
        out_specs=VMEM,
        scratch_shapes=[
            pltpu.VMEM((PARTS, WEIGHT_ROWS - QKV_AT, GROUP), jnp.bfloat16),
            pltpu.VMEM((PARTS - 1, QKV_AT, GROUP), jnp.bfloat16),
            pltpu.SemaphoreType.DMA((2 * PARTS + 1,)),
        ],
        compiler_params=pltpu.CompilerParams(vmem_limit_bytes=20 * MIB),
        cost_estimate=pl.CostEstimate(flops=1, bytes_accessed=1, transcendentals=0),
        name="col_layer",
    )(place, moved, partial, gain, *weights)


SWAP = [(0, 1), (1, 0)]


def after(value, *others):
    return lax.optimization_barrier((value, *others))[0]


def cross_route(outer):
    route = []
    for yh in range(4):
        for core in range(2):
            a = yh * 4 + 2 + core
            b = ((yh + 1) % 4 if core in outer else yh) * 4 + core
            route += [(a, b), (b, a)]
    return route


def on_device(inputs, row_gain, row_qkv, row_out, col_gain, col_qkv, col_out):
    yl, core = lax.axis_index("yl"), lax.axis_index("c")
    place = jnp.stack([yl * 2, (1 - yl) * 2, lax.axis_index(SEQ), core]).astype(jnp.int32)
    row_gain = row_gain.reshape(PARTS, 1, GROUP)
    row_qkv = row_qkv.transpose(1, 0, 2).reshape(3, PARTS, GROUP, GROUP)
    row_qkv = row_qkv * jnp.array([SCALE, 1, 1], jnp.bfloat16)[:, None, None, None]

    before = lax.ppermute(inputs, SEQ, [(i, i + 1) for i in range(127)])
    near = lax.all_gather(inputs, "c", axis=0)
    mine, main, last = pack_weights(row_out, col_qkv.transpose(1, 0, 2).reshape(3 * 1024, GROUP), col_out)
    other = lax.ppermute(after(inputs, near, mine), "yl", SWAP)
    mine, main, last, row_qkv, before = lax.optimization_barrier((mine, main, last, row_qkv, before, near))[:5]
    before_other = lax.ppermute(before, "yl", SWAP)
    far = lax.all_gather(after(other, before), "c", axis=0)
    before_near = lax.all_gather(after(before, far), "c", axis=0)
    place = after(place, before_near)
    state = row_own(place, near, far, row_gain, row_qkv)
    before_far = lax.all_gather(after(before_other, state[0]), "c", axis=0)

    main = after(main, before_other, state[0])
    theirs = lax.ppermute(main, ("yh", "yl", "c"), cross_route((1,)))
    sent = row_halo(place, before_near, before_far, row_gain, row_qkv, state, inputs)
    mine_swapped = lax.ppermute(after(mine, sent), "c", SWAP)

    moved = lax.all_to_all(sent.reshape(COLS, 4, 128), HEAD + SEQ, 0, 0, tiled=True)
    moved = moved.reshape(PARTS, 128, 2 * GROUP)
    theirs_swapped = lax.ppermute(after(theirs, sent), "c", SWAP)
    last_theirs = lax.ppermute(after(last, sent), ("yh", "yl", "c"), cross_route((1,)))
    last_swapped = lax.ppermute(after(last_theirs, moved), "c", SWAP)
    partial = row_output(place, moved, mine)
    mixed = col_layer(
        place,
        moved,
        partial,
        col_gain.reshape(PARTS, 1, GROUP),
        [mine, mine_swapped, theirs, theirs_swapped, last_theirs, last_swapped],
    )
    mixed = lax.all_to_all(mixed.reshape(COLS, 2, 128), HEAD + SEQ, 0, 0, tiled=True)
    return mixed.reshape(COLS, GROUP)


def solution(mesh):
    fine = Mesh(mesh.devices.reshape(4, 8, 4, 2, 2), SEQ + HEAD)
    return jax.shard_map(
        on_device,
        mesh=fine,
        in_specs=(
            P(SEQ, HEAD),
            P(),
            P(None, None, HEAD),
            P(HEAD, None),
            P(),
            P(None, None, HEAD),
            P(HEAD, None),
        ),
        out_specs=P(SEQ, HEAD),
        check_vma=False,
    )
```

```python
import functools

import jax
import jax.numpy as jnp
from jax import lax
from jax.experimental import pallas as pl
from jax.experimental.pallas import tpu as pltpu
from jax.sharding import Mesh, PartitionSpec as P

COLS = 512
HEAD_DIM = 64
SEQ = ("yh", "z", "x")
HEAD = ("yl", "c")
GROUP = 256
PARTS = 4
HEADS_HERE = GROUP // HEAD_DIM
MIB = 1 << 20
VMEM = pl.BlockSpec(memory_space=pltpu.VMEM)
SMEM = pl.BlockSpec(memory_space=pltpu.SMEM)
ANY = pl.BlockSpec(memory_space=pl.ANY)


def dot(a, b):
    return jnp.dot(a, b, preferred_element_type=jnp.float32)


def dot_t(a, b):
    return lax.dot_general(a, b, (((1,), (1,)), ((), ())), preferred_element_type=jnp.float32)


def normed_pieces(pieces, gains):
    flat = [p.astype(jnp.float32) for p in pieces]
    width = sum(p.shape[1] for p in pieces)
    mean = sum(jnp.sum(p, axis=-1, keepdims=True) for p in flat) / width
    flat = [p - mean for p in flat]
    var = sum(jnp.sum(p * p, axis=-1, keepdims=True) for p in flat) / width
    scale = lax.rsqrt(var + 1e-05)
    return [(p * scale * g).astype(jnp.bfloat16) for p, g in zip(flat, gains)]


def project(normed, order, weight, which):
    return sum(dot(p, weight[which, n]) for p, n in zip(normed, order)).astype(jnp.bfloat16)


def head_mask(rows, head):
    lane = lax.broadcasted_iota(jnp.int32, (rows, GROUP), 1)
    return (lane >= head * HEAD_DIM) & (lane < (head + 1) * HEAD_DIM)


def one_head(query, head):
    return jnp.where(head_mask(query.shape[0], head), query, jnp.bfloat16(0))


def triangle(block):
    row = lax.broadcasted_iota(jnp.int32, (block, block), 0)
    col = lax.broadcasted_iota(jnp.int32, (block, block), 1)
    return row, col


def attend_blocks(query, keys, vals, adjust):
    rows = query.shape[0]
    peak_all = norm_all = acc_all = jnp.zeros((rows, GROUP), jnp.float32)
    for head in range(HEADS_HERE):
        mask = head_mask(rows, head)
        qh = one_head(query, head)
        scores = [f(dot_t(qh, k)) for k, f in zip(keys, adjust)]
        peak = functools.reduce(jnp.maximum, scores)
        peak = jnp.max(peak, axis=-1, keepdims=True)
        expo = [jnp.exp(s - peak) for s in scores]
        norm = jnp.sum(sum(expo[1:], expo[0]), axis=-1, keepdims=True)
        acc = sum(dot(w.astype(jnp.bfloat16), v) for w, v in zip(expo, vals))
        peak_all = jnp.where(mask, peak, peak_all)
        norm_all = jnp.where(mask, norm, norm_all)
        acc_all = jnp.where(mask, acc, acc_all)
    return peak_all, norm_all, acc_all


BLOCK = 256
SCALE = HEAD_DIM ** (-0.5)


def row_own_kernel(place, near, far, gain, weight, query, peak, norm, acc, kv):
    order = [place[0], place[0] + 1, place[1], place[1] + 1]
    row, col = triangle(BLOCK)
    for i in range(COLS // BLOCK):
        rows = slice(i * BLOCK, (i + 1) * BLOCK)
        pieces = [near[0, rows], near[1, rows], far[0, rows], far[1, rows]]
        normed = normed_pieces(pieces, [gain[n] for n in order])
        query[rows] = project(normed, order, weight, 0)
        kv[0, rows] = project(normed, order, weight, 1)
        kv[1, rows] = project(normed, order, weight, 2)
    for i in range(COLS // BLOCK):
        rows = slice(i * BLOCK, (i + 1) * BLOCK)
        parts = [slice(j * BLOCK, (j + 1) * BLOCK) for j in range(i + 1)]
        adjust = [lambda s: s] * i + [lambda s: jnp.where(col <= row, s, -1e30)]
        peak[rows], norm[rows], acc[rows] = attend_blocks(
            query[rows], [kv[0, p] for p in parts], [kv[1, p] for p in parts], adjust
        )


def row_own(place, near, far, gain, weight):
    return pl.pallas_call(
        row_own_kernel,
        out_shape=(
            jax.ShapeDtypeStruct((COLS, GROUP), jnp.bfloat16),
            *[jax.ShapeDtypeStruct((COLS, GROUP), jnp.float32)] * 3,
        ),
        in_specs=[SMEM, VMEM, VMEM, VMEM, VMEM],
        out_specs=(VMEM,) * 4,
        scratch_shapes=[
            pltpu.VMEM((2, COLS, GROUP), jnp.bfloat16),
        ],
        compiler_params=pltpu.CompilerParams(vmem_limit_bytes=16 * MIB),
        cost_estimate=pl.CostEstimate(flops=1, bytes_accessed=1, transcendentals=0),
        name="row_own",
    )(place, near, far, gain, weight)


def row_halo_kernel(place, near, far, gain, weight, query, peak, norm, acc, source, out, kv):
    order = [place[0], place[0] + 1, place[1], place[1] + 1]
    row, col = triangle(BLOCK)
    blocked = jnp.where(place[2] > 0, 0.0, -1e30).astype(jnp.float32)
    blocks = COLS // BLOCK
    for i in range(blocks):
        rows = slice(i * BLOCK, (i + 1) * BLOCK)
        pieces = [near[0, rows], near[1, rows], far[0, rows], far[1, rows]]
        normed = normed_pieces(pieces, [gain[n] for n in order])
        kv[0, rows] = project(normed, order, weight, 1)
        kv[1, rows] = project(normed, order, weight, 2)
    for i in range(blocks):
        rows = slice(i * BLOCK, (i + 1) * BLOCK)
        parts = [slice(j * BLOCK, (j + 1) * BLOCK) for j in range(i, blocks)]
        adjust = [lambda s: jnp.where(col > row, s, -1e30) + blocked] + [lambda s: s + blocked] * (blocks - 1 - i)
        peak2, norm2, acc2 = attend_blocks(
            query[rows], [kv[0, p] for p in parts], [kv[1, p] for p in parts], adjust
        )
        top = jnp.maximum(peak[rows], peak2)
        one, two = jnp.exp(peak[rows] - top), jnp.exp(peak2 - top)
        att = (acc[rows] * one + acc2 * two) / (norm[rows] * one + norm2 * two)
        out[rows, :GROUP] = att.astype(jnp.bfloat16)
        out[rows, GROUP:] = source[rows]


def row_halo(place, near, far, gain, weight, state, source):
    return pl.pallas_call(
        row_halo_kernel,
        out_shape=jax.ShapeDtypeStruct((COLS, 2 * GROUP), jnp.bfloat16),
        in_specs=[SMEM] + [VMEM] * 9,
        out_specs=VMEM,
        scratch_shapes=[
            pltpu.VMEM((2, COLS, GROUP), jnp.bfloat16),
        ],
        compiler_params=pltpu.CompilerParams(vmem_limit_bytes=16 * MIB),
        cost_estimate=pl.CostEstimate(flops=1, bytes_accessed=1, transcendentals=0),
        name="row_halo",
    )(place, near, far, gain, weight, *state, source)


QKV_AT, OUT_AT, WEIGHT_ROWS = 1024, 4096, 5120
LONG = 2*10**10


def pack_kernel(row_out, col_qkv, col_out, packed, main, last, sem):
    pairs = [(col_qkv, packed.at[QKV_AT:OUT_AT]), (col_qkv, main.at[QKV_AT:OUT_AT])]
    for n in range(PARTS):
        rows = slice(n * GROUP, (n + 1) * GROUP)
        pairs += [(row_out.at[:, rows], to.at[rows]) for to in (packed, main)]
        pairs += [(col_out.at[:, rows], last.at[rows])]
        pairs += [(col_out.at[:, rows], packed.at[OUT_AT + n * GROUP : OUT_AT + (n + 1) * GROUP])]
    copies = [pltpu.make_async_copy(a, b, sem.at[i]) for i, (a, b) in enumerate(pairs)]
    for copy in copies:
        copy.start()
    for copy in copies:
        copy.wait()


def pack_weights(row_out, col_qkv, col_out):
    return pl.pallas_call(
        pack_kernel,
        out_shape=[jax.ShapeDtypeStruct((n, GROUP), jnp.bfloat16) for n in (WEIGHT_ROWS, OUT_AT, WEIGHT_ROWS - OUT_AT)],
        in_specs=[ANY] * 3,
        out_specs=[ANY] * 3,
        scratch_shapes=[pltpu.SemaphoreType.DMA((4 * PARTS + 2,))],
        compiler_params=pltpu.CompilerParams(vmem_limit_bytes=MIB),
        cost_estimate=pl.CostEstimate(flops=1, bytes_accessed=1, transcendentals=0),
        name="pack_weights",
    )(row_out, col_qkv, col_out)


def weight_groups(place):
    return [place[0] + place[3], place[0] + 1 - place[3], place[1] + place[3], place[1] + 1 - place[3]]


def row_output_kernel(place, moved, weights, out, held, sem):
    copy = pltpu.make_async_copy(weights.at[:QKV_AT], held, sem)
    copy.start()
    att = moved[weight_groups(place)[0], :, :GROUP]
    copy.wait()
    for n in range(PARTS):
        out[n] = moved[n, :, GROUP:].astype(jnp.float32) + dot(att, held[n * GROUP : (n + 1) * GROUP, :])


def row_output(place, moved, weights):
    return pl.pallas_call(
        row_output_kernel,
        out_shape=jax.ShapeDtypeStruct((PARTS, 128, GROUP), jnp.float32),
        in_specs=[SMEM, VMEM, ANY],
        out_specs=VMEM,
        scratch_shapes=[pltpu.VMEM((QKV_AT, GROUP), jnp.bfloat16), pltpu.SemaphoreType.DMA],
        compiler_params=pltpu.CompilerParams(vmem_limit_bytes=8 * MIB),
        cost_estimate=pl.CostEstimate(flops=LONG, bytes_accessed=1, transcendentals=0),
        name="row_output",
    )(place, moved, weights)


def col_layer_kernel(place, moved, partial, gain, w0, w1, w2, w3, out2, out3, out, held, last, sem):
    arrays = (w0, w1, w2, w3)
    first = [pltpu.make_async_copy(w.at[:QKV_AT], last.at[i], sem.at[PARTS + i]) for i, w in enumerate(arrays[1:])]
    rest = [
        pltpu.make_async_copy(w.at[QKV_AT:], held.at[i] if i < 2 else held.at[i, : OUT_AT - QKV_AT], sem.at[i])
        for i, w in enumerate(arrays)
    ]
    ends = [
        pltpu.make_async_copy(w, held.at[2 + i, OUT_AT - QKV_AT :], sem.at[2 * PARTS - 1 + i])
        for i, w in enumerate((out2, out3))
    ]
    for copy in first + rest + ends:
        copy.start()
    atts = [moved[g, :, :GROUP] for g in weight_groups(place)[1:]]
    for copy in first:
        copy.wait()
    pieces = []
    for n in range(PARTS):
        total = sum(dot(a, last[i, n * GROUP : (n + 1) * GROUP, :]) for i, a in enumerate(atts))
        pieces.append((partial[n] + total).astype(jnp.bfloat16))
    normed = normed_pieces(pieces, [gain[n] for n in range(PARTS)])
    normed = jnp.concatenate(normed, axis=1)
    rows = normed.shape[0]
    row, col = triangle(rows)
    allowed = jnp.concatenate([col <= row] * HEADS_HERE, axis=0)
    atts = []
    for i, copy in enumerate(rest):
        copy.wait()
        q, k, v = [dot(normed, held[i, j * 1024 : (j + 1) * 1024, :]).astype(jnp.bfloat16) for j in range(3)]
        q = q * jnp.bfloat16(SCALE)
        scores = dot_t(jnp.concatenate([one_head(q, head) for head in range(HEADS_HERE)], axis=0), k)
        scores = jnp.where(allowed, scores, -1e30)
        expo = jnp.exp(scores - jnp.max(scores, axis=-1, keepdims=True))
        norm = jnp.sum(expo, axis=-1, keepdims=True)
        acc = dot(expo.astype(jnp.bfloat16), v) / norm
        att = acc[:rows]
        for head in range(1, HEADS_HERE):
            att = jnp.where(head_mask(rows, head), acc[head * rows : (head + 1) * rows], att)
        atts.append(att.astype(jnp.bfloat16))
    for copy in ends:
        copy.wait()
    for n in range(PARTS):
        at = OUT_AT - QKV_AT + n * GROUP
        total = sum(dot(a, held[i, at : at + GROUP, :]) for i, a in enumerate(atts))
        out[n] = (pieces[n].astype(jnp.float32) + total).astype(jnp.bfloat16)


def col_layer(place, moved, partial, gain, weights):
    return pl.pallas_call(
        col_layer_kernel,
        out_shape=jax.ShapeDtypeStruct((PARTS, 128, GROUP), jnp.bfloat16),
        in_specs=[SMEM, VMEM, VMEM, VMEM] + [ANY] * 6,
        out_specs=VMEM,
        scratch_shapes=[
            pltpu.VMEM((PARTS, WEIGHT_ROWS - QKV_AT, GROUP), jnp.bfloat16),
            pltpu.VMEM((PARTS - 1, QKV_AT, GROUP), jnp.bfloat16),
            pltpu.SemaphoreType.DMA((2 * PARTS + 1,)),
        ],
        compiler_params=pltpu.CompilerParams(vmem_limit_bytes=20 * MIB),
        cost_estimate=pl.CostEstimate(flops=1, bytes_accessed=1, transcendentals=0),
        name="col_layer",
    )(place, moved, partial, gain, *weights)


SWAP = [(0, 1), (1, 0)]


def after(value, *others):
    return lax.optimization_barrier((value, *others))[0]


def cross_route(outer):
    route = []
    for yh in range(4):
        for core in range(2):
            a = yh * 4 + 2 + core
            b = ((yh + 1) % 4 if core in outer else yh) * 4 + core
            route += [(a, b), (b, a)]
    return route


def on_device(inputs, row_gain, row_qkv, row_out, col_gain, col_qkv, col_out):
    yl, core = lax.axis_index("yl"), lax.axis_index("c")
    place = jnp.stack([yl * 2, (1 - yl) * 2, lax.axis_index(SEQ), core]).astype(jnp.int32)
    row_gain = row_gain.reshape(PARTS, 1, GROUP)
    row_qkv = row_qkv.transpose(1, 0, 2).reshape(3, PARTS, GROUP, GROUP)
    row_qkv = row_qkv * jnp.array([SCALE, 1, 1], jnp.bfloat16)[:, None, None, None]

    before = lax.ppermute(inputs, SEQ, [(i, i + 1) for i in range(127)])
    other = lax.ppermute(inputs, "yl", SWAP)
    near = lax.all_gather(inputs, "c", axis=0)
    mine, main, last = pack_weights(row_out, col_qkv.transpose(1, 0, 2).reshape(3 * 1024, GROUP), col_out)
    mine, main, last, row_qkv, before = lax.optimization_barrier((mine, main, last, row_qkv, before, near))[:5]
    before_other = lax.ppermute(before, "yl", SWAP)
    far = lax.all_gather(after(other, before), "c", axis=0)
    before_near = lax.all_gather(after(before, far), "c", axis=0)
    place = after(place, before_near)
    state = row_own(place, near, far, row_gain, row_qkv)
    before_far = lax.all_gather(after(before_other, state[0]), "c", axis=0)

    main = after(main, before_other, state[0])
    theirs = lax.ppermute(main, ("yh", "yl", "c"), cross_route((1,)))
    sent = row_halo(place, before_near, before_far, row_gain, row_qkv, state, inputs)
    mine_swapped = lax.ppermute(after(mine, sent), "c", SWAP)

    moved = lax.all_to_all(sent.reshape(COLS, 4, 128), HEAD + SEQ, 0, 0, tiled=True)
    moved = moved.reshape(PARTS, 128, 2 * GROUP)
    theirs_swapped = lax.ppermute(after(theirs, sent), "c", SWAP)
    last_theirs = lax.ppermute(after(last, sent), ("yh", "yl", "c"), cross_route((1,)))
    last_swapped = lax.ppermute(after(last_theirs, moved), "c", SWAP)
    partial = row_output(place, moved, mine)
    mixed = col_layer(
        place,
        moved,
        partial,
        col_gain.reshape(PARTS, 1, GROUP),
        [mine, mine_swapped, theirs, theirs_swapped, last_theirs, last_swapped],
    )
    mixed = lax.all_to_all(mixed.reshape(COLS, 2, 128), HEAD + SEQ, 0, 0, tiled=True)
    return mixed.reshape(COLS, GROUP)


def solution(mesh):
    fine = Mesh(mesh.devices.reshape(4, 8, 4, 2, 2), SEQ + HEAD)
    return jax.shard_map(
        on_device,
        mesh=fine,
        in_specs=(
            P(SEQ, HEAD),
            P(),
            P(None, None, HEAD),
            P(HEAD, None),
            P(),
            P(None, None, HEAD),
            P(HEAD, None),
        ),
        out_specs=P(SEQ, HEAD),
        check_vma=False,
    )
```
